256 devices in a mesh: lat: 32 (over x_lo, z, core), lon: 8 (over y, x_hi).
Axes of the slice: x: 4 (x_hi: 2, x_lo: 2; x = x_hi * 2 + x_lo), y: 4, z: 8, core: 2. Of those that a mesh axis runs over, the one named last changes fastest.
Arguments:
- tokens: bfloat16 [4, 192, 96, 512], P(None, 'lat', 'lon'), may hold values from -6 to 6
- cotangent: bfloat16 [4, 192, 96, 512], P(None, 'lat', 'lon'), may hold values from -6 to 6
- region: int32 [4, 192, 96], P(None, 'lat', 'lon'), may hold values from 0 to 7, as said below
- gain: float32 [512], replicated, may hold values from 0.5 to 1.5
- qkv_weight: bfloat16 [512, 1536], replicated, may hold values from -12 to 12
- proj_weight: bfloat16 [512, 512], replicated, may hold values from -0.25 to 0.25
Outputs:
- mixed: bfloat16 [4, 192, 96, 512], P(None, 'lat', 'lon')
- grad_tokens: bfloat16 [4, 192, 96, 512], P(None, 'lat', 'lon')
- grad_qkv: float32 [512, 1536], replicated
- grad_proj: float32 [512, 512], replicated
- grad_gain: float32 [512], replicated
The draws below stay inside these ranges and needn't reach their ends.
Inputs may be any that keep to these rules, and one draw needn't show every extreme that they name: region is constant on aligned blocks of one level, 3 rows and 6 columns; the last level and the last 3 rows of the shifted grid carry ids of their own.
All inputs are finite; a program needn't handle non-finite values.
Results may differ from the reference program's by a relative error of at most 0.013.
Values may be sent and summed in bfloat16 or wider, within the bound.
No kernel may reach another device: no remote copies, remote signals or barrier semaphores. Data moves between devices by JAX's collectives and lax.ppermute only.
A program may use at most 64 MiB of HBM per device.

```python
import jax
import jax.numpy as jnp
from jax import lax

D = 512
HEADS = 8
LEV = 4
WIN_C = 2
WIN_H = 6
WIN_W = 12
NLAT = 192
NLON = 96


def draw_region(key, part):
    key = jax.random.fold_in(key, 7)
    block_rows = NLAT // (WIN_H // 2)
    block_cols = NLON // (WIN_W // 2)
    random_bit = jax.random.randint(key, (LEV, block_rows, block_cols), 0, 2)
    random_bit = random_bit.at[0, 0, 0].set(0).at[LEV - 1, block_rows - 1, 0].set(1)
    level_part = (jnp.arange(LEV) == LEV - 1).astype(jnp.int32)[:, None, None]
    pole_part = (jnp.arange(block_rows) == block_rows - 1).astype(jnp.int32)[None, :, None]
    coarse = level_part + 2 * pole_part + 4 * random_bit
    fine_grid = jnp.repeat(jnp.repeat(coarse, WIN_H // 2, axis=1), WIN_W // 2, axis=2)
    return fine_grid.astype(jnp.int32)


def draw_qkv_weight(key, part):
    key = jax.random.fold_in(key, 11)
    normal_key = jax.random.fold_in(key, 1)
    base = jnp.clip(jax.random.normal(normal_key, (D, 3 * D), jnp.float32), -6.0, 6.0) * D ** (-0.5)
    return base.astype(jnp.bfloat16)


def block_levels(key, shape, pieces, least, high):
    loudness = 1.0
    for axis_at, shards_of in pieces:
        steps = jax.random.uniform(jax.random.fold_in(jax.random.fold_in(key, 6), axis_at), (shards_of,), jnp.float32, least / len(pieces), high / len(pieces))
        loudness = loudness * jnp.repeat(jnp.exp(steps), shape[axis_at] // shards_of).reshape((-1,) + (1,) * (len(shape) - 1 - axis_at))
    return loudness


def scatter_about(stream_key, dims, spread, limit, shards=(), dtype=jnp.bfloat16):
    result = spread * jax.random.normal(stream_key, dims, jnp.float32)
    if shards:
        result = result * block_levels(stream_key, dims, shards, -0.22, 0.18)
    return jnp.clip(result, -limit, limit).astype(dtype)


def setup_inputs(seed: int = 0) -> dict:
    key_of = jax.random.split(jax.random.key(seed), 7)
    tokens = scatter_about(key_of[0], (LEV, NLAT, NLON, D), 1.0, 6.0, ((1, 32), (2, 8)))
    cotangent = scatter_about(key_of[1], (LEV, NLAT, NLON, D), 1.0, 6.0, ((1, 32), (2, 8)))
    region = draw_region(jax.random.fold_in(key_of[6], 71), 0)
    gain = jnp.clip(jax.random.uniform(key_of[3], (D,), jnp.float32, 0.5, 1.5), 0.5, 1.5)
    qkv_weight = draw_qkv_weight(jax.random.fold_in(key_of[6], 71), 0)
    proj_weight = scatter_about(key_of[5], (D, D), D ** -0.5, 0.25)
    return {"tokens": tokens, "cotangent": cotangent, "region": region, "gain": gain, "qkv_weight": qkv_weight, "proj_weight": proj_weight}


EPS = 1e-05

def to_windows(field):
    levels, height, width = (field.shape[0], field.shape[1], field.shape[2])
    extra = field.shape[3:]
    shaped = field.reshape((levels // WIN_C, WIN_C, height // WIN_H, WIN_H, width // WIN_W, WIN_W) + extra)
    order = (0, 2, 4, 1, 3, 5) + tuple(range(6, 6 + len(extra)))
    return shaped.transpose(order).reshape((-1, WIN_C * WIN_H * WIN_W) + extra)

def from_windows(windows, levels, height, width):
    extra = windows.shape[2:]
    shaped = windows.reshape((levels // WIN_C, height // WIN_H, width // WIN_W, WIN_C, WIN_H, WIN_W) + extra)
    order = (0, 3, 1, 4, 2, 5) + tuple(range(6, 6 + len(extra)))
    return shaped.transpose(order).reshape((levels, height, width) + extra)

def dot_first(left_mat, right_mat):
    return lax.dot_general(left_mat, right_mat, (((0,), (0,)), ((), ())), preferred_element_type=jnp.float32)

def dot_last(left_mat, right_mat):
    return lax.dot_general(left_mat, right_mat, (((1,), (1,)), ((), ())), preferred_element_type=jnp.float32)

def window_pass(shift_x, shift_g, region, gain, qkv_weight, proj_weight):
    levels, height, width = (shift_x.shape[0], shift_x.shape[1], shift_x.shape[2])
    width_d = shift_x.shape[3]
    head_size = width_d // HEADS
    factor = head_size ** (-0.5)
    token_win = to_windows(shift_x)
    cot_win = to_windows(shift_g)
    region_win = to_windows(region)
    groups, count = (token_win.shape[0], token_win.shape[1])
    values_f = token_win.astype(jnp.float32)
    row_mean = lax.optimization_barrier(jnp.mean(values_f, -1, keepdims=True))
    centred = values_f - row_mean
    inv_std = lax.rsqrt(lax.optimization_barrier(jnp.mean(centred * centred, -1, keepdims=True)) + EPS)
    normed = centred * inv_std
    hidden = (normed * gain.astype(jnp.float32)).astype(jnp.bfloat16)
    flat_hidden = hidden.reshape(-1, width_d)
    projected = jnp.dot(flat_hidden, qkv_weight, preferred_element_type=jnp.float32).astype(jnp.bfloat16)
    projected = projected.reshape(groups, count, 3, HEADS, head_size)
    query, keys, values = (projected[:, :, 0], projected[:, :, 1], projected[:, :, 2])
    scores = jnp.einsum('gqhe,gkhe->ghqk', query.astype(jnp.float32), keys.astype(jnp.float32)) * factor
    allowed = region_win[:, None, :, None] == region_win[:, None, None, :]
    scores = jnp.where(allowed, scores, -1e+30)
    row_max = lax.optimization_barrier(jnp.max(scores, -1, keepdims=True))
    numer = jnp.exp(scores - row_max)
    weights = numer / lax.optimization_barrier(jnp.sum(numer, -1, keepdims=True))
    weights_low = weights.astype(jnp.bfloat16)
    attended = jnp.einsum('ghqk,gkhe->gqhe', weights_low.astype(jnp.float32), values.astype(jnp.float32))
    attended = attended.astype(jnp.bfloat16).reshape(-1, width_d)
    branch = jnp.dot(attended, proj_weight, preferred_element_type=jnp.float32).astype(jnp.bfloat16)
    flat_cot = cot_win.reshape(-1, width_d)
    grad_proj = dot_first(attended, flat_cot)
    grad_att = dot_last(flat_cot, proj_weight).astype(jnp.bfloat16).reshape(groups, count, HEADS, head_size)
    grad_weights = jnp.einsum('gqhe,gkhe->ghqk', grad_att.astype(jnp.float32), values.astype(jnp.float32))
    grad_value = jnp.einsum('ghqk,gqhe->gkhe', weights_low.astype(jnp.float32), grad_att.astype(jnp.float32)).astype(jnp.bfloat16)
    inner = lax.optimization_barrier(jnp.sum(grad_weights * weights, -1, keepdims=True))
    grad_scores = (weights * (grad_weights - inner) * factor).astype(jnp.bfloat16)
    grad_query = jnp.einsum('ghqk,gkhe->gqhe', grad_scores.astype(jnp.float32), keys.astype(jnp.float32)).astype(jnp.bfloat16)
    grad_key = jnp.einsum('ghqk,gqhe->gkhe', grad_scores.astype(jnp.float32), query.astype(jnp.float32)).astype(jnp.bfloat16)
    grad_rows = jnp.stack([grad_query, grad_key, grad_value], axis=2).reshape(-1, 3 * width_d)
    grad_qkv = dot_first(flat_hidden, grad_rows)
    grad_hidden = dot_last(grad_rows, qkv_weight).reshape(groups, count, width_d)
    grad_gain = lax.optimization_barrier(jnp.sum(grad_hidden * normed, axis=(0, 1)))
    grad_norm = grad_hidden * gain.astype(jnp.float32)
    grad_shift = inv_std * (grad_norm - lax.optimization_barrier(jnp.mean(grad_norm, -1, keepdims=True)) - normed * lax.optimization_barrier(jnp.mean(grad_norm * normed, -1, keepdims=True)))
    grad_shift = grad_shift.astype(jnp.bfloat16)
    branch = from_windows(branch.reshape(groups, count, width_d), levels, height, width)
    grad_shift = from_windows(grad_shift, levels, height, width)
    return (branch, grad_shift, grad_qkv, grad_proj, grad_gain)

def reference(tokens, cotangent, region, gain, qkv_weight, proj_weight):
    offsets = (WIN_C // 2, WIN_H // 2, WIN_W // 2)
    backwards = (-(WIN_C // 2), -(WIN_H // 2), -(WIN_W // 2))
    shifted = jnp.roll(tokens, backwards, (0, 1, 2))
    shifted_cot = jnp.roll(cotangent, backwards, (0, 1, 2))
    bands = NLAT // WIN_H
    token_bands = shifted.reshape(LEV, bands, WIN_H, NLON, D).transpose(1, 0, 2, 3, 4)
    cot_bands = shifted_cot.reshape(LEV, bands, WIN_H, NLON, D).transpose(1, 0, 2, 3, 4)
    region_bands = region.reshape(LEV, bands, WIN_H, NLON).transpose(1, 0, 2, 3)

    def step(carry, inputs):
        band_x, band_g, band_r = inputs
        branch, grad_shift, grad_qkv, grad_proj, grad_gain = window_pass(band_x, band_g, band_r, gain, qkv_weight, proj_weight)
        return ((carry[0] + grad_qkv, carry[1] + grad_proj, carry[2] + grad_gain), (branch, grad_shift))
    start = (jnp.zeros((D, 3 * D), jnp.float32), jnp.zeros((D, D), jnp.float32), jnp.zeros((D,), jnp.float32))
    sums, outputs = lax.scan(step, start, (token_bands, cot_bands, region_bands))
    branch = outputs[0].transpose(1, 0, 2, 3, 4).reshape(LEV, NLAT, NLON, D)
    grad_shift = outputs[1].transpose(1, 0, 2, 3, 4).reshape(LEV, NLAT, NLON, D)
    branch = jnp.roll(branch, offsets, (0, 1, 2))
    grad_shift = jnp.roll(grad_shift, offsets, (0, 1, 2))
    mixed = (tokens.astype(jnp.float32) + branch.astype(jnp.float32)).astype(jnp.bfloat16)
    grad_tokens = (cotangent.astype(jnp.float32) + grad_shift.astype(jnp.float32)).astype(jnp.bfloat16)
    return (mixed, grad_tokens, sums[0], sums[1], sums[2])
```

```python
import itertools

import jax
import jax.numpy as jnp
from jax import lax
from jax.experimental import pallas as pl
from jax.experimental.pallas import tpu as pltpu
from jax.sharding import Mesh, PartitionSpec as P

D = 512
HEADS = 8
HEAD = 64
PAIRS = HEADS // 2
WINDOWS = 2
COUNT = 144
TOKENS = WINDOWS * COUNT
HALF_R = 3
HALF_C = 6
EPS = 1e-05
SIZES = {"xl": 2, "z": 8, "c": 2, "y": 4, "xh": 2}
AXES = tuple(SIZES)
PLANE = ("xh", "xl", "y")
PIECE = (2, HALF_R, HALF_C, 4, D)
F32 = jnp.float32
BF16 = jnp.bfloat16


def dot(left, right):
    return jnp.dot(left, right, preferred_element_type=F32)


def dot_first(left, right):
    return lax.dot_general(left, right, (((0,), (0,)), ((), ())), preferred_element_type=F32)


def dot_last(left, right):
    return lax.dot_general(left, right, (((1,), (1,)), ((), ())), preferred_element_type=F32)


def pack_kernel(tok_ref, cot_ref, own_ref, right_ref, below_ref, corner_ref):
    for n, ref in enumerate((tok_ref, cot_ref)):
        own_ref[n] = ref[HALF_R:, HALF_C:]
        right_ref[n] = ref[HALF_R:, :HALF_C]
        below_ref[n] = ref[:HALF_R, HALF_C:]
        corner_ref[n] = ref[:HALF_R, :HALF_C]


def source_of(place):
    window = place // COUNT
    rest = place - window * COUNT
    level = (1 + 2 * window + rest % 2) % 4
    return (rest // 2) * 4 + level


def block_kernel(
    own_ref, right_ref, below_ref, corner_ref, bias_ref, gain_ref, qkv_ref, proj_ref,
    keep_ref, send_ref, own_out, right_out, below_out, corner_out,
    rows_ref, left_ref, att_ref,
):
    first = lax.broadcasted_iota(jnp.int32, (TOKENS, TOKENS), 0)
    second = lax.broadcasted_iota(jnp.int32, (TOKENS, TOKENS), 1)
    to_order = (second == source_of(first)).astype(BF16)
    from_order = (first == source_of(second)).astype(BF16)
    pieces = (own_ref, right_ref, below_ref, corner_ref)

    def gathered(n):
        return jnp.concatenate([ref[n] for ref in pieces], axis=0).reshape(TOKENS, D)

    values = dot(to_order, gathered(0))
    cot = dot(to_order, gathered(1)).astype(BF16)
    gain = gain_ref[...]
    mean = jnp.mean(values, -1, keepdims=True)
    centred = values - mean
    inv_std = lax.rsqrt(jnp.mean(centred * centred, -1, keepdims=True) + EPS)
    normed = centred * inv_std
    hidden = (normed * gain).astype(BF16)
    projected = dot(hidden, qkv_ref[...]).astype(BF16)
    grad_att = dot_last(cot, proj_ref[...]).astype(BF16)
    left_ref[0] = hidden.T
    rows_ref[3] = cot

    lane = lax.broadcasted_iota(jnp.int32, (COUNT, 2 * HEAD), 1)
    low = lane < HEAD
    zero = jnp.zeros((COUNT, 2 * HEAD), BF16)

    def both(pair):
        return jnp.concatenate([jnp.where(low, pair, zero), jnp.where(low, zero, pair)], axis=0)

    def merged(stacked):
        return jnp.where(low, stacked[:COUNT], stacked[COUNT:]).astype(BF16)

    factor = HEAD ** (-0.5)
    for window in range(WINDOWS):
        here = slice(window * COUNT, (window + 1) * COUNT)
        bias = jnp.concatenate([bias_ref[window]] * 2, axis=0)
        for pair in range(PAIRS):
            cols = slice(pair * 2 * HEAD, (pair + 1) * 2 * HEAD)
            query = both(projected[here, cols])
            keys = projected[here, D + cols.start : D + cols.stop]
            vals = projected[here, 2 * D + cols.start : 2 * D + cols.stop]
            grad_out = both(grad_att[here, cols])
            scores = dot_last(query, keys) * factor + bias
            numer = jnp.exp(scores - jnp.max(scores, -1, keepdims=True))
            weights = numer * (1.0 / jnp.sum(numer, -1, keepdims=True))
            weights_low = weights.astype(BF16)
            att_ref[here, cols] = merged(dot(weights_low, vals))
            grad_weights = dot_last(grad_out, vals)
            inner = jnp.sum(grad_weights * weights, -1, keepdims=True)
            grad_scores = (weights * (grad_weights - inner) * factor).astype(BF16)
            rows_ref[0, here, cols] = merged(dot(grad_scores, keys))
            rows_ref[1, here, cols] = dot_first(grad_scores, query).astype(BF16)
            rows_ref[2, here, cols] = dot_first(weights_low, grad_out).astype(BF16)

    attended = att_ref[...]
    left_ref[1] = attended.T
    core = lax.axis_index("c")
    for s in range(2):
        part = slice(s * D, (s + 1) * D)
        away = 2 * (1 - core) + s
        send_ref[part] = dot(left_ref[away // 3], rows_ref[away]).astype(BF16)
    for s in range(2):
        part = slice(s * D, (s + 1) * D)
        stay = 2 * core + s
        keep_ref[part] = dot(left_ref[stay // 3], rows_ref[stay])

    branch = dot(attended, proj_ref[...]).astype(BF16)
    grad_hidden = dot_last(rows_ref[0], qkv_ref[:, :D])
    grad_hidden += dot_last(rows_ref[1], qkv_ref[:, D : 2 * D])
    grad_hidden += dot_last(rows_ref[2], qkv_ref[:, 2 * D :])
    grad_norm = grad_hidden * gain
    grad_shift = inv_std * (
        grad_norm
        - jnp.mean(grad_norm, -1, keepdims=True)
        - normed * jnp.mean(grad_norm * normed, -1, keepdims=True)
    )
    for n, result in enumerate((branch, grad_shift.astype(BF16))):
        back = dot(from_order, result).reshape(4, HALF_R, HALF_C, 4, D).astype(BF16)
        for k, ref in enumerate((own_out, right_out, below_out, corner_out)):
            ref[n] = back[k]


def finish_kernel(tok_ref, cot_ref, own_ref, right_ref, below_ref, corner_ref, mixed_ref, grad_ref):
    for n, (ref, out) in enumerate(((tok_ref, mixed_ref), (cot_ref, grad_ref))):
        for rows, cols, piece in (
            (slice(HALF_R, None), slice(HALF_C, None), own_ref),
            (slice(HALF_R, None), slice(0, HALF_C), right_ref),
            (slice(0, HALF_R), slice(HALF_C, None), below_ref),
            (slice(0, HALF_R), slice(0, HALF_C), corner_ref),
        ):
            out[rows, cols] = (ref[rows, cols].astype(F32) + piece[n].astype(F32)).astype(BF16)


def grads_kernel(mine_ref, other_ref, qkv_ref, gain_ref, grad_qkv_ref, grad_proj_ref, grad_gain_ref):
    core = lax.axis_index("c")

    def put(low, high):
        total = jnp.zeros((D, 128), F32)
        for block, (ref, at) in enumerate(((low, 0), (low, D), (high, 0))):
            part = ref[at : at + D].astype(F32)
            cols = slice(block * D, (block + 1) * D)
            grad_qkv_ref[:, cols] = part
            product = part * qkv_ref[:, cols].astype(F32)
            for q in range(4):
                total += product[:, q * 128 : (q + 1) * 128]
        grad_proj_ref[...] = high[D:].astype(F32)
        grad_gain_ref[...] = jnp.sum(total, -1, keepdims=True) / gain_ref[...]

    @pl.when(core == 0)
    def _():
        put(mine_ref, other_ref)

    @pl.when(core == 1)
    def _():
        put(other_ref, mine_ref)


def call(kernel, outs, scratch=()):
    return pl.pallas_call(
        kernel,
        out_shape=outs,
        scratch_shapes=list(scratch),
        compiler_params=pltpu.CompilerParams(vmem_limit_bytes=48 * 1024 * 1024),
    )


def shaped(shape, dtype):
    return jax.ShapeDtypeStruct(shape, dtype)


def moved(block, lat_step, lon_step):
    where = {}
    for spot in itertools.product(*(range(n) for n in SIZES.values())):
        xl, z, c, y, xh = spot
        where[(xl * 16 + z * 2 + c, y * 2 + xh)] = ((((xl * 8 + z) * 2 + c) * 4 + y) * 2) + xh
    route = [
        (at, where[((lat + lat_step) % 32, (lon + lon_step) % 8)])
        for (lat, lon), at in where.items()
    ]
    return lax.ppermute(block, AXES, route)


def swapped(block):
    return lax.ppermute(block, "c", [(0, 1), (1, 0)])


def on_device(tokens, cotangent, region, gain, qkv_weight, proj_weight):
    tok = tokens.transpose(1, 2, 0, 3)
    cot = cotangent.transpose(1, 2, 0, 3)
    own, right, below, corner = call(pack_kernel, [shaped(PIECE, BF16)] * 4)(tok, cot)
    right = moved(right, 0, -1)
    below = moved(below, -1, 0)
    corner = moved(corner, -1, -1)
    ids = region.reshape(2, 2, 2, HALF_R, 2, HALF_C).transpose(0, 2, 4, 3, 5, 1).reshape(2, COUNT)
    bias = jnp.where(ids[:, :, None] == ids[:, None, :], 0.0, -1e30).astype(F32)
    keep, send, own_back, right_back, below_back, corner_back = call(
        block_kernel,
        [shaped((2 * D, D), F32), shaped((2 * D, D), BF16)] + [shaped(PIECE, BF16)] * 4,
        [
            pltpu.VMEM((4, TOKENS, D), BF16),
            pltpu.VMEM((2, D, TOKENS), BF16),
            pltpu.VMEM((TOKENS, D), BF16),
        ],
    )(own, right, below, corner, bias, gain.reshape(1, D), qkv_weight, proj_weight)

    got = swapped(send)
    half = (keep + got.astype(F32)).astype(BF16)
    got = lax.all_to_all(half.reshape(16, 64, D), PLANE, 0, 0)
    part = jnp.sum(got.astype(F32), axis=0).astype(BF16)
    got = lax.all_to_all(part.reshape(8, 8, D), "z", 0, 0)
    part = jnp.sum(got.astype(F32), axis=0).astype(BF16)
    part = lax.all_to_all(jnp.broadcast_to(part, (8, 8, D)), "z", 0, 0).reshape(64, D)
    mine = lax.all_to_all(jnp.broadcast_to(part, (16, 64, D)), PLANE, 0, 0).reshape(2 * D, D)
    other = swapped(mine)
    grad_qkv, grad_proj, grad_gain = call(
        grads_kernel, [shaped((D, 3 * D), F32), shaped((D, D), F32), shaped((D, 1), F32)]
    )(mine, other, qkv_weight, gain.reshape(D, 1))

    right_back = moved(right_back, 0, 1)
    below_back = moved(below_back, 1, 0)
    corner_back = moved(corner_back, 1, 1)
    mixed, grad_tokens = call(finish_kernel, [shaped((6, 12, 4, D), BF16)] * 2)(
        tok, cot, own_back, right_back, below_back, corner_back
    )
    return (
        mixed.transpose(2, 0, 1, 3),
        grad_tokens.transpose(2, 0, 1, 3),
        grad_qkv,
        grad_proj,
        grad_gain.reshape(D),
    )


def solution(mesh):
    fine = Mesh(mesh.devices.reshape(tuple(SIZES.values())), AXES)
    grid = P(None, ("xl", "z", "c"), ("y", "xh"), None)
    return jax.shard_map(
        on_device,
        mesh=fine,
        in_specs=(grid, grid, P(None, ("xl", "z", "c"), ("y", "xh")), P(), P(), P()),
        out_specs=(grid, grid, P(), P(), P()),
        check_vma=False,
    )
```

```python
import itertools

import jax
import jax.numpy as jnp
from jax import lax
from jax.experimental import pallas as pl
from jax.experimental.pallas import tpu as pltpu
from jax.sharding import Mesh, PartitionSpec as P

D = 512
HALF_D = D // 2
HEADS = 8
HEAD = 64
PAIRS = HEADS // 2
WINDOWS = 2
COUNT = 144
TOKENS = WINDOWS * COUNT
HALF_R = 3
HALF_C = 6
EPS = 1e-05
SIZES = {"xl": 2, "z": 8, "c": 2, "y": 4, "xh": 2}
AXES = tuple(SIZES)
PLANE = ("y", "xh", "xl")
PIECE = (2, HALF_R, HALF_C, 4, D)
F32 = jnp.float32
BF16 = jnp.bfloat16


def dot(left, right):
    return jnp.dot(left, right, preferred_element_type=F32)


def dot_first(left, right):
    return lax.dot_general(left, right, (((0,), (0,)), ((), ())), preferred_element_type=F32)


def dot_last(left, right):
    return lax.dot_general(left, right, (((1,), (1,)), ((), ())), preferred_element_type=F32)


def pack_kernel(tok_ref, cot_ref, own_ref, right_ref, below_ref, corner_ref, sems):
    copies = []
    for n, ref in enumerate((tok_ref, cot_ref)):
        for rows, cols, piece in quadrants(own_ref, right_ref, below_ref, corner_ref):
            sem = sems.at[len(copies)]
            copies.append(pltpu.make_async_copy(ref.at[rows, cols], piece.at[n], sem))
    for copy in copies:
        copy.start()
    for copy in copies:
        copy.wait()


def quadrants(own, right, below, corner):
    late_r, early_r = pl.ds(HALF_R, HALF_R), pl.ds(0, HALF_R)
    late_c, early_c = pl.ds(HALF_C, HALF_C), pl.ds(0, HALF_C)
    return (
        (late_r, late_c, own),
        (late_r, early_c, right),
        (early_r, late_c, below),
        (early_r, early_c, corner),
    )


def source_of(place):
    window = place // COUNT
    rest = place - window * COUNT
    level = (1 + 2 * window + rest % 2) % 4
    return (rest // 2) * 4 + level


def attend_kernel(
    own_ref, right_ref, below_ref, corner_ref, bias_ref, gain_ref, qkv_ref, proj_ref,
    send_ref, left_ref, rows_ref, att_ref, normed_ref, inv_ref,
):
    first = lax.broadcasted_iota(jnp.int32, (TOKENS, TOKENS), 0)
    second = lax.broadcasted_iota(jnp.int32, (TOKENS, TOKENS), 1)
    to_order = (second == source_of(first)).astype(BF16)
    pieces = (own_ref, right_ref, below_ref, corner_ref)

    def gathered(n):
        return jnp.concatenate([ref[n] for ref in pieces], axis=0).reshape(TOKENS, D)

    values = dot(to_order, gathered(0))
    cot = dot(to_order, gathered(1)).astype(BF16)
    gain = gain_ref[...]
    mean = jnp.mean(values, -1, keepdims=True)
    centred = values - mean
    inv_std = lax.rsqrt(jnp.mean(centred * centred, -1, keepdims=True) + EPS)
    normed = centred * inv_std
    hidden = (normed * gain).astype(BF16)
    projected = dot(hidden, qkv_ref[...]).astype(BF16)
    grad_att = dot_last(cot, proj_ref[...]).astype(BF16)
    normed_ref[...] = normed
    inv_ref[...] = inv_std
    left_ref[0] = hidden.T
    rows_ref[3] = cot

    lane = lax.broadcasted_iota(jnp.int32, (COUNT, 2 * HEAD), 1)
    low = lane < HEAD
    zero = jnp.zeros((COUNT, 2 * HEAD), BF16)

    def both(pair):
        return jnp.concatenate([jnp.where(low, pair, zero), jnp.where(low, zero, pair)], axis=0)

    def merged(stacked):
        return jnp.where(low, stacked[:COUNT], stacked[COUNT:]).astype(BF16)

    factor = HEAD ** (-0.5)
    for window in range(WINDOWS):
        here = slice(window * COUNT, (window + 1) * COUNT)
        bias = jnp.concatenate([bias_ref[window]] * 2, axis=0)
        for pair in range(PAIRS):
            cols = slice(pair * 2 * HEAD, (pair + 1) * 2 * HEAD)
            query = both(projected[here, cols])
            keys = projected[here, D + cols.start : D + cols.stop]
            vals = projected[here, 2 * D + cols.start : 2 * D + cols.stop]
            grad_out = both(grad_att[here, cols])
            scores = dot_last(query, keys) * factor + bias
            numer = jnp.exp(scores - jnp.max(scores, -1, keepdims=True))
            weights = numer * (1.0 / jnp.sum(numer, -1, keepdims=True))
            weights_low = weights.astype(BF16)
            att_ref[here, cols] = merged(dot(weights_low, vals))
            grad_weights = dot_last(grad_out, vals)
            inner = jnp.sum(grad_weights * weights, -1, keepdims=True)
            grad_scores = (weights * (grad_weights - inner) * factor).astype(BF16)
            rows_ref[0, here, cols] = merged(dot(grad_scores, keys))
            rows_ref[1, here, cols] = dot_first(grad_scores, query).astype(BF16)
            rows_ref[2, here, cols] = dot_first(weights_low, grad_out).astype(BF16)

    left_ref[1] = att_ref[...].T
    half_grads(1 - lax.axis_index("c"), left_ref, rows_ref, send_ref)


def half_grads(half, left_ref, rows_ref, out_ref):
    here = pl.ds(pl.multiple_of(half * HALF_D, HALF_D), HALF_D)
    for block in range(4):
        out_ref[block] = dot(left_ref[block // 3, here], rows_ref[block]).astype(BF16)


def rest_kernel(
    left_ref, rows_ref, att_ref, normed_ref, inv_ref, gain_ref, qkv_ref, proj_ref,
    keep_ref, own_out, right_out, below_out, corner_out,
):
    half_grads(lax.axis_index("c"), left_ref, rows_ref, keep_ref)
    first = lax.broadcasted_iota(jnp.int32, (TOKENS, TOKENS), 0)
    second = lax.broadcasted_iota(jnp.int32, (TOKENS, TOKENS), 1)
    from_order = (first == source_of(second)).astype(BF16)
    normed = normed_ref[...]
    inv_std = inv_ref[...]
    attended = att_ref[...]
    gain = gain_ref[...]
    branch = dot(attended, proj_ref[...]).astype(BF16)
    grad_hidden = dot_last(rows_ref[0], qkv_ref[:, :D])
    grad_hidden += dot_last(rows_ref[1], qkv_ref[:, D : 2 * D])
    grad_hidden += dot_last(rows_ref[2], qkv_ref[:, 2 * D :])
    grad_norm = grad_hidden * gain
    grad_shift = inv_std * (
        grad_norm
        - jnp.mean(grad_norm, -1, keepdims=True)
        - normed * jnp.mean(grad_norm * normed, -1, keepdims=True)
    )
    for n, result in enumerate((branch, grad_shift.astype(BF16))):
        back = dot(from_order, result).reshape(4, HALF_R, HALF_C, 4, D).astype(BF16)
        for k, ref in enumerate((own_out, right_out, below_out, corner_out)):
            ref[n] = back[k]


def sum_kernel(got_ref, right_ref, below_ref, corner_ref, out_ref):
    del right_ref, below_ref, corner_ref
    total = got_ref[0].astype(F32)
    for n in range(1, got_ref.shape[0]):
        total += got_ref[n].astype(F32)
    out_ref[...] = total.astype(BF16)


def finish_kernel(tok_ref, cot_ref, own_ref, right_ref, below_ref, corner_ref, mixed_ref, grad_ref):
    for n, (ref, out) in enumerate(((tok_ref, mixed_ref), (cot_ref, grad_ref))):
        for rows, cols, piece in quadrants(own_ref, right_ref, below_ref, corner_ref):
            out[rows, cols] = (ref[rows, cols].astype(F32) + piece[n].astype(F32)).astype(BF16)


def grads_kernel(
    mine_ref, other_ref, qkv_ref, gain_ref, grad_qkv_ref, grad_proj_ref, grad_gain_ref, wide, sems
):
    core = lax.axis_index("c")
    copies = []
    for n, (ref, half) in enumerate(((mine_ref, core), (other_ref, 1 - core))):
        here = pl.ds(pl.multiple_of(half * HALF_D, HALF_D), HALF_D)
        total = jnp.zeros((HALF_D, 128), F32)
        for block in range(4):
            part = ref[block].astype(F32)
            wide[n, block] = part
            cols = pl.ds(block * D, D)
            out = grad_proj_ref.at[here] if block == 3 else grad_qkv_ref.at[here, cols]
            copy = pltpu.make_async_copy(wide.at[n, block], out, sems.at[n, block])
            copy.start()
            copies.append(copy)
            if block < 3:
                product = part * qkv_ref[here, cols].astype(F32)
                for q in range(4):
                    total += product[:, q * 128 : (q + 1) * 128]
        sums = jnp.sum(total.T, axis=0, keepdims=True)
        grad_gain_ref[:, here] = sums / gain_ref[:, here]
    for copy in copies:
        copy.wait()


def call(kernel, outs, scratch=(), ins=None, out_specs=None, mib=8):
    more = {}
    if ins is not None:
        more["in_specs"] = ins
    if out_specs is not None:
        more["out_specs"] = out_specs
    return pl.pallas_call(
        kernel,
        out_shape=outs,
        scratch_shapes=list(scratch),
        compiler_params=pltpu.CompilerParams(vmem_limit_bytes=mib * 1024 * 1024),
        **more,
    )


def shaped(shape, dtype):
    return jax.ShapeDtypeStruct(shape, dtype)


def moved(block, lat_step, lon_step):
    where = {}
    for spot in itertools.product(*(range(n) for n in SIZES.values())):
        xl, z, c, y, xh = spot
        where[(xl * 16 + z * 2 + c, y * 2 + xh)] = ((((xl * 8 + z) * 2 + c) * 4 + y) * 2) + xh
    route = [
        (at, where[((lat + lat_step) % 32, (lon + lon_step) % 8)])
        for (lat, lon), at in where.items()
    ]
    return lax.ppermute(block, AXES, route)


def swapped(block):
    return lax.ppermute(block, "c", [(0, 1), (1, 0)])


def on_device(tokens, cotangent, region, gain, qkv_weight, proj_weight):
    tok = tokens.transpose(1, 2, 0, 3)
    cot = cotangent.transpose(1, 2, 0, 3)
    anywhere = pl.BlockSpec(memory_space=pl.ANY)
    vmem = pl.BlockSpec(memory_space=pltpu.VMEM)
    own, right, below, corner = call(
        pack_kernel,
        [shaped(PIECE, BF16)] * 4,
        [pltpu.SemaphoreType.DMA((8,))],
        [anywhere] * 2,
        [vmem] * 4,
        mib=2,
    )(tok, cot)
    right = moved(right, 0, -1)
    below = moved(below, -1, 0)
    corner = moved(corner, -1, -1)
    ids = region.reshape(2, 2, 2, HALF_R, 2, HALF_C).transpose(0, 2, 4, 3, 5, 1).reshape(2, COUNT)
    bias = jnp.where(ids[:, :, None] == ids[:, None, :], 0.0, -1e30).astype(F32)
    gain = gain.reshape(1, D)
    send, *state = call(
        attend_kernel,
        [
            shaped((4, HALF_D, D), BF16),
            shaped((2, D, TOKENS), BF16),
            shaped((4, TOKENS, D), BF16),
            shaped((TOKENS, D), BF16),
            shaped((TOKENS, D), F32),
            shaped((TOKENS, 1), F32),
        ],
        mib=16,
    )(own, right, below, corner, bias, gain, qkv_weight, proj_weight)
    got = swapped(send)
    keep, own_back, right_back, below_back, corner_back = call(
        rest_kernel, [shaped((4, HALF_D, D), BF16)] + [shaped(PIECE, BF16)] * 4, mib=16
    )(*state, gain, qkv_weight, proj_weight)
    right_back = moved(right_back, 0, 1)
    below_back = moved(below_back, 1, 0)
    corner_back = moved(corner_back, 1, 1)

    half = (keep.astype(F32) + got.astype(F32)).astype(BF16)
    got = lax.all_to_all(half.reshape(16, 64, D), PLANE, 0, 0)
    part = call(
        sum_kernel, shaped((64, D), BF16), ins=[vmem] + [anywhere] * 3, out_specs=vmem, mib=4
    )(got, right_back, below_back, corner_back)
    got = lax.all_to_all(part.reshape(8, 8, D), "z", 0, 0)
    part = jnp.sum(got.astype(F32), axis=0).astype(BF16)
    part = lax.all_to_all(jnp.broadcast_to(part, (8, 8, D)), "z", 0, 0).reshape(64, D)
    mine = lax.all_to_all(jnp.broadcast_to(part, (16, 64, D)), PLANE, 0, 0)
    mine = mine.reshape(4, HALF_D, D)
    other = swapped(mine)
    grad_qkv, grad_proj, grad_gain = call(
        grads_kernel,
        [shaped((D, 3 * D), F32), shaped((D, D), F32), shaped((1, D), F32)],
        [pltpu.VMEM((2, 4, HALF_D, D), F32), pltpu.SemaphoreType.DMA((2, 4))],
        [vmem] * 4,
        [anywhere, anywhere, vmem],
        mib=10,
    )(mine, other, qkv_weight, gain)
    mixed, grad_tokens = call(finish_kernel, [shaped((6, 12, 4, D), BF16)] * 2, mib=6)(
        tok, cot, own_back, right_back, below_back, corner_back
    )
    return (
        mixed.transpose(2, 0, 1, 3),
        grad_tokens.transpose(2, 0, 1, 3),
        grad_qkv,
        grad_proj,
        grad_gain.reshape(D),
    )


def solution(mesh):
    fine = Mesh(mesh.devices.reshape(tuple(SIZES.values())), AXES)
    grid = P(None, ("xl", "z", "c"), ("y", "xh"), None)
    return jax.shard_map(
        on_device,
        mesh=fine,
        in_specs=(grid, grid, P(None, ("xl", "z", "c"), ("y", "xh")), P(), P(), P()),
        out_specs=(grid, grid, P(), P(), P()),
        check_vma=False,
    )
```

```python
import itertools

import jax
import jax.numpy as jnp
from jax import lax
from jax.experimental import pallas as pl
from jax.experimental.pallas import tpu as pltpu
from jax.sharding import Mesh, PartitionSpec as P

D = 512
HALF_D = D // 2
HEADS = 8
HEAD = 64
PAIRS = HEADS // 2
WINDOWS = 2
COUNT = 144
TOKENS = WINDOWS * COUNT
HALF_R = 3
HALF_C = 6
EPS = 1e-05
SIZES = {"xl": 2, "z": 8, "c": 2, "y": 4, "xh": 2}
AXES = tuple(SIZES)
PLANE = ("y", "xh", "xl")
PIECE = (2, HALF_R, HALF_C, 4, D)
F32 = jnp.float32
BF16 = jnp.bfloat16


def dot(left, right):
    return jnp.dot(left, right, preferred_element_type=F32)


def dot_first(left, right):
    return lax.dot_general(left, right, (((0,), (0,)), ((), ())), preferred_element_type=F32)


def dot_last(left, right):
    return lax.dot_general(left, right, (((1,), (1,)), ((), ())), preferred_element_type=F32)


def pack_kernel(tok_ref, cot_ref, own_ref, right_ref, below_ref, corner_ref, sems):
    copies = []
    for n, ref in enumerate((tok_ref, cot_ref)):
        for rows, cols, piece in quadrants(own_ref, right_ref, below_ref, corner_ref):
            sem = sems.at[len(copies)]
            copies.append(pltpu.make_async_copy(ref.at[rows, cols], piece.at[n], sem))
    for copy in copies:
        copy.start()
    for copy in copies:
        copy.wait()


def quadrants(own, right, below, corner):
    late_r, early_r = pl.ds(HALF_R, HALF_R), pl.ds(0, HALF_R)
    late_c, early_c = pl.ds(HALF_C, HALF_C), pl.ds(0, HALF_C)
    return (
        (late_r, late_c, own),
        (late_r, early_c, right),
        (early_r, late_c, below),
        (early_r, early_c, corner),
    )


def source_of(place):
    window = place // COUNT
    rest = place - window * COUNT
    level = (1 + 2 * window + rest % 2) % 4
    return (rest // 2) * 4 + level


def attend_kernel(
    own_ref, right_ref, below_ref, corner_ref, bias_ref, gain_ref, qkv_ref, proj_ref,
    send_ref, left_ref, rows_ref, att_ref, normed_ref, inv_ref,
):
    first = lax.broadcasted_iota(jnp.int32, (TOKENS, TOKENS), 0)
    second = lax.broadcasted_iota(jnp.int32, (TOKENS, TOKENS), 1)
    to_order = (second == source_of(first)).astype(BF16)
    pieces = (own_ref, right_ref, below_ref, corner_ref)

    def gathered(n):
        return jnp.concatenate([ref[n] for ref in pieces], axis=0).reshape(TOKENS, D)

    values = dot(to_order, gathered(0))
    cot = dot(to_order, gathered(1)).astype(BF16)
    gain = gain_ref[...]
    mean = jnp.mean(values, -1, keepdims=True)
    centred = values - mean
    inv_std = lax.rsqrt(jnp.mean(centred * centred, -1, keepdims=True) + EPS)
    normed = centred * inv_std
    hidden = (normed * gain).astype(BF16)
    projected = dot(hidden, qkv_ref[...]).astype(BF16)
    grad_att = dot_last(cot, proj_ref[...]).astype(BF16)
    normed_ref[...] = normed
    inv_ref[...] = inv_std
    left_ref[0] = hidden.T
    rows_ref[3] = cot

    lane = lax.broadcasted_iota(jnp.int32, (COUNT, 2 * HEAD), 1)
    low = lane < HEAD
    zero = jnp.zeros((COUNT, 2 * HEAD), BF16)

    def both(pair):
        return jnp.concatenate([jnp.where(low, pair, zero), jnp.where(low, zero, pair)], axis=0)

    def merged(stacked):
        return jnp.where(low, stacked[:COUNT], stacked[COUNT:]).astype(BF16)

    factor = HEAD ** (-0.5)
    for window in range(WINDOWS):
        here = slice(window * COUNT, (window + 1) * COUNT)
        bias = jnp.concatenate([bias_ref[window]] * 2, axis=0)
        for pair in range(PAIRS):
            cols = slice(pair * 2 * HEAD, (pair + 1) * 2 * HEAD)
            query = both(projected[here, cols])
            keys = projected[here, D + cols.start : D + cols.stop]
            vals = projected[here, 2 * D + cols.start : 2 * D + cols.stop]
            grad_out = both(grad_att[here, cols])
            scores = dot_last(query, keys) * factor + bias
            numer = jnp.exp(scores - jnp.max(scores, -1, keepdims=True))
            weights = numer * (1.0 / jnp.sum(numer, -1, keepdims=True))
            weights_low = weights.astype(BF16)
            att_ref[here, cols] = merged(dot(weights_low, vals))
            grad_weights = dot_last(grad_out, vals)
            inner = jnp.sum(grad_weights * weights, -1, keepdims=True)
            grad_scores = (weights * (grad_weights - inner) * factor).astype(BF16)
            rows_ref[0, here, cols] = merged(dot(grad_scores, keys))
            rows_ref[1, here, cols] = dot_first(grad_scores, query).astype(BF16)
            rows_ref[2, here, cols] = dot_first(weights_low, grad_out).astype(BF16)

    left_ref[1] = att_ref[...].T
    half_grads(1 - lax.axis_index("c"), left_ref, rows_ref, send_ref)


def half_grads(half, left_ref, rows_ref, out_ref):
    here = pl.ds(pl.multiple_of(half * HALF_D, HALF_D), HALF_D)
    for block in range(4):
        out_ref[block] = dot(left_ref[block // 3, here], rows_ref[block]).astype(BF16)


def rest_kernel(
    left_ref, rows_ref, att_ref, normed_ref, inv_ref, gain_ref, qkv_ref, proj_ref,
    keep_ref, own_out, right_out, below_out, corner_out,
):
    half_grads(lax.axis_index("c"), left_ref, rows_ref, keep_ref)
    first = lax.broadcasted_iota(jnp.int32, (TOKENS, TOKENS), 0)
    second = lax.broadcasted_iota(jnp.int32, (TOKENS, TOKENS), 1)
    from_order = (first == source_of(second)).astype(BF16)
    normed = normed_ref[...]
    inv_std = inv_ref[...]
    attended = att_ref[...]
    gain = gain_ref[...]
    branch = dot(attended, proj_ref[...]).astype(BF16)
    grad_hidden = dot_last(rows_ref[0], qkv_ref[:, :D])
    grad_hidden += dot_last(rows_ref[1], qkv_ref[:, D : 2 * D])
    grad_hidden += dot_last(rows_ref[2], qkv_ref[:, 2 * D :])
    grad_norm = grad_hidden * gain
    grad_shift = inv_std * (
        grad_norm
        - jnp.mean(grad_norm, -1, keepdims=True)
        - normed * jnp.mean(grad_norm * normed, -1, keepdims=True)
    )
    for n, result in enumerate((branch, grad_shift.astype(BF16))):
        back = dot(from_order, result).reshape(4, HALF_R, HALF_C, 4, D).astype(BF16)
        for k, ref in enumerate((own_out, right_out, below_out, corner_out)):
            ref[n] = back[k]


def weights_kernel(qkv_ref, proj_ref, gain_ref, qkv_out, proj_out, gain_out, sems):
    copies = [
        pltpu.make_async_copy(ref, out, sems.at[n])
        for n, (ref, out) in enumerate(
            ((qkv_ref, qkv_out), (proj_ref, proj_out), (gain_ref, gain_out))
        )
    ]
    for copy in copies:
        copy.start()
    for copy in copies:
        copy.wait()


def add_kernel(keep_ref, got_ref, out_ref):
    out_ref[...] = (keep_ref[...].astype(F32) + got_ref[...].astype(F32)).astype(BF16)


def summed(got_ref):
    total = got_ref[0].astype(F32)
    for n in range(1, got_ref.shape[0]):
        total += got_ref[n].astype(F32)
    return total.astype(BF16)


def sum_kernel(got_ref, a_ref, b_ref, c_ref, out_ref, a_out, b_out, c_out):
    del a_ref, b_ref, c_ref, a_out, b_out, c_out
    out_ref[...] = summed(got_ref)


def spread_kernel(got_ref, right_ref, below_ref, corner_ref, out_ref):
    del right_ref, below_ref, corner_ref
    total = summed(got_ref)
    for n in range(out_ref.shape[0]):
        out_ref[n] = total


def finish_kernel(tok_ref, cot_ref, own_ref, right_ref, below_ref, corner_ref, mixed_ref, grad_ref):
    for n, (ref, out) in enumerate(((tok_ref, mixed_ref), (cot_ref, grad_ref))):
        for rows, cols, piece in quadrants(own_ref, right_ref, below_ref, corner_ref):
            out[rows, cols] = (ref[rows, cols].astype(F32) + piece[n].astype(F32)).astype(BF16)


def grads_half(half, ref, qkv_ref, gain_ref, qkv_out, proj_out, gain_out, wide, sems):
    copies = []
    here = pl.ds(pl.multiple_of(half * HALF_D, HALF_D), HALF_D)
    total = jnp.zeros((HALF_D, 128), F32)
    for block in range(4):
        part = ref[block].astype(F32)
        wide[block] = part
        cols = pl.ds(block * D, D)
        out = proj_out.at[here] if block == 3 else qkv_out.at[here, cols]
        copy = pltpu.make_async_copy(wide.at[block], out, sems.at[block])
        copy.start()
        copies.append(copy)
        if block < 3:
            product = part * qkv_ref[here, cols].astype(F32)
            for q in range(4):
                total += product[:, q * 128 : (q + 1) * 128]
    sums = jnp.sum(total.T, axis=0, keepdims=True)
    gain_out[:, here] = sums / gain_ref[:, here]
    for copy in copies:
        copy.wait()


def mine_kernel(ref, qkv_ref, gain_ref, qkv_out, proj_out, gain_out, wide, sems):
    gain_out[...] = jnp.zeros_like(gain_out)
    core = lax.axis_index("c")
    grads_half(core, ref, qkv_ref, gain_ref, qkv_out, proj_out, gain_out, wide, sems)


def other_kernel(
    ref, qkv_ref, gain_ref, qkv_in, proj_in, gain_in, qkv_out, proj_out, gain_out, wide, sems
):
    del qkv_in, proj_in
    gain_out[...] = gain_in[...]
    core = lax.axis_index("c")
    grads_half(1 - core, ref, qkv_ref, gain_ref, qkv_out, proj_out, gain_out, wide, sems)


def call(kernel, outs, scratch=(), ins=None, out_specs=None, mib=8, aliases=None):
    more = {"input_output_aliases": aliases or {}}
    if ins is not None:
        more["in_specs"] = ins
    if out_specs is not None:
        more["out_specs"] = out_specs
    return pl.pallas_call(
        kernel,
        out_shape=outs,
        scratch_shapes=list(scratch),
        compiler_params=pltpu.CompilerParams(vmem_limit_bytes=mib * 1024 * 1024),
        **more,
    )


def in_hbm(array):
    return pltpu.with_memory_space_constraint(array, pltpu.HBM)


def shaped(shape, dtype):
    return jax.ShapeDtypeStruct(shape, dtype)


def moved(block, lat_step, lon_step):
    where = {}
    for spot in itertools.product(*(range(n) for n in SIZES.values())):
        xl, z, c, y, xh = spot
        where[(xl * 16 + z * 2 + c, y * 2 + xh)] = ((((xl * 8 + z) * 2 + c) * 4 + y) * 2) + xh
    route = [
        (at, where[((lat + lat_step) % 32, (lon + lon_step) % 8)])
        for (lat, lon), at in where.items()
    ]
    return lax.ppermute(block, AXES, route)


def swapped(block):
    return lax.ppermute(block, "c", [(0, 1), (1, 0)])


def on_device(tokens, cotangent, region, gain, qkv_weight, proj_weight):
    tok = tokens.transpose(1, 2, 0, 3)
    cot = cotangent.transpose(1, 2, 0, 3)
    anywhere = pl.BlockSpec(memory_space=pl.ANY)
    vmem = pl.BlockSpec(memory_space=pltpu.VMEM)
    hbm = pl.BlockSpec(memory_space=pltpu.HBM)
    own, right, below, corner = call(
        pack_kernel,
        [shaped(PIECE, BF16)] * 4,
        [pltpu.SemaphoreType.DMA((8,))],
        [hbm] * 2,
        [vmem] * 4,
        mib=2,
    )(in_hbm(tok), in_hbm(cot))
    right = moved(right, 0, -1)
    below = moved(below, -1, 0)
    corner = moved(corner, -1, -1)
    ids = region.reshape(2, 2, 2, HALF_R, 2, HALF_C).transpose(0, 2, 4, 3, 5, 1).reshape(2, COUNT)
    bias = jnp.where(ids[:, :, None] == ids[:, None, :], 0.0, -1e30).astype(F32)
    gain = gain.reshape(1, D)
    qkv_weight, proj_weight, gain = call(
        weights_kernel,
        [shaped((D, 3 * D), BF16), shaped((D, D), BF16), shaped((1, D), F32)],
        [pltpu.SemaphoreType.DMA((3,))],
        [hbm] * 3,
        [vmem] * 3,
        mib=1,
    )(in_hbm(qkv_weight), in_hbm(proj_weight), in_hbm(gain))
    send, *state = call(
        attend_kernel,
        [
            shaped((4, HALF_D, D), BF16),
            shaped((2, D, TOKENS), BF16),
            shaped((4, TOKENS, D), BF16),
            shaped((TOKENS, D), BF16),
            shaped((TOKENS, D), F32),
            shaped((TOKENS, 1), F32),
        ],
        mib=16,
    )(own, right, below, corner, bias, gain, qkv_weight, proj_weight)
    got = swapped(send)
    keep, own_back, right_back, below_back, corner_back = call(
        rest_kernel, [shaped((4, HALF_D, D), BF16)] + [shaped(PIECE, BF16)] * 4, mib=16
    )(*state, gain, qkv_weight, proj_weight)
    half = call(add_kernel, shaped((4, HALF_D, D), BF16), mib=4)(keep, got)
    got = lax.all_to_all(half.reshape(16, 64, D), PLANE, 0, 0)
    part, right_back, below_back, corner_back = call(
        sum_kernel,
        [shaped((64, D), BF16)] + [shaped(PIECE, BF16)] * 3,
        ins=[vmem] + [anywhere] * 3,
        out_specs=[vmem] + [anywhere] * 3,
        mib=4,
        aliases={1: 1, 2: 2, 3: 3},
    )(got, right_back, below_back, corner_back)
    right_back = moved(right_back, 0, 1)
    below_back = moved(below_back, 1, 0)
    corner_back = moved(corner_back, 1, 1)
    got = lax.all_to_all(part.reshape(8, 8, D), "z", 0, 0)
    parts = call(
        spread_kernel, shaped((8, 8, D), BF16), ins=[vmem] + [anywhere] * 3, out_specs=vmem, mib=2
    )(got, right_back, below_back, corner_back)
    part = lax.all_to_all(parts, "z", 0, 0).reshape(64, D)
    mine = lax.all_to_all(jnp.broadcast_to(part, (16, 64, D)), PLANE, 0, 0)
    mine = mine.reshape(4, HALF_D, D)
    other = swapped(mine)
    grads = call(
        mine_kernel,
        [shaped((D, 3 * D), F32), shaped((D, D), F32), shaped((1, D), F32)],
        [pltpu.VMEM((4, HALF_D, D), F32), pltpu.SemaphoreType.DMA((4,))],
        [vmem] * 3,
        [anywhere, anywhere, vmem],
        mib=6,
    )(mine, qkv_weight, gain)
    grad_qkv, grad_proj, grad_gain = call(
        other_kernel,
        [shaped((D, 3 * D), F32), shaped((D, D), F32), shaped((1, D), F32)],
        [pltpu.VMEM((4, HALF_D, D), F32), pltpu.SemaphoreType.DMA((4,))],
        [vmem] * 3 + [anywhere] * 2 + [vmem],
        [anywhere, anywhere, vmem],
        mib=6,
        aliases={3: 0, 4: 1},
    )(other, qkv_weight, gain, *grads)
    mixed, grad_tokens = call(finish_kernel, [shaped((6, 12, 4, D), BF16)] * 2, mib=6)(
        tok, cot, own_back, right_back, below_back, corner_back
    )
    return (
        mixed.transpose(2, 0, 1, 3),
        grad_tokens.transpose(2, 0, 1, 3),
        grad_qkv,
        grad_proj,
        grad_gain.reshape(D),
    )


def solution(mesh):
    fine = Mesh(mesh.devices.reshape(tuple(SIZES.values())), AXES)
    grid = P(None, ("xl", "z", "c"), ("y", "xh"), None)
    return jax.shard_map(
        on_device,
        mesh=fine,
        in_specs=(grid, grid, P(None, ("xl", "z", "c"), ("y", "xh")), P(), P(), P()),
        out_specs=(grid, grid, P(), P(), P()),
        check_vma=False,
    )
```

```python
import jax
import jax.numpy as jnp
from jax import lax
from jax.experimental import pallas as pl
from jax.experimental.pallas import tpu as pltpu
from jax.sharding import Mesh, PartitionSpec as P

D = 512
HALF_D = D // 2
HEADS = 8
HEAD = 64
PAIRS = HEADS // 2
WINDOWS = 2
COUNT = 144
TOKENS = WINDOWS * COUNT
HALF_R = 3
HALF_C = 6
EPS = 1e-05
SIZES = {"xl": 2, "zh": 4, "zl": 2, "c": 2, "y": 4, "xh": 2}
AXES = tuple(SIZES)
LAT = AXES[:4]
LON = AXES[4:]
NEAR = ("xh", "xl", "y", "zl")
N_NEAR = 32
FAR = "zh"
N_FAR = 4
CHUNK = 2 * D // N_NEAR
PIECE = (2, HALF_R, HALF_C, 4, D)
F32 = jnp.float32
BF16 = jnp.bfloat16


def dot(left, right):
    return jnp.dot(left, right, preferred_element_type=F32)


def dot_first(left, right):
    return lax.dot_general(left, right, (((0,), (0,)), ((), ())), preferred_element_type=F32)


def dot_last(left, right):
    return lax.dot_general(left, right, (((1,), (1,)), ((), ())), preferred_element_type=F32)


def pack_kernel(tok_ref, cot_ref, own_ref, right_ref, below_ref, corner_ref, sems):
    copies = []
    for n, ref in enumerate((tok_ref, cot_ref)):
        for rows, cols, piece in quadrants(own_ref, right_ref, below_ref, corner_ref):
            sem = sems.at[len(copies)]
            copies.append(pltpu.make_async_copy(ref.at[rows, cols], piece.at[n], sem))
    for copy in copies:
        copy.start()
    for copy in copies:
        copy.wait()


def quadrants(own, right, below, corner):
    late_r, early_r = pl.ds(HALF_R, HALF_R), pl.ds(0, HALF_R)
    late_c, early_c = pl.ds(HALF_C, HALF_C), pl.ds(0, HALF_C)
    return (
        (late_r, late_c, own),
        (late_r, early_c, right),
        (early_r, late_c, below),
        (early_r, early_c, corner),
    )


def source_of(place):
    window = place // COUNT
    rest = place - window * COUNT
    level = (1 + 2 * window + rest % 2) % 4
    return (rest // 2) * 4 + level


def attend_kernel(
    own_ref, right_ref, below_ref, corner_ref, bias_ref, gain_ref, qkv_ref, proj_ref,
    send_ref, left_ref, rows_ref, att_ref, normed_ref, inv_ref,
):
    first = lax.broadcasted_iota(jnp.int32, (TOKENS, TOKENS), 0)
    second = lax.broadcasted_iota(jnp.int32, (TOKENS, TOKENS), 1)
    to_order = (second == source_of(first)).astype(BF16)
    pieces = (own_ref, right_ref, below_ref, corner_ref)

    def gathered(n):
        return jnp.concatenate([ref[n] for ref in pieces], axis=0).reshape(TOKENS, D)

    values = dot(to_order, gathered(0))
    cot = dot(to_order, gathered(1)).astype(BF16)
    gain = gain_ref[...]
    mean = jnp.mean(values, -1, keepdims=True)
    centred = values - mean
    inv_std = lax.rsqrt(jnp.mean(centred * centred, -1, keepdims=True) + EPS)
    normed = centred * inv_std
    hidden = (normed * gain).astype(BF16)
    projected = dot(hidden, qkv_ref[...]).astype(BF16)
    grad_att = dot_last(cot, proj_ref[...]).astype(BF16)
    normed_ref[...] = normed
    inv_ref[...] = inv_std
    left_ref[0] = hidden.T
    rows_ref[3] = cot

    lane = lax.broadcasted_iota(jnp.int32, (COUNT, 2 * HEAD), 1)
    low = lane < HEAD
    zero = jnp.zeros((COUNT, 2 * HEAD), BF16)

    def both(pair):
        return jnp.concatenate([jnp.where(low, pair, zero), jnp.where(low, zero, pair)], axis=0)

    def merged(stacked):
        return jnp.where(low, stacked[:COUNT], stacked[COUNT:]).astype(BF16)

    factor = HEAD ** (-0.5)
    for window in range(WINDOWS):
        here = slice(window * COUNT, (window + 1) * COUNT)
        bias = jnp.concatenate([bias_ref[window]] * 2, axis=0)
        for pair in range(PAIRS):
            cols = slice(pair * 2 * HEAD, (pair + 1) * 2 * HEAD)
            query = both(projected[here, cols])
            keys = projected[here, D + cols.start : D + cols.stop]
            vals = projected[here, 2 * D + cols.start : 2 * D + cols.stop]
            grad_out = both(grad_att[here, cols])
            scores = dot_last(query, keys) * factor + bias
            numer = jnp.exp(scores - jnp.max(scores, -1, keepdims=True))
            weights = numer * (1.0 / jnp.sum(numer, -1, keepdims=True))
            weights_low = weights.astype(BF16)
            att_ref[here, cols] = merged(dot(weights_low, vals))
            grad_weights = dot_last(grad_out, vals)
            inner = jnp.sum(grad_weights * weights, -1, keepdims=True)
            grad_scores = (weights * (grad_weights - inner) * factor).astype(BF16)
            rows_ref[0, here, cols] = merged(dot(grad_scores, keys))
            rows_ref[1, here, cols] = dot_first(grad_scores, query).astype(BF16)
            rows_ref[2, here, cols] = dot_first(weights_low, grad_out).astype(BF16)

    left_ref[1] = att_ref[...].T
    half_grads(1 - lax.axis_index("c"), left_ref, rows_ref, send_ref)


def half_grads(half, left_ref, rows_ref, out_ref):
    here = pl.ds(pl.multiple_of(half * HALF_D, HALF_D), HALF_D)
    for block in range(4):
        out_ref[block] = dot(left_ref[block // 3, here], rows_ref[block]).astype(BF16)


def rest_kernel(
    left_ref, rows_ref, att_ref, normed_ref, inv_ref, gain_ref, qkv_ref, proj_ref,
    keep_ref, own_out, right_out, below_out, corner_out,
):
    half_grads(lax.axis_index("c"), left_ref, rows_ref, keep_ref)
    first = lax.broadcasted_iota(jnp.int32, (TOKENS, TOKENS), 0)
    second = lax.broadcasted_iota(jnp.int32, (TOKENS, TOKENS), 1)
    from_order = (first == source_of(second)).astype(BF16)
    normed = normed_ref[...]
    inv_std = inv_ref[...]
    attended = att_ref[...]
    gain = gain_ref[...]
    branch = dot(attended, proj_ref[...]).astype(BF16)
    grad_hidden = dot_last(rows_ref[0], qkv_ref[:, :D])
    grad_hidden += dot_last(rows_ref[1], qkv_ref[:, D : 2 * D])
    grad_hidden += dot_last(rows_ref[2], qkv_ref[:, 2 * D :])
    grad_norm = grad_hidden * gain
    grad_shift = inv_std * (
        grad_norm
        - jnp.mean(grad_norm, -1, keepdims=True)
        - normed * jnp.mean(grad_norm * normed, -1, keepdims=True)
    )
    for n, result in enumerate((branch, grad_shift.astype(BF16))):
        back = dot(from_order, result).reshape(4, HALF_R, HALF_C, 4, D).astype(BF16)
        for k, ref in enumerate((own_out, right_out, below_out, corner_out)):
            ref[n] = back[k]


def weights_kernel(qkv_ref, proj_ref, gain_ref, qkv_out, proj_out, gain_out, sems):
    copies = [
        pltpu.make_async_copy(ref, out, sems.at[n])
        for n, (ref, out) in enumerate(
            ((qkv_ref, qkv_out), (proj_ref, proj_out), (gain_ref, gain_out))
        )
    ]
    for copy in copies:
        copy.start()
    for copy in copies:
        copy.wait()


def add_kernel(keep_ref, got_ref, out_ref):
    out_ref[...] = (keep_ref[...].astype(F32) + got_ref[...].astype(F32)).astype(BF16)


def spread(got_ref, out_ref):
    total = got_ref[0].astype(F32)
    for n in range(1, got_ref.shape[0]):
        total += got_ref[n].astype(F32)
    total = total.astype(BF16)
    for n in range(out_ref.shape[0]):
        out_ref[n] = total


def sum_kernel(got_ref, a_ref, b_ref, c_ref, out_ref, a_out, b_out, c_out):
    del a_ref, b_ref, c_ref, a_out, b_out, c_out
    spread(got_ref, out_ref)


def spread_kernel(got_ref, right_ref, below_ref, corner_ref, out_ref):
    del right_ref, below_ref, corner_ref
    spread(got_ref, out_ref)


def finish_kernel(tok_ref, cot_ref, own_ref, right_ref, below_ref, corner_ref, mixed_ref, grad_ref):
    for n, (ref, out) in enumerate(((tok_ref, mixed_ref), (cot_ref, grad_ref))):
        for rows, cols, piece in quadrants(own_ref, right_ref, below_ref, corner_ref):
            out[rows, cols] = (ref[rows, cols].astype(F32) + piece[n].astype(F32)).astype(BF16)


def grads_half(half, ref, qkv_ref, gain_ref, qkv_out, proj_out, gain_out, wide, sems):
    copies = []
    here = pl.ds(pl.multiple_of(half * HALF_D, HALF_D), HALF_D)
    total = jnp.zeros((HALF_D, 128), F32)
    for block in range(4):
        part = ref[block].astype(F32)
        wide[block] = part
        cols = pl.ds(block * D, D)
        out = proj_out.at[here] if block == 3 else qkv_out.at[here, cols]
        copy = pltpu.make_async_copy(wide.at[block], out, sems.at[block])
        copy.start()
        copies.append(copy)
        if block < 3:
            product = part * qkv_ref[here, cols].astype(F32)
            for q in range(4):
                total += product[:, q * 128 : (q + 1) * 128]
    sums = jnp.sum(total.T, axis=0, keepdims=True)
    gain_out[:, here] = sums / gain_ref[:, here]
    for copy in copies:
        copy.wait()


def mine_kernel(ref, qkv_ref, gain_ref, qkv_out, proj_out, gain_out, wide, sems):
    gain_out[...] = jnp.zeros_like(gain_out)
    core = lax.axis_index("c")
    grads_half(core, ref, qkv_ref, gain_ref, qkv_out, proj_out, gain_out, wide, sems)


def other_kernel(
    ref, qkv_ref, gain_ref, qkv_in, proj_in, gain_in, qkv_out, proj_out, gain_out, wide, sems
):
    del qkv_in, proj_in
    gain_out[...] = gain_in[...]
    core = lax.axis_index("c")
    grads_half(1 - core, ref, qkv_ref, gain_ref, qkv_out, proj_out, gain_out, wide, sems)


def call(kernel, outs, scratch=(), ins=None, out_specs=None, mib=8, aliases=None):
    more = {"input_output_aliases": aliases or {}}
    if ins is not None:
        more["in_specs"] = ins
    if out_specs is not None:
        more["out_specs"] = out_specs
    return pl.pallas_call(
        kernel,
        out_shape=outs,
        scratch_shapes=list(scratch),
        compiler_params=pltpu.CompilerParams(vmem_limit_bytes=mib * 1024 * 1024),
        **more,
    )


def in_hbm(array):
    return pltpu.with_memory_space_constraint(array, pltpu.HBM)


def shaped(shape, dtype):
    return jax.ShapeDtypeStruct(shape, dtype)


def moved(block, lat_step, lon_step):
    route = [
        (lat * 8 + lon, (lat + lat_step) % 32 * 8 + (lon + lon_step) % 8)
        for lat in range(32)
        for lon in range(8)
    ]
    return lax.ppermute(block, AXES, route)


def swapped(block):
    return lax.ppermute(block, "c", [(0, 1), (1, 0)])


def on_device(tokens, cotangent, region, gain, qkv_weight, proj_weight):
    tok = tokens.transpose(1, 2, 0, 3)
    cot = cotangent.transpose(1, 2, 0, 3)
    anywhere = pl.BlockSpec(memory_space=pl.ANY)
    vmem = pl.BlockSpec(memory_space=pltpu.VMEM)
    hbm = pl.BlockSpec(memory_space=pltpu.HBM)
    own, right, below, corner = call(
        pack_kernel,
        [shaped(PIECE, BF16)] * 4,
        [pltpu.SemaphoreType.DMA((8,))],
        [hbm] * 2,
        [vmem] * 4,
        mib=2,
    )(in_hbm(tok), in_hbm(cot))
    right = moved(right, 0, -1)
    below = moved(below, -1, 0)
    corner = moved(corner, -1, -1)
    ids = region.reshape(2, 2, 2, HALF_R, 2, HALF_C).transpose(0, 2, 4, 3, 5, 1).reshape(2, COUNT)
    bias = jnp.where(ids[:, :, None] == ids[:, None, :], 0.0, -1e30).astype(F32)
    gain = gain.reshape(1, D)
    qkv_weight, proj_weight, gain = call(
        weights_kernel,
        [shaped((D, 3 * D), BF16), shaped((D, D), BF16), shaped((1, D), F32)],
        [pltpu.SemaphoreType.DMA((3,))],
        [hbm] * 3,
        [vmem] * 3,
        mib=1,
    )(in_hbm(qkv_weight), in_hbm(proj_weight), in_hbm(gain))
    send, *state = call(
        attend_kernel,
        [
            shaped((4, HALF_D, D), BF16),
            shaped((2, D, TOKENS), BF16),
            shaped((4, TOKENS, D), BF16),
            shaped((TOKENS, D), BF16),
            shaped((TOKENS, D), F32),
            shaped((TOKENS, 1), F32),
        ],
        mib=16,
    )(own, right, below, corner, bias, gain, qkv_weight, proj_weight)
    got = swapped(send)
    keep, own_back, right_back, below_back, corner_back = call(
        rest_kernel, [shaped((4, HALF_D, D), BF16)] + [shaped(PIECE, BF16)] * 4, mib=16
    )(*state, gain, qkv_weight, proj_weight)
    half = call(add_kernel, shaped((4, HALF_D, D), BF16), mib=4)(keep, got)
    got = lax.all_to_all(half.reshape(N_NEAR, CHUNK, D), NEAR, 0, 0)
    parts, right_back, below_back, corner_back = call(
        sum_kernel,
        [shaped((N_FAR, CHUNK, D), BF16)] + [shaped(PIECE, BF16)] * 3,
        ins=[vmem] + [anywhere] * 3,
        out_specs=[vmem] + [anywhere] * 3,
        mib=4,
        aliases={1: 1, 2: 2, 3: 3},
    )(got, right_back, below_back, corner_back)
    right_back = moved(right_back, 0, 1)
    below_back = moved(below_back, 1, 0)
    corner_back = moved(corner_back, 1, 1)
    got = lax.all_to_all(parts, FAR, 0, 0)
    parts = call(
        spread_kernel,
        shaped((N_NEAR, CHUNK, D), BF16),
        ins=[vmem] + [anywhere] * 3,
        out_specs=vmem,
        mib=4,
    )(got, right_back, below_back, corner_back)
    mine = lax.all_to_all(parts, NEAR, 0, 0)
    mine = mine.reshape(4, HALF_D, D)
    other = swapped(mine)
    grads = call(
        mine_kernel,
        [shaped((D, 3 * D), F32), shaped((D, D), F32), shaped((1, D), F32)],
        [pltpu.VMEM((4, HALF_D, D), F32), pltpu.SemaphoreType.DMA((4,))],
        [vmem] * 3,
        [anywhere, anywhere, vmem],
        mib=6,
    )(mine, qkv_weight, gain)
    grad_qkv, grad_proj, grad_gain = call(
        other_kernel,
        [shaped((D, 3 * D), F32), shaped((D, D), F32), shaped((1, D), F32)],
        [pltpu.VMEM((4, HALF_D, D), F32), pltpu.SemaphoreType.DMA((4,))],
        [vmem] * 3 + [anywhere] * 2 + [vmem],
        [anywhere, anywhere, vmem],
        mib=6,
        aliases={3: 0, 4: 1},
    )(other, qkv_weight, gain, *grads)
    mixed, grad_tokens = call(finish_kernel, [shaped((6, 12, 4, D), BF16)] * 2, mib=6)(
        tok, cot, own_back, right_back, below_back, corner_back
    )
    return (
        mixed.transpose(2, 0, 1, 3),
        grad_tokens.transpose(2, 0, 1, 3),
        grad_qkv,
        grad_proj,
        grad_gain.reshape(D),
    )


def solution(mesh):
    fine = Mesh(mesh.devices.reshape(tuple(SIZES.values())), AXES)
    grid = P(None, LAT, LON, None)
    return jax.shard_map(
        on_device,
        mesh=fine,
        in_specs=(grid, grid, P(None, LAT, LON), P(), P(), P()),
        out_specs=(grid, grid, P(), P(), P()),
        check_vma=False,
    )
```

```python
import jax
import jax.numpy as jnp
from jax import lax
from jax.experimental import pallas as pl
from jax.experimental.pallas import tpu as pltpu
from jax.sharding import Mesh, PartitionSpec as P

D = 512
HALF_D = D // 2
HEADS = 8
HEAD = 64
PAIRS = HEADS // 2
WINDOWS = 2
COUNT = 144
TOKENS = WINDOWS * COUNT
HALF_R = 3
HALF_C = 6
EPS = 1e-05
SIZES = {"xl": 2, "zh": 4, "zl": 2, "c": 2, "y": 4, "xh": 2}
AXES = tuple(SIZES)
LAT = AXES[:4]
LON = AXES[4:]
NEAR = ("xh", "xl", "y", "zl")
N_NEAR = 32
FAR = "zh"
N_FAR = 4
CHUNK = 2 * D // N_NEAR
PIECE = (2, HALF_R, HALF_C, 4, D)
F32 = jnp.float32
BF16 = jnp.bfloat16


def dot(left, right):
    return jnp.dot(left, right, preferred_element_type=F32)


def dot_first(left, right):
    return lax.dot_general(left, right, (((0,), (0,)), ((), ())), preferred_element_type=F32)


def dot_last(left, right):
    return lax.dot_general(left, right, (((1,), (1,)), ((), ())), preferred_element_type=F32)


def pack_kernel(tok_ref, cot_ref, own_ref, right_ref, below_ref, corner_ref, sems):
    copies = []
    for n, ref in enumerate((tok_ref, cot_ref)):
        for rows, cols, piece in quadrants(own_ref, right_ref, below_ref, corner_ref):
            sem = sems.at[len(copies)]
            copies.append(pltpu.make_async_copy(ref.at[rows, cols], piece.at[n], sem))
    for copy in copies:
        copy.start()
    for copy in copies:
        copy.wait()


def quadrants(own, right, below, corner):
    late_r, early_r = pl.ds(HALF_R, HALF_R), pl.ds(0, HALF_R)
    late_c, early_c = pl.ds(HALF_C, HALF_C), pl.ds(0, HALF_C)
    return (
        (late_r, late_c, own),
        (late_r, early_c, right),
        (early_r, late_c, below),
        (early_r, early_c, corner),
    )


def source_of(place):
    window = place // COUNT
    rest = place - window * COUNT
    level = (1 + 2 * window + rest % 2) % 4
    return (rest // 2) * 4 + level


def attend_kernel(
    own_ref, right_ref, below_ref, corner_ref, bias_ref, gain_ref, qkv_ref, proj_ref,
    send_ref, left_ref, rows_ref, att_ref, normed_ref, inv_ref,
):
    first = lax.broadcasted_iota(jnp.int32, (TOKENS, TOKENS), 0)
    second = lax.broadcasted_iota(jnp.int32, (TOKENS, TOKENS), 1)
    to_order = (second == source_of(first)).astype(BF16)
    pieces = (own_ref, right_ref, below_ref, corner_ref)

    def gathered(n):
        return jnp.concatenate([ref[n] for ref in pieces], axis=0).reshape(TOKENS, D)

    values = dot(to_order, gathered(0))
    cot = dot(to_order, gathered(1)).astype(BF16)
    gain = gain_ref[...]
    mean = jnp.mean(values, -1, keepdims=True)
    centred = values - mean
    inv_std = lax.rsqrt(jnp.mean(centred * centred, -1, keepdims=True) + EPS)
    normed = centred * inv_std
    hidden = (normed * gain).astype(BF16)
    projected = dot(hidden, qkv_ref[...]).astype(BF16)
    grad_att = dot_last(cot, proj_ref[...]).astype(BF16)
    normed_ref[...] = normed
    inv_ref[...] = inv_std
    left_ref[0] = hidden.T
    rows_ref[3] = cot

    lane = lax.broadcasted_iota(jnp.int32, (COUNT, 2 * HEAD), 1)
    low = lane < HEAD
    zero = jnp.zeros((COUNT, 2 * HEAD), BF16)

    def both(pair):
        return jnp.concatenate([jnp.where(low, pair, zero), jnp.where(low, zero, pair)], axis=0)

    def merged(stacked):
        return jnp.where(low, stacked[:COUNT], stacked[COUNT:]).astype(BF16)

    factor = HEAD ** (-0.5)
    for window in range(WINDOWS):
        here = slice(window * COUNT, (window + 1) * COUNT)
        bias = jnp.concatenate([bias_ref[window]] * 2, axis=0)
        for pair in range(PAIRS):
            cols = slice(pair * 2 * HEAD, (pair + 1) * 2 * HEAD)
            query = both(projected[here, cols])
            keys = projected[here, D + cols.start : D + cols.stop]
            vals = projected[here, 2 * D + cols.start : 2 * D + cols.stop]
            grad_out = both(grad_att[here, cols])
            scores = dot_last(query, keys) * factor + bias
            numer = jnp.exp(scores - jnp.max(scores, -1, keepdims=True))
            weights = numer * (1.0 / jnp.sum(numer, -1, keepdims=True))
            weights_low = weights.astype(BF16)
            att_ref[here, cols] = merged(dot(weights_low, vals))
            grad_weights = dot_last(grad_out, vals)
            inner = jnp.sum(grad_weights * weights, -1, keepdims=True)
            grad_scores = (weights * (grad_weights - inner) * factor).astype(BF16)
            rows_ref[0, here, cols] = merged(dot(grad_scores, keys))
            rows_ref[1, here, cols] = dot_first(grad_scores, query).astype(BF16)
            rows_ref[2, here, cols] = dot_first(weights_low, grad_out).astype(BF16)

    left_ref[1] = att_ref[...].T
    half_grads(1 - lax.axis_index("c"), left_ref, rows_ref, send_ref)


def half_grads(half, left_ref, rows_ref, out_ref):
    here = pl.ds(pl.multiple_of(half * HALF_D, HALF_D), HALF_D)
    for block in range(4):
        out_ref[block] = dot(left_ref[block // 3, here], rows_ref[block]).astype(BF16)


def rest_kernel(
    left_ref, rows_ref, att_ref, normed_ref, inv_ref, gain_ref, qkv_ref, proj_ref,
    keep_ref, own_out, right_out, below_out, corner_out,
):
    half_grads(lax.axis_index("c"), left_ref, rows_ref, keep_ref)
    first = lax.broadcasted_iota(jnp.int32, (TOKENS, TOKENS), 0)
    second = lax.broadcasted_iota(jnp.int32, (TOKENS, TOKENS), 1)
    from_order = (first == source_of(second)).astype(BF16)
    normed = normed_ref[...]
    inv_std = inv_ref[...]
    attended = att_ref[...]
    gain = gain_ref[...]
    branch = dot(attended, proj_ref[...]).astype(BF16)
    grad_hidden = dot_last(rows_ref[0], qkv_ref[:, :D])
    grad_hidden += dot_last(rows_ref[1], qkv_ref[:, D : 2 * D])
    grad_hidden += dot_last(rows_ref[2], qkv_ref[:, 2 * D :])
    grad_norm = grad_hidden * gain
    grad_shift = inv_std * (
        grad_norm
        - jnp.mean(grad_norm, -1, keepdims=True)
        - normed * jnp.mean(grad_norm * normed, -1, keepdims=True)
    )
    for n, result in enumerate((branch, grad_shift.astype(BF16))):
        back = dot(from_order, result).reshape(4, HALF_R, HALF_C, 4, D).astype(BF16)
        for k, ref in enumerate((own_out, right_out, below_out, corner_out)):
            ref[n] = back[k]


def weights_kernel(qkv_ref, proj_ref, gain_ref, qkv_out, proj_out, gain_out, sems):
    copies = [
        pltpu.make_async_copy(ref, out, sems.at[n])
        for n, (ref, out) in enumerate(
            ((qkv_ref, qkv_out), (proj_ref, proj_out), (gain_ref, gain_out))
        )
    ]
    for copy in copies:
        copy.start()
    for copy in copies:
        copy.wait()


def add_kernel(keep_ref, got_ref, out_ref):
    out_ref[...] = (keep_ref[...].astype(F32) + got_ref[...].astype(F32)).astype(BF16)


def sum_kernel(got_ref, below_ref, a_ref, b_ref, out_ref, a_out, b_out):
    del below_ref
    del a_ref, b_ref, a_out, b_out
    total = got_ref[0].astype(F32)
    for n in range(1, got_ref.shape[0]):
        total += got_ref[n].astype(F32)
    out_ref[...] = total.astype(BF16)


def spread_kernel(own_ref, one_ref, two_ref, three_ref, right_ref, corner_ref, out_ref):
    del right_ref, corner_ref
    even = own_ref[...].astype(F32) + two_ref[...].astype(F32)
    odd = one_ref[...].astype(F32) + three_ref[...].astype(F32)
    total = (even + odd).astype(BF16)
    for n in range(out_ref.shape[0]):
        out_ref[n] = total


def finish_kernel(tok_ref, cot_ref, own_ref, right_ref, below_ref, corner_ref, mixed_ref, grad_ref):
    for n, (ref, out) in enumerate(((tok_ref, mixed_ref), (cot_ref, grad_ref))):
        for rows, cols, piece in quadrants(own_ref, right_ref, below_ref, corner_ref):
            out[rows, cols] = (ref[rows, cols].astype(F32) + piece[n].astype(F32)).astype(BF16)


def grads_half(half, ref, qkv_ref, gain_ref, qkv_out, proj_out, gain_out, wide, sems):
    copies = []
    here = pl.ds(pl.multiple_of(half * HALF_D, HALF_D), HALF_D)
    total = jnp.zeros((HALF_D, 128), F32)
    for block in range(4):
        part = ref[block].astype(F32)
        wide[block] = part
        cols = pl.ds(block * D, D)
        out = proj_out.at[here] if block == 3 else qkv_out.at[here, cols]
        copy = pltpu.make_async_copy(wide.at[block], out, sems.at[block])
        copy.start()
        copies.append(copy)
        if block < 3:
            product = part * qkv_ref[here, cols].astype(F32)
            for q in range(4):
                total += product[:, q * 128 : (q + 1) * 128]
    sums = jnp.sum(total.T, axis=0, keepdims=True)
    gain_out[:, here] = sums / gain_ref[:, here]
    for copy in copies:
        copy.wait()


def mine_kernel(ref, qkv_ref, gain_ref, qkv_out, proj_out, gain_out, wide, sems):
    gain_out[...] = jnp.zeros_like(gain_out)
    core = lax.axis_index("c")
    grads_half(core, ref, qkv_ref, gain_ref, qkv_out, proj_out, gain_out, wide, sems)


def other_kernel(
    ref, qkv_ref, gain_ref, qkv_in, proj_in, gain_in, qkv_out, proj_out, gain_out, wide, sems
):
    del qkv_in, proj_in
    gain_out[...] = gain_in[...]
    core = lax.axis_index("c")
    grads_half(1 - core, ref, qkv_ref, gain_ref, qkv_out, proj_out, gain_out, wide, sems)


def call(kernel, outs, scratch=(), ins=None, out_specs=None, mib=8, aliases=None):
    more = {"input_output_aliases": aliases or {}}
    if ins is not None:
        more["in_specs"] = ins
    if out_specs is not None:
        more["out_specs"] = out_specs
    return pl.pallas_call(
        kernel,
        out_shape=outs,
        scratch_shapes=list(scratch),
        compiler_params=pltpu.CompilerParams(vmem_limit_bytes=mib * 1024 * 1024),
        **more,
    )


def in_hbm(array):
    return pltpu.with_memory_space_constraint(array, pltpu.HBM)


def shaped(shape, dtype):
    return jax.ShapeDtypeStruct(shape, dtype)


def moved(block, lat_step, lon_step):
    route = [
        (lat * 8 + lon, (lat + lat_step) % 32 * 8 + (lon + lon_step) % 8)
        for lat in range(32)
        for lon in range(8)
    ]
    return lax.ppermute(block, AXES, route)


def swapped(block):
    return lax.ppermute(block, "c", [(0, 1), (1, 0)])


def on_device(tokens, cotangent, region, gain, qkv_weight, proj_weight):
    tok = tokens.transpose(1, 2, 0, 3)
    cot = cotangent.transpose(1, 2, 0, 3)
    anywhere = pl.BlockSpec(memory_space=pl.ANY)
    vmem = pl.BlockSpec(memory_space=pltpu.VMEM)
    hbm = pl.BlockSpec(memory_space=pltpu.HBM)
    own, right, below, corner = call(
        pack_kernel,
        [shaped(PIECE, BF16)] * 4,
        [pltpu.SemaphoreType.DMA((8,))],
        [hbm] * 2,
        [vmem] * 4,
        mib=2,
    )(in_hbm(tok), in_hbm(cot))
    corner = moved(corner, -1, -1)
    right = moved(right, 0, -1)
    below = moved(below, -1, 0)
    ids = region.reshape(2, 2, 2, HALF_R, 2, HALF_C).transpose(0, 2, 4, 3, 5, 1).reshape(2, COUNT)
    bias = jnp.where(ids[:, :, None] == ids[:, None, :], 0.0, -1e30).astype(F32)
    gain = gain.reshape(1, D)
    qkv_weight, proj_weight, gain = call(
        weights_kernel,
        [shaped((D, 3 * D), BF16), shaped((D, D), BF16), shaped((1, D), F32)],
        [pltpu.SemaphoreType.DMA((3,))],
        [hbm] * 3,
        [vmem] * 3,
        mib=1,
    )(in_hbm(qkv_weight), in_hbm(proj_weight), in_hbm(gain))
    send, *state = call(
        attend_kernel,
        [
            shaped((4, HALF_D, D), BF16),
            shaped((2, D, TOKENS), BF16),
            shaped((4, TOKENS, D), BF16),
            shaped((TOKENS, D), BF16),
            shaped((TOKENS, D), F32),
            shaped((TOKENS, 1), F32),
        ],
        mib=16,
    )(own, right, below, corner, bias, gain, qkv_weight, proj_weight)
    got = swapped(send)
    keep, own_back, right_back, below_back, corner_back = call(
        rest_kernel, [shaped((4, HALF_D, D), BF16)] + [shaped(PIECE, BF16)] * 4, mib=16
    )(*state, gain, qkv_weight, proj_weight)
    half = call(add_kernel, shaped((4, HALF_D, D), BF16), mib=4)(keep, got)
    got = lax.all_to_all(half.reshape(N_NEAR, CHUNK, D), NEAR, 0, 0)
    below_back = moved(below_back, 1, 0)
    part, right_back, corner_back = call(
        sum_kernel,
        [shaped((CHUNK, D), BF16)] + [shaped(PIECE, BF16)] * 2,
        ins=[vmem] + [anywhere] * 3,
        out_specs=[vmem] + [anywhere] * 2,
        mib=4,
        aliases={2: 1, 3: 2},
    )(got, below_back, right_back, corner_back)
    others = [
        lax.ppermute(part, FAR, [(n, (n - step) % N_FAR) for n in range(N_FAR)])
        for step in range(1, N_FAR)
    ]
    corner_back = moved(corner_back, 1, 1)
    right_back = moved(right_back, 0, 1)
    parts = call(
        spread_kernel,
        shaped((N_NEAR, CHUNK, D), BF16),
        ins=[vmem] * 4 + [anywhere] * 2,
        out_specs=vmem,
        mib=4,
    )(part, *others, right_back, corner_back)
    mine = lax.all_to_all(parts, NEAR, 0, 0)
    mine = mine.reshape(4, HALF_D, D)
    other = swapped(mine)
    grads = call(
        mine_kernel,
        [shaped((D, 3 * D), F32), shaped((D, D), F32), shaped((1, D), F32)],
        [pltpu.VMEM((4, HALF_D, D), F32), pltpu.SemaphoreType.DMA((4,))],
        [vmem] * 3,
        [anywhere, anywhere, vmem],
        mib=6,
    )(mine, qkv_weight, gain)
    grad_qkv, grad_proj, grad_gain = call(
        other_kernel,
        [shaped((D, 3 * D), F32), shaped((D, D), F32), shaped((1, D), F32)],
        [pltpu.VMEM((4, HALF_D, D), F32), pltpu.SemaphoreType.DMA((4,))],
        [vmem] * 3 + [anywhere] * 2 + [vmem],
        [anywhere, anywhere, vmem],
        mib=6,
        aliases={3: 0, 4: 1},
    )(other, qkv_weight, gain, *grads)
    mixed, grad_tokens = call(finish_kernel, [shaped((6, 12, 4, D), BF16)] * 2, mib=6)(
        tok, cot, own_back, right_back, below_back, corner_back
    )
    return (
        mixed.transpose(2, 0, 1, 3),
        grad_tokens.transpose(2, 0, 1, 3),
        grad_qkv,
        grad_proj,
        grad_gain.reshape(D),
    )


def solution(mesh):
    fine = Mesh(mesh.devices.reshape(tuple(SIZES.values())), AXES)
    grid = P(None, LAT, LON, None)
    return jax.shard_map(
        on_device,
        mesh=fine,
        in_specs=(grid, grid, P(None, LAT, LON), P(), P(), P()),
        out_specs=(grid, grid, P(), P(), P()),
        check_vma=False,
    )
```

```python
import jax
import jax.numpy as jnp
from jax import lax
from jax.experimental import pallas as pl
from jax.experimental.pallas import tpu as pltpu
from jax.sharding import Mesh, PartitionSpec as P

D = 512
HALF_D = D // 2
HEADS = 8
HEAD = 64
PAIRS = HEADS // 2
WINDOWS = 2
COUNT = 144
TOKENS = WINDOWS * COUNT
HALF_R = 3
HALF_C = 6
EPS = 1e-05
SIZES = {"xl": 2, "zh": 4, "zl": 2, "c": 2, "y": 4, "xh": 2}
AXES = tuple(SIZES)
LAT = AXES[:4]
LON = AXES[4:]
NEAR = ("xh", "xl", "y", "zl")
N_NEAR = 32
FAR = "zh"
N_FAR = 4
CHUNK = D // N_NEAR
CHAINS = ((2, 3), (0, 1))
PIECE = (2, HALF_R, HALF_C, 4, D)
F32 = jnp.float32
BF16 = jnp.bfloat16


def dot(left, right):
    return jnp.dot(left, right, preferred_element_type=F32)


def dot_first(left, right):
    return lax.dot_general(left, right, (((0,), (0,)), ((), ())), preferred_element_type=F32)


def dot_last(left, right):
    return lax.dot_general(left, right, (((1,), (1,)), ((), ())), preferred_element_type=F32)


def pack_kernel(tok_ref, cot_ref, own_ref, right_ref, below_ref, corner_ref, sems):
    copies = []
    for n, ref in enumerate((tok_ref, cot_ref)):
        for rows, cols, piece in quadrants(own_ref, right_ref, below_ref, corner_ref):
            sem = sems.at[len(copies)]
            copies.append(pltpu.make_async_copy(ref.at[rows, cols], piece.at[n], sem))
    for copy in copies:
        copy.start()
    for copy in copies:
        copy.wait()


def quadrants(own, right, below, corner):
    late_r, early_r = pl.ds(HALF_R, HALF_R), pl.ds(0, HALF_R)
    late_c, early_c = pl.ds(HALF_C, HALF_C), pl.ds(0, HALF_C)
    return (
        (late_r, late_c, own),
        (late_r, early_c, right),
        (early_r, late_c, below),
        (early_r, early_c, corner),
    )


def source_of(place):
    window = place // COUNT
    rest = place - window * COUNT
    level = (1 + 2 * window + rest % 2) % 4
    return (rest // 2) * 4 + level


def attend_kernel(
    own_ref, right_ref, below_ref, corner_ref, bias_ref, gain_ref, qkv_ref, proj_ref,
    send_1, send_2, left_ref, rows_ref, att_ref, normed_ref, inv_ref,
):
    first = lax.broadcasted_iota(jnp.int32, (TOKENS, TOKENS), 0)
    second = lax.broadcasted_iota(jnp.int32, (TOKENS, TOKENS), 1)
    to_order = (second == source_of(first)).astype(BF16)
    pieces = (own_ref, right_ref, below_ref, corner_ref)

    def gathered(n):
        return jnp.concatenate([ref[n] for ref in pieces], axis=0).reshape(TOKENS, D)

    values = dot(to_order, gathered(0))
    cot = dot(to_order, gathered(1)).astype(BF16)
    gain = gain_ref[...]
    mean = jnp.mean(values, -1, keepdims=True)
    centred = values - mean
    inv_std = lax.rsqrt(jnp.mean(centred * centred, -1, keepdims=True) + EPS)
    normed = centred * inv_std
    hidden = (normed * gain).astype(BF16)
    projected = dot(hidden, qkv_ref[...]).astype(BF16)
    grad_att = dot_last(cot, proj_ref[...]).astype(BF16)
    normed_ref[...] = normed
    inv_ref[...] = inv_std
    left_ref[0] = hidden.T
    rows_ref[3] = cot

    lane = lax.broadcasted_iota(jnp.int32, (COUNT, 2 * HEAD), 1)
    low = lane < HEAD
    zero = jnp.zeros((COUNT, 2 * HEAD), BF16)

    def both(pair):
        return jnp.concatenate([jnp.where(low, pair, zero), jnp.where(low, zero, pair)], axis=0)

    def merged(stacked):
        return jnp.where(low, stacked[:COUNT], stacked[COUNT:]).astype(BF16)

    factor = HEAD ** (-0.5)
    for window in range(WINDOWS):
        here = slice(window * COUNT, (window + 1) * COUNT)
        bias = jnp.concatenate([bias_ref[window]] * 2, axis=0)
        for pair in range(PAIRS):
            cols = slice(pair * 2 * HEAD, (pair + 1) * 2 * HEAD)
            query = both(projected[here, cols])
            keys = projected[here, D + cols.start : D + cols.stop]
            vals = projected[here, 2 * D + cols.start : 2 * D + cols.stop]
            grad_out = both(grad_att[here, cols])
            scores = dot_last(query, keys) * factor + bias
            numer = jnp.exp(scores - jnp.max(scores, -1, keepdims=True))
            weights = numer * (1.0 / jnp.sum(numer, -1, keepdims=True))
            weights_low = weights.astype(BF16)
            att_ref[here, cols] = merged(dot(weights_low, vals))
            grad_weights = dot_last(grad_out, vals)
            inner = jnp.sum(grad_weights * weights, -1, keepdims=True)
            grad_scores = (weights * (grad_weights - inner) * factor).astype(BF16)
            rows_ref[0, here, cols] = merged(dot(grad_scores, keys))
            rows_ref[1, here, cols] = dot_first(grad_scores, query).astype(BF16)
            rows_ref[2, here, cols] = dot_first(weights_low, grad_out).astype(BF16)

    left_ref[1] = att_ref[...].T
    for blocks, out_ref in zip(CHAINS, (send_1, send_2)):
        half_grads(1 - lax.axis_index("c"), blocks, left_ref, rows_ref, out_ref)


def half_grads(half, blocks, left_ref, rows_ref, out_ref):
    here = pl.ds(pl.multiple_of(half * HALF_D, HALF_D), HALF_D)
    for n, block in enumerate(blocks):
        out_ref[n] = dot(left_ref[block // 3, here], rows_ref[block]).astype(BF16)


def keep_kernel(left_ref, rows_ref, keep_ref):
    half_grads(lax.axis_index("c"), CHAINS[0], left_ref, rows_ref, keep_ref)


def rest_kernel(
    left_ref, rows_ref, att_ref, normed_ref, inv_ref, gain_ref, qkv_ref, proj_ref,
    keep_ref, own_out, right_out, below_out, corner_out,
):
    half_grads(lax.axis_index("c"), CHAINS[1], left_ref, rows_ref, keep_ref)
    first = lax.broadcasted_iota(jnp.int32, (TOKENS, TOKENS), 0)
    second = lax.broadcasted_iota(jnp.int32, (TOKENS, TOKENS), 1)
    from_order = (first == source_of(second)).astype(BF16)
    normed = normed_ref[...]
    inv_std = inv_ref[...]
    attended = att_ref[...]
    gain = gain_ref[...]
    branch = dot(attended, proj_ref[...]).astype(BF16)
    grad_hidden = dot_last(rows_ref[0], qkv_ref[:, :D])
    grad_hidden += dot_last(rows_ref[1], qkv_ref[:, D : 2 * D])
    grad_hidden += dot_last(rows_ref[2], qkv_ref[:, 2 * D :])
    grad_norm = grad_hidden * gain
    grad_shift = inv_std * (
        grad_norm
        - jnp.mean(grad_norm, -1, keepdims=True)
        - normed * jnp.mean(grad_norm * normed, -1, keepdims=True)
    )
    for n, result in enumerate((branch, grad_shift.astype(BF16))):
        back = dot(from_order, result).reshape(4, HALF_R, HALF_C, 4, D).astype(BF16)
        for k, ref in enumerate((own_out, right_out, below_out, corner_out)):
            ref[n] = back[k]


def weights_kernel(qkv_ref, proj_ref, gain_ref, qkv_out, proj_out, gain_out, sems):
    copies = [
        pltpu.make_async_copy(ref, out, sems.at[n])
        for n, (ref, out) in enumerate(
            ((qkv_ref, qkv_out), (proj_ref, proj_out), (gain_ref, gain_out))
        )
    ]
    for copy in copies:
        copy.start()
    for copy in copies:
        copy.wait()


def add_kernel(keep_ref, got_ref, out_ref):
    out_ref[...] = (keep_ref[...].astype(F32) + got_ref[...].astype(F32)).astype(BF16)


def sum_kernel(got_ref, *refs):
    total = got_ref[0].astype(F32)
    for n in range(1, got_ref.shape[0]):
        total += got_ref[n].astype(F32)
    refs[-1][...] = total.astype(BF16)


def spread_kernel(own_ref, one_ref, two_ref, three_ref, *refs):
    even = own_ref[...].astype(F32) + two_ref[...].astype(F32)
    odd = one_ref[...].astype(F32) + three_ref[...].astype(F32)
    total = (even + odd).astype(BF16)
    for n in range(N_NEAR):
        refs[-1][n] = total


def finish_kernel(tok_ref, cot_ref, own_ref, right_ref, below_ref, corner_ref, mixed_ref, grad_ref):
    for n, (ref, out) in enumerate(((tok_ref, mixed_ref), (cot_ref, grad_ref))):
        for rows, cols, piece in quadrants(own_ref, right_ref, below_ref, corner_ref):
            out[rows, cols] = (ref[rows, cols].astype(F32) + piece[n].astype(F32)).astype(BF16)


def write_half(half, ref, blocks, qkv_ref, qkv_out, proj_out, wide, sems):
    copies = []
    here = pl.ds(pl.multiple_of(half * HALF_D, HALF_D), HALF_D)
    total = jnp.zeros((HALF_D, 128), F32)
    for n, block in enumerate(blocks):
        part = ref[n].astype(F32)
        wide[n] = part
        cols = pl.ds(block * D, D)
        out = proj_out.at[here] if block == 3 else qkv_out.at[here, cols]
        copy = pltpu.make_async_copy(wide.at[n], out, sems.at[n])
        copy.start()
        copies.append(copy)
        if block < 3:
            product = part * qkv_ref[here, cols].astype(F32)
            for q in range(4):
                total += product[:, q * 128 : (q + 1) * 128]
    return here, jnp.sum(total.T, axis=0, keepdims=True), copies


def first_kernel(mine_ref, other_ref, qkv_ref, qkv_out, proj_out, gain_out, wide, sems):
    core = lax.axis_index("c")
    started = []
    for n, (ref, half) in enumerate(((mine_ref, core), (other_ref, 1 - core))):
        here, sums, copies = write_half(
            half, ref, CHAINS[0], qkv_ref, qkv_out, proj_out, wide.at[n], sems.at[n]
        )
        gain_out[:, here] = sums
        started += copies
    for copy in started:
        copy.wait()


def mine_kernel(ref, qkv_ref, gain_in, qkv_in, qkv_out, gain_out, wide, sems):
    del qkv_in
    gain_out[...] = gain_in[...]
    core = lax.axis_index("c")
    here, sums, copies = write_half(core, ref, CHAINS[1], qkv_ref, qkv_out, None, wide, sems)
    gain_out[:, here] += sums
    for copy in copies:
        copy.wait()


def other_kernel(ref, qkv_ref, gain_in, qkv_in, gain_ref, qkv_out, gain_out, wide, sems):
    del qkv_in
    gain_out[...] = gain_in[...]
    core = lax.axis_index("c")
    here, sums, copies = write_half(1 - core, ref, CHAINS[1], qkv_ref, qkv_out, None, wide, sems)
    gain_out[:, here] += sums
    gain_out[...] = gain_out[...] / gain_ref[...]
    for copy in copies:
        copy.wait()


def call(kernel, outs, scratch=(), ins=None, out_specs=None, mib=8, aliases=None):
    more = {"input_output_aliases": aliases or {}}
    if ins is not None:
        more["in_specs"] = ins
    if out_specs is not None:
        more["out_specs"] = out_specs
    return pl.pallas_call(
        kernel,
        out_shape=outs,
        scratch_shapes=list(scratch),
        compiler_params=pltpu.CompilerParams(vmem_limit_bytes=mib * 1024 * 1024),
        **more,
    )


def in_hbm(array):
    return pltpu.with_memory_space_constraint(array, pltpu.HBM)


def shaped(shape, dtype):
    return jax.ShapeDtypeStruct(shape, dtype)


def moved(block, lat_step, lon_step):
    route = [
        (lat * 8 + lon, (lat + lat_step) % 32 * 8 + (lon + lon_step) % 8)
        for lat in range(32)
        for lon in range(8)
    ]
    return lax.ppermute(block, AXES, route)


def swapped(block):
    return lax.ppermute(block, "c", [(0, 1), (1, 0)])


def on_device(tokens, cotangent, region, gain, qkv_weight, proj_weight):
    tok = tokens.transpose(1, 2, 0, 3)
    cot = cotangent.transpose(1, 2, 0, 3)
    anywhere = pl.BlockSpec(memory_space=pl.ANY)
    vmem = pl.BlockSpec(memory_space=pltpu.VMEM)
    hbm = pl.BlockSpec(memory_space=pltpu.HBM)
    own, right, below, corner = call(
        pack_kernel,
        [shaped(PIECE, BF16)] * 4,
        [pltpu.SemaphoreType.DMA((8,))],
        [hbm] * 2,
        [vmem] * 4,
        mib=2,
    )(in_hbm(tok), in_hbm(cot))
    corner = moved(corner, -1, -1)
    right = moved(right, 0, -1)
    below = moved(below, -1, 0)
    ids = region.reshape(2, 2, 2, HALF_R, 2, HALF_C).transpose(0, 2, 4, 3, 5, 1).reshape(2, COUNT)
    bias = jnp.where(ids[:, :, None] == ids[:, None, :], 0.0, -1e30).astype(F32)
    gain = gain.reshape(1, D)
    qkv_weight, proj_weight, gain = call(
        weights_kernel,
        [shaped((D, 3 * D), BF16), shaped((D, D), BF16), shaped((1, D), F32)],
        [pltpu.SemaphoreType.DMA((3,))],
        [hbm] * 3,
        [vmem] * 3,
        mib=1,
    )(in_hbm(qkv_weight), in_hbm(proj_weight), in_hbm(gain))
    two = shaped((2, HALF_D, D), BF16)
    send_1, send_2, *state = call(
        attend_kernel,
        [
            two,
            two,
            shaped((2, D, TOKENS), BF16),
            shaped((4, TOKENS, D), BF16),
            shaped((TOKENS, D), BF16),
            shaped((TOKENS, D), F32),
            shaped((TOKENS, 1), F32),
        ],
        mib=16,
    )(own, right, below, corner, bias, gain, qkv_weight, proj_weight)
    got_1, got_2 = swapped(send_1), swapped(send_2)
    keep_1 = call(keep_kernel, two, mib=4)(*state[:2])
    keep_2, own_back, right_back, below_back, corner_back = call(
        rest_kernel, [two] + [shaped(PIECE, BF16)] * 4, mib=16
    )(*state, gain, qkv_weight, proj_weight)

    def scattered(keep, got):
        half = call(add_kernel, two, mib=4)(keep, got)
        return lax.all_to_all(half.reshape(N_NEAR, CHUNK, D), NEAR, 0, 0)

    def combined(got, after):
        return call(
            sum_kernel,
            shaped((CHUNK, D), BF16),
            ins=[vmem] + [anywhere] * len(after),
            out_specs=vmem,
            mib=4,
        )(got, *after)

    def gathered(part, after):
        others = [
            lax.ppermute(part, FAR, [(n, (n - step) % N_FAR) for n in range(N_FAR)])
            for step in range(1, N_FAR)
        ]
        parts = call(
            spread_kernel,
            shaped((N_NEAR, CHUNK, D), BF16),
            ins=[vmem] * 4 + [anywhere] * len(after),
            out_specs=vmem,
            mib=4,
        )(part, *others, *after)
        return lax.all_to_all(parts, NEAR, 0, 0).reshape(2, HALF_D, D)

    got_1 = scattered(keep_1, got_1)
    got_2 = scattered(keep_2, got_2)
    corner_back = moved(corner_back, 1, 1)
    below_back = moved(below_back, 1, 0)
    right_back = moved(right_back, 0, 1)
    part_1 = combined(got_1, [])
    part_2 = combined(got_2, [corner_back, below_back])
    mine_1 = gathered(part_1, [])
    mine_2 = gathered(part_2, [right_back])
    other_1 = swapped(mine_1)
    other_2 = swapped(mine_2)
    grad_qkv, grad_proj, grad_gain = call(
        first_kernel,
        [shaped((D, 3 * D), F32), shaped((D, D), F32), shaped((1, D), F32)],
        [pltpu.VMEM((2, 2, HALF_D, D), F32), pltpu.SemaphoreType.DMA((2, 2))],
        [vmem] * 3,
        [anywhere, anywhere, vmem],
        mib=6,
    )(mine_1, other_1, qkv_weight)
    tail = dict(
        outs=[shaped((D, 3 * D), F32), shaped((1, D), F32)],
        scratch=[pltpu.VMEM((2, HALF_D, D), F32), pltpu.SemaphoreType.DMA((2,))],
        out_specs=[anywhere, vmem],
        mib=4,
        aliases={3: 0},
    )
    grad_qkv, grad_gain = call(mine_kernel, ins=[vmem] * 3 + [anywhere], **tail)(
        mine_2, qkv_weight, grad_gain, grad_qkv
    )
    grad_qkv, grad_gain = call(other_kernel, ins=[vmem] * 3 + [anywhere, vmem], **tail)(
        other_2, qkv_weight, grad_gain, grad_qkv, gain
    )
    mixed, grad_tokens = call(finish_kernel, [shaped((6, 12, 4, D), BF16)] * 2, mib=6)(
        tok, cot, own_back, right_back, below_back, corner_back
    )
    return (
        mixed.transpose(2, 0, 1, 3),
        grad_tokens.transpose(2, 0, 1, 3),
        grad_qkv,
        grad_proj,
        grad_gain.reshape(D),
    )


def solution(mesh):
    fine = Mesh(mesh.devices.reshape(tuple(SIZES.values())), AXES)
    grid = P(None, LAT, LON, None)
    return jax.shard_map(
        on_device,
        mesh=fine,
        in_specs=(grid, grid, P(None, LAT, LON), P(), P(), P()),
        out_specs=(grid, grid, P(), P(), P()),
        check_vma=False,
    )
```

```python
import jax
import jax.numpy as jnp
from jax import lax
from jax.experimental import pallas as pl
from jax.experimental.pallas import tpu as pltpu
from jax.sharding import Mesh, PartitionSpec as P

D = 512
HALF_D = D // 2
HEADS = 8
HEAD = 64
PAIRS = HEADS // 2
WINDOWS = 2
COUNT = 144
TOKENS = WINDOWS * COUNT
HALF_R = 3
HALF_C = 6
EPS = 1e-05
SIZES = {"xl": 2, "zh": 4, "zl": 2, "c": 2, "y": 4, "xh": 2}
AXES = tuple(SIZES)
LAT = AXES[:4]
LON = AXES[4:]
NEAR = ("xh", "xl", "y", "zl")
N_NEAR = 32
FAR = "zh"
N_FAR = 4
CHUNK = 2 * D // N_NEAR
PIECE = (2, HALF_R, HALF_C, 4, D)
F32 = jnp.float32
BF16 = jnp.bfloat16


def dot(left, right):
    return jnp.dot(left, right, preferred_element_type=F32)


def dot_first(left, right):
    return lax.dot_general(left, right, (((0,), (0,)), ((), ())), preferred_element_type=F32)


def dot_last(left, right):
    return lax.dot_general(left, right, (((1,), (1,)), ((), ())), preferred_element_type=F32)


def pack_kernel(tok_ref, cot_ref, own_ref, right_ref, below_ref, corner_ref, sems):
    copies = []
    for n, ref in enumerate((tok_ref, cot_ref)):
        for rows, cols, piece in quadrants(own_ref, right_ref, below_ref, corner_ref):
            sem = sems.at[len(copies)]
            copies.append(pltpu.make_async_copy(ref.at[rows, cols], piece.at[n], sem))
    for copy in copies:
        copy.start()
    for copy in copies:
        copy.wait()


def quadrants(own, right, below, corner):
    late_r, early_r = pl.ds(HALF_R, HALF_R), pl.ds(0, HALF_R)
    late_c, early_c = pl.ds(HALF_C, HALF_C), pl.ds(0, HALF_C)
    return (
        (late_r, late_c, own),
        (late_r, early_c, right),
        (early_r, late_c, below),
        (early_r, early_c, corner),
    )


def source_of(place):
    window = place // COUNT
    rest = place - window * COUNT
    level = (1 + 2 * window + rest % 2) % 4
    return (rest // 2) * 4 + level


def attend_kernel(
    corner_ref, right_ref, below_ref, own_ref, bias_ref, gain_ref, qkv_ref, proj_ref,
    send_ref, left_ref, rows_ref, att_ref, normed_ref, inv_ref,
):
    first = lax.broadcasted_iota(jnp.int32, (TOKENS, 1), 0)
    second = lax.broadcasted_iota(jnp.int32, (TOKENS, TOKENS), 1)
    to_order = (second == source_of(first)).astype(BF16)
    pieces = (own_ref, right_ref, below_ref, corner_ref)

    def gathered(n):
        return jnp.concatenate([ref[n] for ref in pieces], axis=0).reshape(TOKENS, D)

    values = dot(to_order, gathered(0))
    cot = dot(to_order, gathered(1)).astype(BF16)
    gain = gain_ref[...]
    mean = jnp.mean(values, -1, keepdims=True)
    centred = values - mean
    inv_std = lax.rsqrt(jnp.mean(centred * centred, -1, keepdims=True) + EPS)
    normed = centred * inv_std
    hidden = (normed * gain).astype(BF16)
    projected = dot(hidden, qkv_ref[...]).astype(BF16)
    grad_att = dot_last(cot, proj_ref[...]).astype(BF16)
    normed_ref[...] = normed
    inv_ref[...] = inv_std
    left_ref[0] = hidden.T
    rows_ref[3] = cot

    lane = lax.broadcasted_iota(jnp.int32, (COUNT, 2 * HEAD), 1)
    low = lane < HEAD
    zero = jnp.zeros((COUNT, 2 * HEAD), BF16)

    def both(pair):
        return jnp.concatenate([jnp.where(low, pair, zero), jnp.where(low, zero, pair)], axis=0)

    def merged(stacked):
        return jnp.where(low, stacked[:COUNT], stacked[COUNT:]).astype(BF16)

    factor = HEAD ** (-0.5)
    for window in range(WINDOWS):
        here = slice(window * COUNT, (window + 1) * COUNT)
        bias = jnp.concatenate([bias_ref[window]] * 2, axis=0)
        for pair in range(PAIRS):
            cols = slice(pair * 2 * HEAD, (pair + 1) * 2 * HEAD)
            query = both(projected[here, cols])
            keys = projected[here, D + cols.start : D + cols.stop]
            vals = projected[here, 2 * D + cols.start : 2 * D + cols.stop]
            grad_out = both(grad_att[here, cols])
            scores = dot_last(query, keys) * factor + bias
            numer = jnp.exp(scores - jnp.max(scores, -1, keepdims=True))
            weights = numer * (1.0 / jnp.sum(numer, -1, keepdims=True))
            weights_low = weights.astype(BF16)
            att_ref[here, cols] = merged(dot(weights_low, vals))
            grad_weights = dot_last(grad_out, vals)
            inner = jnp.sum(grad_weights * weights, -1, keepdims=True)
            grad_scores = (weights * (grad_weights - inner) * factor).astype(BF16)
            rows_ref[0, here, cols] = merged(dot(grad_scores, keys))
            rows_ref[1, here, cols] = dot_first(grad_scores, query).astype(BF16)
            rows_ref[2, here, cols] = dot_first(weights_low, grad_out).astype(BF16)

    left_ref[1] = att_ref[...].T
    half_grads(1 - lax.axis_index("c"), left_ref, rows_ref, send_ref)


def half_grads(half, left_ref, rows_ref, out_ref):
    here = pl.ds(pl.multiple_of(half * HALF_D, HALF_D), HALF_D)
    for block in range(4):
        out_ref[block] = dot(left_ref[block // 3, here], rows_ref[block]).astype(BF16)


def rest_kernel(
    left_ref, rows_ref, att_ref, normed_ref, inv_ref, gain_ref, qkv_ref, proj_ref,
    keep_ref, own_out, right_out, lower_out,
):
    half_grads(lax.axis_index("c"), left_ref, rows_ref, keep_ref)
    first = lax.broadcasted_iota(jnp.int32, (TOKENS, TOKENS), 0)
    second = lax.broadcasted_iota(jnp.int32, (1, TOKENS), 1)
    from_order = (first == source_of(second)).astype(BF16)
    normed = normed_ref[...]
    inv_std = inv_ref[...]
    attended = att_ref[...]
    gain = gain_ref[...]
    branch = dot(attended, proj_ref[...]).astype(BF16)
    grad_hidden = dot_last(rows_ref[0], qkv_ref[:, :D])
    grad_hidden += dot_last(rows_ref[1], qkv_ref[:, D : 2 * D])
    grad_hidden += dot_last(rows_ref[2], qkv_ref[:, 2 * D :])
    grad_norm = grad_hidden * gain
    grad_shift = inv_std * (
        grad_norm
        - jnp.mean(grad_norm, -1, keepdims=True)
        - normed * jnp.mean(grad_norm * normed, -1, keepdims=True)
    )
    for n, result in enumerate((branch, grad_shift.astype(BF16))):
        back = dot(from_order, result).reshape(4, HALF_R, HALF_C, 4, D).astype(BF16)
        own_out[n] = back[0]
        right_out[n] = back[1]
        lower_out[0, n] = back[2]
        lower_out[1, n] = back[3]


def weights_kernel(qkv_ref, proj_ref, gain_ref, qkv_out, proj_out, gain_out, sems):
    copies = [
        pltpu.make_async_copy(ref, out, sems.at[n])
        for n, (ref, out) in enumerate(
            ((qkv_ref, qkv_out), (proj_ref, proj_out), (gain_ref, gain_out))
        )
    ]
    for copy in copies:
        copy.start()
    for copy in copies:
        copy.wait()


def add_kernel(keep_ref, got_ref, out_ref):
    out_ref[...] = (keep_ref[...].astype(F32) + got_ref[...].astype(F32)).astype(BF16)


def sum_kernel(got_ref, lower_ref, right_ref, out_ref, side_ref):
    side_ref[0] = right_ref[...]
    side_ref[1] = lower_ref[1]
    total = got_ref[0].astype(F32)
    for n in range(1, got_ref.shape[0]):
        total += got_ref[n].astype(F32)
    out_ref[...] = total.astype(BF16)


def spread_kernel(own_ref, one_ref, two_ref, three_ref, side_ref, out_ref):
    del side_ref
    even = own_ref[...].astype(F32) + two_ref[...].astype(F32)
    odd = one_ref[...].astype(F32) + three_ref[...].astype(F32)
    total = (even + odd).astype(BF16)
    for n in range(out_ref.shape[0]):
        out_ref[n] = total


def finish_kernel(tok_ref, cot_ref, own_ref, lower_ref, side_ref, mixed_ref, grad_ref):
    right_ref, below_ref, corner_ref = side_ref.at[0], lower_ref.at[0], side_ref.at[1]
    for n, (ref, out) in enumerate(((tok_ref, mixed_ref), (cot_ref, grad_ref))):
        for rows, cols, piece in quadrants(own_ref, right_ref, below_ref, corner_ref):
            out[rows, cols] = (ref[rows, cols].astype(F32) + piece[n].astype(F32)).astype(BF16)


def grads_half(half, ref, qkv_ref, gain_ref, qkv_out, proj_out, gain_out, wide, sems):
    copies = []
    here = pl.ds(pl.multiple_of(half * HALF_D, HALF_D), HALF_D)
    total = jnp.zeros((HALF_D, 128), F32)
    for block in range(4):
        part = ref[block].astype(F32)
        wide[block] = part
        cols = pl.ds(block * D, D)
        out = proj_out.at[here] if block == 3 else qkv_out.at[here, cols]
        copy = pltpu.make_async_copy(wide.at[block], out, sems.at[block])
        copy.start()
        copies.append(copy)
        if block < 3:
            product = part * qkv_ref[here, cols].astype(F32)
            for q in range(4):
                total += product[:, q * 128 : (q + 1) * 128]
    sums = jnp.sum(total.T, axis=0, keepdims=True)
    gain_out[:, here] = sums / gain_ref[:, here]
    for copy in copies:
        copy.wait()


def mine_kernel(ref, qkv_ref, gain_ref, qkv_out, proj_out, gain_out, wide, sems):
    gain_out[...] = jnp.zeros_like(gain_out)
    core = lax.axis_index("c")
    grads_half(core, ref, qkv_ref, gain_ref, qkv_out, proj_out, gain_out, wide, sems)


def other_kernel(
    ref, qkv_ref, gain_ref, qkv_in, proj_in, gain_in, qkv_out, proj_out, gain_out, wide, sems
):
    del qkv_in, proj_in
    gain_out[...] = gain_in[...]
    core = lax.axis_index("c")
    grads_half(1 - core, ref, qkv_ref, gain_ref, qkv_out, proj_out, gain_out, wide, sems)


def call(kernel, outs, scratch=(), ins=None, out_specs=None, mib=8, aliases=None):
    more = {"input_output_aliases": aliases or {}}
    if ins is not None:
        more["in_specs"] = ins
    if out_specs is not None:
        more["out_specs"] = out_specs
    return pl.pallas_call(
        kernel,
        out_shape=outs,
        scratch_shapes=list(scratch),
        compiler_params=pltpu.CompilerParams(vmem_limit_bytes=mib * 1024 * 1024),
        **more,
    )


def in_hbm(array):
    return pltpu.with_memory_space_constraint(array, pltpu.HBM)


def shaped(shape, dtype):
    return jax.ShapeDtypeStruct(shape, dtype)


def moved(block, lat_step, lon_step):
    route = [
        (lat * 8 + lon, (lat + lat_step) % 32 * 8 + (lon + lon_step) % 8)
        for lat in range(32)
        for lon in range(8)
    ]
    return lax.ppermute(block, AXES, route)


def swapped(block):
    return lax.ppermute(block, "c", [(0, 1), (1, 0)])


def on_device(tokens, cotangent, region, gain, qkv_weight, proj_weight):
    tok = tokens.transpose(1, 2, 0, 3)
    cot = cotangent.transpose(1, 2, 0, 3)
    anywhere = pl.BlockSpec(memory_space=pl.ANY)
    vmem = pl.BlockSpec(memory_space=pltpu.VMEM)
    hbm = pl.BlockSpec(memory_space=pltpu.HBM)
    own, right, below, corner = call(
        pack_kernel,
        [shaped(PIECE, BF16)] * 4,
        [pltpu.SemaphoreType.DMA((8,))],
        [hbm] * 2,
        [vmem] * 4,
        mib=2,
    )(in_hbm(tok), in_hbm(cot))
    corner = moved(corner, -1, -1)
    right = moved(right, 0, -1)
    below = moved(below, -1, 0)
    ids = region.reshape(2, 2, 2, HALF_R, 2, HALF_C).transpose(0, 2, 4, 3, 5, 1).reshape(2, COUNT)
    bias = jnp.where(ids[:, :, None] == ids[:, None, :], 0.0, -1e30).astype(F32)
    gain = gain.reshape(1, D)
    qkv_weight, proj_weight, gain = call(
        weights_kernel,
        [shaped((D, 3 * D), BF16), shaped((D, D), BF16), shaped((1, D), F32)],
        [pltpu.SemaphoreType.DMA((3,))],
        [hbm] * 3,
        [vmem] * 3,
        mib=1,
    )(in_hbm(qkv_weight), in_hbm(proj_weight), in_hbm(gain))
    send, *state = call(
        attend_kernel,
        [
            shaped((4, HALF_D, D), BF16),
            shaped((2, D, TOKENS), BF16),
            shaped((4, TOKENS, D), BF16),
            shaped((TOKENS, D), BF16),
            shaped((TOKENS, D), F32),
            shaped((TOKENS, 1), F32),
        ],
        mib=16,
    )(corner, right, below, own, bias, gain, qkv_weight, proj_weight)
    got = swapped(send)
    pair = shaped((2,) + PIECE, BF16)
    keep, own_back, right_back, lower_back = call(
        rest_kernel,
        [shaped((4, HALF_D, D), BF16), shaped(PIECE, BF16), shaped(PIECE, BF16), pair],
        mib=16,
    )(*state, gain, qkv_weight, proj_weight)
    half = call(add_kernel, shaped((4, HALF_D, D), BF16), mib=4)(keep, got)
    got = lax.all_to_all(half.reshape(N_NEAR, CHUNK, D), NEAR, 0, 0)
    lower_back = moved(lower_back, 1, 0)
    part, side_back = call(
        sum_kernel, [shaped((CHUNK, D), BF16), pair], ins=[vmem] * 3, out_specs=[vmem] * 2, mib=6
    )(got, lower_back, right_back)
    others = [
        lax.ppermute(part, FAR, [(n, (n - step) % N_FAR) for n in range(N_FAR)])
        for step in range(1, N_FAR)
    ]
    side_back = moved(side_back, 0, 1)
    parts = call(
        spread_kernel,
        shaped((N_NEAR, CHUNK, D), BF16),
        ins=[vmem] * 4 + [anywhere],
        out_specs=vmem,
        mib=4,
    )(part, *others, side_back)
    mine = lax.all_to_all(parts, NEAR, 0, 0)
    mine = mine.reshape(4, HALF_D, D)
    other = swapped(mine)
    grads = call(
        mine_kernel,
        [shaped((D, 3 * D), F32), shaped((D, D), F32), shaped((1, D), F32)],
        [pltpu.VMEM((4, HALF_D, D), F32), pltpu.SemaphoreType.DMA((4,))],
        [vmem] * 3,
        [anywhere, anywhere, vmem],
        mib=6,
    )(mine, qkv_weight, gain)
    grad_qkv, grad_proj, grad_gain = call(
        other_kernel,
        [shaped((D, 3 * D), F32), shaped((D, D), F32), shaped((1, D), F32)],
        [pltpu.VMEM((4, HALF_D, D), F32), pltpu.SemaphoreType.DMA((4,))],
        [vmem] * 3 + [anywhere] * 2 + [vmem],
        [anywhere, anywhere, vmem],
        mib=6,
        aliases={3: 0, 4: 1},
    )(other, qkv_weight, gain, *grads)
    mixed, grad_tokens = call(finish_kernel, [shaped((6, 12, 4, D), BF16)] * 2, mib=6)(
        tok, cot, own_back, lower_back, side_back
    )
    return (
        mixed.transpose(2, 0, 1, 3),
        grad_tokens.transpose(2, 0, 1, 3),
        grad_qkv,
        grad_proj,
        grad_gain.reshape(D),
    )


def solution(mesh):
    fine = Mesh(mesh.devices.reshape(tuple(SIZES.values())), AXES)
    grid = P(None, LAT, LON, None)
    return jax.shard_map(
        on_device,
        mesh=fine,
        in_specs=(grid, grid, P(None, LAT, LON), P(), P(), P()),
        out_specs=(grid, grid, P(), P(), P()),
        check_vma=False,
    )
```

```python
import jax
import jax.numpy as jnp
from jax import lax
from jax.experimental import pallas as pl
from jax.experimental.pallas import tpu as pltpu
from jax.sharding import Mesh, PartitionSpec as P

D = 512
HALF_D = D // 2
HEADS = 8
HEAD = 64
PAIRS = HEADS // 2
WINDOWS = 2
COUNT = 144
TOKENS = WINDOWS * COUNT
HALF_R = 3
HALF_C = 6
EPS = 1e-05
TOGETHER = 4
SIZES = {"xl": 2, "zh": 4, "zl": 2, "c": 2, "y": 4, "xh": 2}
AXES = tuple(SIZES)
LAT = AXES[:4]
LON = AXES[4:]
NEAR = ("xh", "xl", "y", "zl")
N_NEAR = 32
FAR = "zh"
N_FAR = 4
CHUNK = 2 * D // N_NEAR
PIECE = (2, HALF_R, HALF_C, 4, D)
F32 = jnp.float32
BF16 = jnp.bfloat16


def dot(left, right):
    return jnp.dot(left, right, preferred_element_type=F32)


def dot_first(left, right):
    return lax.dot_general(left, right, (((0,), (0,)), ((), ())), preferred_element_type=F32)


def dot_last(left, right):
    return lax.dot_general(left, right, (((1,), (1,)), ((), ())), preferred_element_type=F32)


def pack_kernel(tok_ref, cot_ref, own_ref, right_ref, below_ref, corner_ref, sems):
    copies = []
    for n, ref in enumerate((tok_ref, cot_ref)):
        for rows, cols, piece in quadrants(own_ref, right_ref, below_ref, corner_ref):
            sem = sems.at[len(copies)]
            copies.append(pltpu.make_async_copy(ref.at[rows, cols], piece.at[n], sem))
    for copy in copies:
        copy.start()
    for copy in copies:
        copy.wait()


def quadrants(own, right, below, corner):
    late_r, early_r = pl.ds(HALF_R, HALF_R), pl.ds(0, HALF_R)
    late_c, early_c = pl.ds(HALF_C, HALF_C), pl.ds(0, HALF_C)
    return (
        (late_r, late_c, own),
        (late_r, early_c, right),
        (early_r, late_c, below),
        (early_r, early_c, corner),
    )


def source_of(place):
    window = place // COUNT
    rest = place - window * COUNT
    level = (1 + 2 * window + rest % 2) % 4
    return (rest // 2) * 4 + level


def attend_kernel(
    corner_ref, right_ref, below_ref, own_ref, bias_ref, gain_ref, qkv_ref, proj_ref,
    send_ref, left_ref, rows_ref, att_ref, normed_ref, inv_ref,
):
    first = lax.broadcasted_iota(jnp.int32, (TOKENS, 1), 0)
    second = lax.broadcasted_iota(jnp.int32, (TOKENS, TOKENS), 1)
    to_order = (second == source_of(first)).astype(BF16)
    pieces = (own_ref, right_ref, below_ref, corner_ref)

    def gathered(n):
        return jnp.concatenate([ref[n] for ref in pieces], axis=0).reshape(TOKENS, D)

    values = dot(to_order, gathered(0))
    cot = dot(to_order, gathered(1)).astype(BF16)
    gain = gain_ref[...]
    mean = jnp.mean(values, -1, keepdims=True)
    centred = values - mean
    inv_std = lax.rsqrt(jnp.mean(centred * centred, -1, keepdims=True) + EPS)
    normed = centred * inv_std
    hidden = (normed * gain).astype(BF16)
    projected = dot(hidden, qkv_ref[...]).astype(BF16)
    grad_att = dot_last(cot, proj_ref[...]).astype(BF16)
    normed_ref[...] = normed
    inv_ref[...] = inv_std
    left_ref[0] = hidden.T
    rows_ref[3] = cot

    lane = lax.broadcasted_iota(jnp.int32, (COUNT, 2 * HEAD), 1)
    low = lane < HEAD
    zero = jnp.zeros((COUNT, 2 * HEAD), BF16)

    def both(pair):
        return jnp.concatenate([jnp.where(low, pair, zero), jnp.where(low, zero, pair)], axis=0)

    def merged(stacked):
        return jnp.where(low, stacked[:COUNT], stacked[COUNT:])

    factor = HEAD ** (-0.5)
    biases = [jnp.concatenate([bias_ref[w]] * 2, axis=1) for w in range(WINDOWS)]
    spots = [(w, p) for w in range(WINDOWS) for p in range(PAIRS)]
    for at in range(0, len(spots), TOGETHER):
        here, cols, bias = [], [], []
        for window, pair in spots[at : at + TOGETHER]:
            here.append(slice(window * COUNT, (window + 1) * COUNT))
            cols.append(slice(pair * 2 * HEAD, (pair + 1) * 2 * HEAD))
            bias.append(biases[window])
        each = range(len(here))
        query = [both(projected[here[i], cols[i]] * jnp.asarray(factor, BF16)) for i in each]
        keys = [projected[here[i], D + cols[i].start : D + cols[i].stop] for i in each]
        vals = [projected[here[i], 2 * D + cols[i].start : 2 * D + cols[i].stop] for i in each]
        grad_out = [both(grad_att[here[i], cols[i]]) for i in each]
        scores = [dot_last(keys[i], query[i]) + bias[i] for i in each]
        grad_weights = [dot_last(vals[i], grad_out[i]) for i in each]
        numer = [jnp.exp(s - jnp.max(s, 0, keepdims=True)) for s in scores]
        weights = [n * (1.0 / jnp.sum(n, 0, keepdims=True)) for n in numer]
        weights_low = [w.astype(BF16) for w in weights]
        inner = [jnp.sum(g * w, 0, keepdims=True) for g, w in zip(grad_weights, weights)]
        grad_scores = [
            (w * (g - i)).astype(BF16) for w, g, i in zip(weights, grad_weights, inner)
        ]
        for i in each:
            att_ref[here[i], cols[i]] = merged(dot_first(weights_low[i], vals[i])).astype(BF16)
            rows_ref[2, here[i], cols[i]] = dot(weights_low[i], grad_out[i]).astype(BF16)
        for i in each:
            grad_query = merged(dot_first(grad_scores[i], keys[i])) * factor
            rows_ref[0, here[i], cols[i]] = grad_query.astype(BF16)
            rows_ref[1, here[i], cols[i]] = dot(grad_scores[i], query[i]).astype(BF16)

    left_ref[1] = att_ref[...].T
    half_grads(1 - lax.axis_index("c"), left_ref, rows_ref, send_ref)


def half_grads(half, left_ref, rows_ref, out_ref):
    here = pl.ds(pl.multiple_of(half * HALF_D, HALF_D), HALF_D)
    for block in range(4):
        out_ref[block] = dot(left_ref[block // 3, here], rows_ref[block]).astype(BF16)


def rest_kernel(
    left_ref, rows_ref, att_ref, normed_ref, inv_ref, gain_ref, qkv_ref, proj_ref,
    keep_ref, own_out, right_out, lower_out,
):
    half_grads(lax.axis_index("c"), left_ref, rows_ref, keep_ref)
    first = lax.broadcasted_iota(jnp.int32, (TOKENS, TOKENS), 0)
    second = lax.broadcasted_iota(jnp.int32, (1, TOKENS), 1)
    from_order = (first == source_of(second)).astype(BF16)
    normed = normed_ref[...]
    inv_std = inv_ref[...]
    attended = att_ref[...]
    gain = gain_ref[...]
    branch = dot(attended, proj_ref[...]).astype(BF16)
    grad_hidden = dot_last(rows_ref[0], qkv_ref[:, :D])
    grad_hidden += dot_last(rows_ref[1], qkv_ref[:, D : 2 * D])
    grad_hidden += dot_last(rows_ref[2], qkv_ref[:, 2 * D :])
    grad_norm = grad_hidden * gain
    grad_shift = inv_std * (
        grad_norm
        - jnp.mean(grad_norm, -1, keepdims=True)
        - normed * jnp.mean(grad_norm * normed, -1, keepdims=True)
    )
    for n, result in enumerate((branch, grad_shift.astype(BF16))):
        back = dot(from_order, result).reshape(4, HALF_R, HALF_C, 4, D).astype(BF16)
        own_out[n] = back[0]
        right_out[n] = back[1]
        lower_out[0, n] = back[2]
        lower_out[1, n] = back[3]


def weights_kernel(qkv_ref, proj_ref, gain_ref, qkv_out, proj_out, gain_out, sems):
    copies = [
        pltpu.make_async_copy(ref, out, sems.at[n])
        for n, (ref, out) in enumerate(
            ((qkv_ref, qkv_out), (proj_ref, proj_out), (gain_ref, gain_out))
        )
    ]
    for copy in copies:
        copy.start()
    for copy in copies:
        copy.wait()


def add_kernel(keep_ref, got_ref, out_ref):
    out_ref[...] = (keep_ref[...].astype(F32) + got_ref[...].astype(F32)).astype(BF16)


def sum_kernel(got_ref, lower_ref, right_ref, out_ref, side_ref):
    side_ref[0] = right_ref[...]
    side_ref[1] = lower_ref[1]
    total = got_ref[0].astype(F32)
    for n in range(1, got_ref.shape[0]):
        total += got_ref[n].astype(F32)
    out_ref[...] = total.astype(BF16)


def spread_kernel(own_ref, one_ref, two_ref, three_ref, side_ref, out_ref):
    del side_ref
    even = own_ref[...].astype(F32) + two_ref[...].astype(F32)
    odd = one_ref[...].astype(F32) + three_ref[...].astype(F32)
    total = (even + odd).astype(BF16)
    for n in range(out_ref.shape[0]):
        out_ref[n] = total


def finish_kernel(tok_ref, cot_ref, own_ref, lower_ref, side_ref, mixed_ref, grad_ref):
    right_ref, below_ref, corner_ref = side_ref.at[0], lower_ref.at[0], side_ref.at[1]
    for n, (ref, out) in enumerate(((tok_ref, mixed_ref), (cot_ref, grad_ref))):
        for rows, cols, piece in quadrants(own_ref, right_ref, below_ref, corner_ref):
            out[rows, cols] = (ref[rows, cols].astype(F32) + piece[n].astype(F32)).astype(BF16)


def grads_half(half, ref, qkv_ref, gain_ref, qkv_out, proj_out, gain_out, wide, sems):
    copies = []
    here = pl.ds(pl.multiple_of(half * HALF_D, HALF_D), HALF_D)
    total = jnp.zeros((HALF_D, 128), F32)
    for block in range(4):
        part = ref[block].astype(F32)
        wide[block] = part
        cols = pl.ds(block * D, D)
        out = proj_out.at[here] if block == 3 else qkv_out.at[here, cols]
        copy = pltpu.make_async_copy(wide.at[block], out, sems.at[block])
        copy.start()
        copies.append(copy)
        if block < 3:
            product = part * qkv_ref[here, cols].astype(F32)
            for q in range(4):
                total += product[:, q * 128 : (q + 1) * 128]
    sums = jnp.sum(total.T, axis=0, keepdims=True)
    gain_out[:, here] = sums / gain_ref[:, here]
    for copy in copies:
        copy.wait()


def mine_kernel(ref, qkv_ref, gain_ref, qkv_out, proj_out, gain_out, wide, sems):
    gain_out[...] = jnp.zeros_like(gain_out)
    core = lax.axis_index("c")
    grads_half(core, ref, qkv_ref, gain_ref, qkv_out, proj_out, gain_out, wide, sems)


def other_kernel(
    ref, qkv_ref, gain_ref, qkv_in, proj_in, gain_in, qkv_out, proj_out, gain_out, wide, sems
):
    del qkv_in, proj_in
    gain_out[...] = gain_in[...]
    core = lax.axis_index("c")
    grads_half(1 - core, ref, qkv_ref, gain_ref, qkv_out, proj_out, gain_out, wide, sems)


def call(kernel, outs, scratch=(), ins=None, out_specs=None, mib=8, aliases=None):
    more = {"input_output_aliases": aliases or {}}
    if ins is not None:
        more["in_specs"] = ins
    if out_specs is not None:
        more["out_specs"] = out_specs
    return pl.pallas_call(
        kernel,
        out_shape=outs,
        scratch_shapes=list(scratch),
        compiler_params=pltpu.CompilerParams(vmem_limit_bytes=mib * 1024 * 1024),
        **more,
    )


def in_hbm(array):
    return pltpu.with_memory_space_constraint(array, pltpu.HBM)


def shaped(shape, dtype):
    return jax.ShapeDtypeStruct(shape, dtype)


def moved(block, lat_step, lon_step):
    route = [
        (lat * 8 + lon, (lat + lat_step) % 32 * 8 + (lon + lon_step) % 8)
        for lat in range(32)
        for lon in range(8)
    ]
    return lax.ppermute(block, AXES, route)


def swapped(block):
    return lax.ppermute(block, "c", [(0, 1), (1, 0)])


def on_device(tokens, cotangent, region, gain, qkv_weight, proj_weight):
    tok = tokens.transpose(1, 2, 0, 3)
    cot = cotangent.transpose(1, 2, 0, 3)
    anywhere = pl.BlockSpec(memory_space=pl.ANY)
    vmem = pl.BlockSpec(memory_space=pltpu.VMEM)
    hbm = pl.BlockSpec(memory_space=pltpu.HBM)
    own, right, below, corner = call(
        pack_kernel,
        [shaped(PIECE, BF16)] * 4,
        [pltpu.SemaphoreType.DMA((8,))],
        [hbm] * 2,
        [vmem] * 4,
        mib=2,
    )(in_hbm(tok), in_hbm(cot))
    corner = moved(corner, -1, -1)
    right = moved(right, 0, -1)
    below = moved(below, -1, 0)
    ids = region.reshape(2, 2, 2, HALF_R, 2, HALF_C).transpose(0, 2, 4, 3, 5, 1).reshape(2, COUNT)
    bias = jnp.where(ids[:, :, None] == ids[:, None, :], 0.0, -1e30).astype(F32)
    gain = gain.reshape(1, D)
    qkv_weight, proj_weight, gain = call(
        weights_kernel,
        [shaped((D, 3 * D), BF16), shaped((D, D), BF16), shaped((1, D), F32)],
        [pltpu.SemaphoreType.DMA((3,))],
        [hbm] * 3,
        [vmem] * 3,
        mib=1,
    )(in_hbm(qkv_weight), in_hbm(proj_weight), in_hbm(gain))
    send, *state = call(
        attend_kernel,
        [
            shaped((4, HALF_D, D), BF16),
            shaped((2, D, TOKENS), BF16),
            shaped((4, TOKENS, D), BF16),
            shaped((TOKENS, D), BF16),
            shaped((TOKENS, D), F32),
            shaped((TOKENS, 1), F32),
        ],
        mib=16,
    )(corner, right, below, own, bias, gain, qkv_weight, proj_weight)
    got = swapped(send)
    pair = shaped((2,) + PIECE, BF16)
    keep, own_back, right_back, lower_back = call(
        rest_kernel,
        [shaped((4, HALF_D, D), BF16), shaped(PIECE, BF16), shaped(PIECE, BF16), pair],
        mib=16,
    )(*state, gain, qkv_weight, proj_weight)
    half = call(add_kernel, shaped((4, HALF_D, D), BF16), mib=4)(keep, got)
    got = lax.all_to_all(half.reshape(N_NEAR, CHUNK, D), NEAR, 0, 0)
    lower_back = moved(lower_back, 1, 0)
    part, side_back = call(
        sum_kernel, [shaped((CHUNK, D), BF16), pair], ins=[vmem] * 3, out_specs=[vmem] * 2, mib=6
    )(got, lower_back, right_back)
    others = [
        lax.ppermute(part, FAR, [(n, (n - step) % N_FAR) for n in range(N_FAR)])
        for step in range(1, N_FAR)
    ]
    side_back = moved(side_back, 0, 1)
    parts = call(
        spread_kernel,
        shaped((N_NEAR, CHUNK, D), BF16),
        ins=[vmem] * 4 + [anywhere],
        out_specs=vmem,
        mib=4,
    )(part, *others, side_back)
    mine = lax.all_to_all(parts, NEAR, 0, 0)
    mine = mine.reshape(4, HALF_D, D)
    other = swapped(mine)
    grads = call(
        mine_kernel,
        [shaped((D, 3 * D), F32), shaped((D, D), F32), shaped((1, D), F32)],
        [pltpu.VMEM((4, HALF_D, D), F32), pltpu.SemaphoreType.DMA((4,))],
        [vmem] * 3,
        [anywhere, anywhere, vmem],
        mib=6,
    )(mine, qkv_weight, gain)
    grad_qkv, grad_proj, grad_gain = call(
        other_kernel,
        [shaped((D, 3 * D), F32), shaped((D, D), F32), shaped((1, D), F32)],
        [pltpu.VMEM((4, HALF_D, D), F32), pltpu.SemaphoreType.DMA((4,))],
        [vmem] * 3 + [anywhere] * 2 + [vmem],
        [anywhere, anywhere, vmem],
        mib=6,
        aliases={3: 0, 4: 1},
    )(other, qkv_weight, gain, *grads)
    mixed, grad_tokens = call(finish_kernel, [shaped((6, 12, 4, D), BF16)] * 2, mib=6)(
        tok, cot, own_back, lower_back, side_back
    )
    return (
        mixed.transpose(2, 0, 1, 3),
        grad_tokens.transpose(2, 0, 1, 3),
        grad_qkv,
        grad_proj,
        grad_gain.reshape(D),
    )


def solution(mesh):
    fine = Mesh(mesh.devices.reshape(tuple(SIZES.values())), AXES)
    grid = P(None, LAT, LON, None)
    return jax.shard_map(
        on_device,
        mesh=fine,
        in_specs=(grid, grid, P(None, LAT, LON), P(), P(), P()),
        out_specs=(grid, grid, P(), P(), P()),
        check_vma=False,
    )
```

```python
import jax
import jax.numpy as jnp
from jax import lax
from jax.experimental import pallas as pl
from jax.experimental.pallas import tpu as pltpu
from jax.sharding import Mesh, PartitionSpec as P

D = 512
HALF_D = D // 2
HEADS = 8
HEAD = 64
PAIRS = HEADS // 2
WINDOWS = 2
COUNT = 144
TOKENS = WINDOWS * COUNT
HALF_R = 3
HALF_C = 6
EPS = 1e-05
TOGETHER = 8
SIZES = {"xl": 2, "zh": 4, "zl": 2, "c": 2, "y": 4, "xh": 2}
AXES = tuple(SIZES)
LAT = AXES[:4]
LON = AXES[4:]
NEAR = ("xh", "xl", "y", "zl")
N_NEAR = 32
FAR = "zh"
N_FAR = 4
CHUNK = 2 * D // N_NEAR
PIECE = (2, HALF_R, HALF_C, 4, D)
F32 = jnp.float32
BF16 = jnp.bfloat16


def dot(left, right):
    return jnp.dot(left, right, preferred_element_type=F32)


def dot_first(left, right):
    return lax.dot_general(left, right, (((0,), (0,)), ((), ())), preferred_element_type=F32)


def dot_last(left, right):
    return lax.dot_general(left, right, (((1,), (1,)), ((), ())), preferred_element_type=F32)


def pack_kernel(tok_ref, cot_ref, own_ref, right_ref, below_ref, corner_ref, sems):
    copies = []
    for n, ref in enumerate((tok_ref, cot_ref)):
        for rows, cols, piece in quadrants(own_ref, right_ref, below_ref, corner_ref):
            sem = sems.at[len(copies)]
            copies.append(pltpu.make_async_copy(ref.at[rows, cols], piece.at[n], sem))
    for copy in copies:
        copy.start()
    for copy in copies:
        copy.wait()


def quadrants(own, right, below, corner):
    late_r, early_r = pl.ds(HALF_R, HALF_R), pl.ds(0, HALF_R)
    late_c, early_c = pl.ds(HALF_C, HALF_C), pl.ds(0, HALF_C)
    return (
        (late_r, late_c, own),
        (late_r, early_c, right),
        (early_r, late_c, below),
        (early_r, early_c, corner),
    )


def source_of(place):
    window = place // COUNT
    rest = place - window * COUNT
    level = (1 + 2 * window + rest % 2) % 4
    return (rest // 2) * 4 + level


def attend_kernel(
    corner_ref, right_ref, below_ref, own_ref, bias_ref, gain_ref, qkv_ref, proj_ref,
    send_ref, left_ref, rows_ref, att_ref, normed_ref, inv_ref,
):
    first = lax.broadcasted_iota(jnp.int32, (TOKENS, 1), 0)
    second = lax.broadcasted_iota(jnp.int32, (TOKENS, TOKENS), 1)
    to_order = (second == source_of(first)).astype(BF16)
    pieces = (own_ref, right_ref, below_ref, corner_ref)

    def gathered(n):
        return jnp.concatenate([ref[n] for ref in pieces], axis=0).reshape(TOKENS, D)

    values = dot(to_order, gathered(0))
    cot = dot(to_order, gathered(1)).astype(BF16)
    gain = gain_ref[...]
    mean = jnp.mean(values, -1, keepdims=True)
    centred = values - mean
    inv_std = lax.rsqrt(jnp.mean(centred * centred, -1, keepdims=True) + EPS)
    normed = centred * inv_std
    hidden = (normed * gain).astype(BF16)
    projected = dot(hidden, qkv_ref[...]).astype(BF16)
    grad_att = dot_last(cot, proj_ref[...]).astype(BF16)
    normed_ref[...] = normed
    inv_ref[...] = inv_std
    left_ref[0] = hidden.T
    rows_ref[3] = cot

    lane = lax.broadcasted_iota(jnp.int32, (COUNT, 2 * HEAD), 1)
    low = lane < HEAD
    zero = jnp.zeros((COUNT, 2 * HEAD), BF16)

    def both(pair):
        return jnp.concatenate([jnp.where(low, pair, zero), jnp.where(low, zero, pair)], axis=0)

    def merged(stacked):
        return jnp.where(low, stacked[:COUNT], stacked[COUNT:])

    factor = HEAD ** (-0.5)
    biases = [jnp.concatenate([bias_ref[w]] * 2, axis=1) for w in range(WINDOWS)]
    spots = [(w, p) for w in range(WINDOWS) for p in range(PAIRS)]
    for at in range(0, len(spots), TOGETHER):
        here, cols, bias = [], [], []
        for window, pair in spots[at : at + TOGETHER]:
            here.append(slice(window * COUNT, (window + 1) * COUNT))
            cols.append(slice(pair * 2 * HEAD, (pair + 1) * 2 * HEAD))
            bias.append(biases[window])
        each = range(len(here))
        query = [both(projected[here[i], cols[i]] * jnp.asarray(factor, BF16)) for i in each]
        keys = [projected[here[i], D + cols[i].start : D + cols[i].stop] for i in each]
        vals = [projected[here[i], 2 * D + cols[i].start : 2 * D + cols[i].stop] for i in each]
        grad_out = [both(grad_att[here[i], cols[i]]) for i in each]
        scores = [dot_last(keys[i], query[i]) + bias[i] for i in each]
        grad_weights = [dot_last(vals[i], grad_out[i]) for i in each]
        numer = [jnp.exp(s - jnp.max(s, 0, keepdims=True)) for s in scores]
        weights = [n * (1.0 / jnp.sum(n, 0, keepdims=True)) for n in numer]
        weights_low = [w.astype(BF16) for w in weights]
        inner = [jnp.sum(g * w, 0, keepdims=True) for g, w in zip(grad_weights, weights)]
        grad_scores = [
            (w * (g - i)).astype(BF16) for w, g, i in zip(weights, grad_weights, inner)
        ]
        for i in each:
            att_ref[here[i], cols[i]] = merged(dot_first(weights_low[i], vals[i])).astype(BF16)
            rows_ref[2, here[i], cols[i]] = dot(weights_low[i], grad_out[i]).astype(BF16)
        for i in each:
            grad_query = merged(dot_first(grad_scores[i], keys[i])) * factor
            rows_ref[0, here[i], cols[i]] = grad_query.astype(BF16)
            rows_ref[1, here[i], cols[i]] = dot(grad_scores[i], query[i]).astype(BF16)

    left_ref[1] = att_ref[...].T
    half_grads(1 - lax.axis_index("c"), left_ref, rows_ref, send_ref)


def half_grads(half, left_ref, rows_ref, out_ref):
    here = pl.ds(pl.multiple_of(half * HALF_D, HALF_D), HALF_D)
    for block in range(4):
        out_ref[block] = dot(left_ref[block // 3, here], rows_ref[block]).astype(BF16)


def rest_kernel(
    left_ref, rows_ref, att_ref, normed_ref, inv_ref, gain_ref, qkv_ref, proj_ref,
    keep_ref, own_out, right_out, lower_out,
):
    half_grads(lax.axis_index("c"), left_ref, rows_ref, keep_ref)
    first = lax.broadcasted_iota(jnp.int32, (TOKENS, TOKENS), 0)
    second = lax.broadcasted_iota(jnp.int32, (1, TOKENS), 1)
    from_order = (first == source_of(second)).astype(BF16)
    normed = normed_ref[...]
    inv_std = inv_ref[...]
    attended = att_ref[...]
    gain = gain_ref[...]
    branch = dot(attended, proj_ref[...]).astype(BF16)
    grad_hidden = dot_last(rows_ref[0], qkv_ref[:, :D])
    grad_hidden += dot_last(rows_ref[1], qkv_ref[:, D : 2 * D])
    grad_hidden += dot_last(rows_ref[2], qkv_ref[:, 2 * D :])
    grad_norm = grad_hidden * gain
    grad_shift = inv_std * (
        grad_norm
        - jnp.mean(grad_norm, -1, keepdims=True)
        - normed * jnp.mean(grad_norm * normed, -1, keepdims=True)
    )
    for n, result in enumerate((branch, grad_shift.astype(BF16))):
        back = dot(from_order, result).reshape(4, HALF_R, HALF_C, 4, D).astype(BF16)
        own_out[n] = back[0]
        right_out[n] = back[1]
        lower_out[0, n] = back[2]
        lower_out[1, n] = back[3]


def weights_kernel(qkv_ref, proj_ref, gain_ref, qkv_out, proj_out, gain_out, sems):
    copies = [
        pltpu.make_async_copy(ref, out, sems.at[n])
        for n, (ref, out) in enumerate(
            ((qkv_ref, qkv_out), (proj_ref, proj_out), (gain_ref, gain_out))
        )
    ]
    for copy in copies:
        copy.start()
    for copy in copies:
        copy.wait()


def add_kernel(keep_ref, got_ref, out_ref, held, sems):
    copies = []
    for block in range(4):
        held[block] = (keep_ref[block].astype(F32) + got_ref[block].astype(F32)).astype(BF16)
        copy = pltpu.make_async_copy(held.at[block], out_ref.at[block], sems.at[block])
        copy.start()
        copies.append(copy)
    for copy in copies:
        copy.wait()


def sum_kernel(got_ref, lower_ref, right_ref, out_ref, side_ref):
    side_ref[0] = right_ref[...]
    side_ref[1] = lower_ref[1]
    total = got_ref[0].astype(F32)
    for n in range(1, got_ref.shape[0]):
        total += got_ref[n].astype(F32)
    out_ref[...] = total.astype(BF16)


def spread_kernel(own_ref, one_ref, two_ref, three_ref, side_ref, out_ref):
    del side_ref
    even = own_ref[...].astype(F32) + two_ref[...].astype(F32)
    odd = one_ref[...].astype(F32) + three_ref[...].astype(F32)
    total = (even + odd).astype(BF16)
    for n in range(out_ref.shape[0]):
        out_ref[n] = total


def finish_kernel(tok_ref, cot_ref, own_ref, lower_ref, side_ref, mixed_ref, grad_ref):
    right_ref, below_ref, corner_ref = side_ref.at[0], lower_ref.at[0], side_ref.at[1]
    for n, (ref, out) in enumerate(((tok_ref, mixed_ref), (cot_ref, grad_ref))):
        for rows, cols, piece in quadrants(own_ref, right_ref, below_ref, corner_ref):
            out[rows, cols] = (ref[rows, cols].astype(F32) + piece[n].astype(F32)).astype(BF16)


def grads_half(half, ref, qkv_ref, gain_ref, qkv_out, proj_out, gain_out, wide, sems):
    copies = []
    here = pl.ds(pl.multiple_of(half * HALF_D, HALF_D), HALF_D)
    total = jnp.zeros((HALF_D, 128), F32)
    for block in range(4):
        part = ref[block].astype(F32)
        wide[block] = part
        cols = pl.ds(block * D, D)
        out = proj_out.at[here] if block == 3 else qkv_out.at[here, cols]
        copy = pltpu.make_async_copy(wide.at[block], out, sems.at[block])
        copy.start()
        copies.append(copy)
        if block < 3:
            product = part * qkv_ref[here, cols].astype(F32)
            for q in range(4):
                total += product[:, q * 128 : (q + 1) * 128]
    sums = jnp.sum(total.T, axis=0, keepdims=True)
    gain_out[:, here] = sums / gain_ref[:, here]
    return copies


def mine_kernel(ref, qkv_ref, gain_ref, qkv_out, proj_out, gain_out, wide, sems):
    gain_out[...] = jnp.zeros_like(gain_out)
    core = lax.axis_index("c")
    copies = grads_half(core, ref, qkv_ref, gain_ref, qkv_out, proj_out, gain_out, wide, sems)
    for copy in copies:
        copy.wait()


def other_kernel(
    ref, qkv_ref, gain_ref, qkv_in, proj_in, gain_in, qkv_out, proj_out, gain_out, wide, sems,
    held, gain_sem,
):
    del qkv_in, proj_in
    held[...] = gain_in[...]
    half = 1 - lax.axis_index("c")
    copies = grads_half(half, ref, qkv_ref, gain_ref, qkv_out, proj_out, held, wide, sems)
    copies.append(pltpu.make_async_copy(held, gain_out, gain_sem))
    copies[-1].start()
    for copy in copies:
        copy.wait()


def call(kernel, outs, scratch=(), ins=None, out_specs=None, mib=8, aliases=None):
    more = {"input_output_aliases": aliases or {}}
    if ins is not None:
        more["in_specs"] = ins
    if out_specs is not None:
        more["out_specs"] = out_specs
    return pl.pallas_call(
        kernel,
        out_shape=outs,
        scratch_shapes=list(scratch),
        compiler_params=pltpu.CompilerParams(vmem_limit_bytes=mib * 1024 * 1024),
        **more,
    )


def in_hbm(array):
    return pltpu.with_memory_space_constraint(array, pltpu.HBM)


def shaped(shape, dtype):
    return jax.ShapeDtypeStruct(shape, dtype)


def moved(block, lat_step, lon_step):
    route = [
        (lat * 8 + lon, (lat + lat_step) % 32 * 8 + (lon + lon_step) % 8)
        for lat in range(32)
        for lon in range(8)
    ]
    return lax.ppermute(block, AXES, route)


def swapped(block):
    return lax.ppermute(block, "c", [(0, 1), (1, 0)])


def on_device(tokens, cotangent, region, gain, qkv_weight, proj_weight):
    tok = tokens.transpose(1, 2, 0, 3)
    cot = cotangent.transpose(1, 2, 0, 3)
    anywhere = pl.BlockSpec(memory_space=pl.ANY)
    vmem = pl.BlockSpec(memory_space=pltpu.VMEM)
    hbm = pl.BlockSpec(memory_space=pltpu.HBM)
    own, right, below, corner = call(
        pack_kernel,
        [shaped(PIECE, BF16)] * 4,
        [pltpu.SemaphoreType.DMA((8,))],
        [hbm] * 2,
        [vmem] * 4,
        mib=2,
    )(in_hbm(tok), in_hbm(cot))
    corner = moved(corner, -1, -1)
    right = moved(right, 0, -1)
    below = moved(below, -1, 0)
    ids = region.reshape(2, 2, 2, HALF_R, 2, HALF_C).transpose(0, 2, 4, 3, 5, 1).reshape(2, COUNT)
    bias = jnp.where(ids[:, :, None] == ids[:, None, :], 0.0, -1e30).astype(F32)
    gain = gain.reshape(1, D)
    qkv_weight, proj_weight, gain = call(
        weights_kernel,
        [shaped((D, 3 * D), BF16), shaped((D, D), BF16), shaped((1, D), F32)],
        [pltpu.SemaphoreType.DMA((3,))],
        [hbm] * 3,
        [vmem] * 3,
        mib=1,
    )(in_hbm(qkv_weight), in_hbm(proj_weight), in_hbm(gain))
    send, *state = call(
        attend_kernel,
        [
            shaped((4, HALF_D, D), BF16),
            shaped((2, D, TOKENS), BF16),
            shaped((4, TOKENS, D), BF16),
            shaped((TOKENS, D), BF16),
            shaped((TOKENS, D), F32),
            shaped((TOKENS, 1), F32),
        ],
        mib=16,
    )(corner, right, below, own, bias, gain, qkv_weight, proj_weight)
    got = swapped(send)
    pair = shaped((2,) + PIECE, BF16)
    keep, own_back, right_back, lower_back = call(
        rest_kernel,
        [shaped((4, HALF_D, D), BF16), shaped(PIECE, BF16), shaped(PIECE, BF16), pair],
        mib=16,
    )(*state, gain, qkv_weight, proj_weight)
    half = call(
        add_kernel,
        shaped((4, HALF_D, D), BF16),
        [pltpu.VMEM((4, HALF_D, D), BF16), pltpu.SemaphoreType.DMA((4,))],
        [vmem] * 2,
        anywhere,
        mib=4,
    )(keep, got)
    got = lax.all_to_all(half.reshape(N_NEAR, CHUNK, D), NEAR, 0, 0)
    lower_back = moved(lower_back, 1, 0)
    part, side_back = call(
        sum_kernel, [shaped((CHUNK, D), BF16), pair], ins=[vmem] * 3, out_specs=[vmem] * 2, mib=6
    )(got, lower_back, right_back)
    others = [
        lax.ppermute(part, FAR, [(n, (n - step) % N_FAR) for n in range(N_FAR)])
        for step in range(1, N_FAR)
    ]
    side_back = moved(side_back, 0, 1)
    parts = call(
        spread_kernel,
        shaped((N_NEAR, CHUNK, D), BF16),
        ins=[vmem] * 4 + [anywhere],
        out_specs=vmem,
        mib=4,
    )(part, *others, side_back)
    mine = lax.all_to_all(parts, NEAR, 0, 0)
    mine = mine.reshape(4, HALF_D, D)
    other = swapped(mine)
    grads = call(
        mine_kernel,
        [shaped((D, 3 * D), F32), shaped((D, D), F32), shaped((1, D), F32)],
        [pltpu.VMEM((4, HALF_D, D), F32), pltpu.SemaphoreType.DMA((4,))],
        [vmem] * 3,
        [anywhere, anywhere, vmem],
        mib=6,
    )(mine, qkv_weight, gain)
    grad_qkv, grad_proj, grad_gain = call(
        other_kernel,
        [shaped((D, 3 * D), F32), shaped((D, D), F32), shaped((1, D), F32)],
        [
            pltpu.VMEM((4, HALF_D, D), F32),
            pltpu.SemaphoreType.DMA((4,)),
            pltpu.VMEM((1, D), F32),
            pltpu.SemaphoreType.DMA,
        ],
        [vmem] * 3 + [anywhere] * 2 + [vmem],
        [anywhere] * 3,
        mib=6,
        aliases={3: 0, 4: 1},
    )(other, qkv_weight, gain, *grads)
    mixed, grad_tokens = call(finish_kernel, [shaped((6, 12, 4, D), BF16)] * 2, mib=6)(
        tok, cot, own_back, lower_back, side_back
    )
    return (
        mixed.transpose(2, 0, 1, 3),
        grad_tokens.transpose(2, 0, 1, 3),
        grad_qkv,
        grad_proj,
        grad_gain.reshape(D),
    )


def solution(mesh):
    fine = Mesh(mesh.devices.reshape(tuple(SIZES.values())), AXES)
    grid = P(None, LAT, LON, None)
    return jax.shard_map(
        on_device,
        mesh=fine,
        in_specs=(grid, grid, P(None, LAT, LON), P(), P(), P()),
        out_specs=(grid, grid, P(), P(), P()),
        check_vma=False,
    )
```

```python
import jax
import jax.numpy as jnp
from jax import lax
from jax.experimental import pallas as pl
from jax.experimental.pallas import tpu as pltpu
from jax.sharding import Mesh, PartitionSpec as P

D = 512
HALF_D = D // 2
HEADS = 8
HEAD = 64
PAIRS = HEADS // 2
WINDOWS = 2
COUNT = 144
TOKENS = WINDOWS * COUNT
HALF_R = 3
HALF_C = 6
EPS = 1e-05
TOGETHER = 8
SIZES = {"xl": 2, "zh": 4, "zl": 2, "c": 2, "y": 4, "xh": 2}
AXES = tuple(SIZES)
LAT = AXES[:4]
LON = AXES[4:]
NEAR = ("xh", "xl", "y", "zl")
N_NEAR = 32
FAR = "zh"
N_FAR = 4
CHUNK = 2 * D // N_NEAR
PIECE = (2, HALF_R, HALF_C, 4, D)
F32 = jnp.float32
BF16 = jnp.bfloat16


def dot(left, right):
    return jnp.dot(left, right, preferred_element_type=F32)


def dot_first(left, right):
    return lax.dot_general(left, right, (((0,), (0,)), ((), ())), preferred_element_type=F32)


def dot_last(left, right):
    return lax.dot_general(left, right, (((1,), (1,)), ((), ())), preferred_element_type=F32)


def pack_kernel(tok_ref, cot_ref, own_ref, right_ref, below_ref, corner_ref, sems):
    copies = []
    for n, ref in enumerate((tok_ref, cot_ref)):
        for rows, cols, piece in quadrants(own_ref, right_ref, below_ref, corner_ref):
            sem = sems.at[len(copies)]
            copies.append(pltpu.make_async_copy(ref.at[rows, cols], piece.at[n], sem))
    for copy in copies:
        copy.start()
    for copy in copies:
        copy.wait()


def quadrants(own, right, below, corner):
    late_r, early_r = pl.ds(HALF_R, HALF_R), pl.ds(0, HALF_R)
    late_c, early_c = pl.ds(HALF_C, HALF_C), pl.ds(0, HALF_C)
    return (
        (late_r, late_c, own),
        (late_r, early_c, right),
        (early_r, late_c, below),
        (early_r, early_c, corner),
    )


def source_of(place):
    window = place // COUNT
    rest = place - window * COUNT
    level = (1 + 2 * window + rest % 2) % 4
    return (rest // 2) * 4 + level


def attend_kernel(
    corner_ref, right_ref, below_ref, own_ref, bias_ref, gain_ref, qkv_ref, proj_ref,
    send_ref, left_ref, rows_ref, att_ref, normed_ref, inv_ref,
):
    first = lax.broadcasted_iota(jnp.int32, (TOKENS, 1), 0)
    second = lax.broadcasted_iota(jnp.int32, (TOKENS, TOKENS), 1)
    to_order = (second == source_of(first)).astype(BF16)
    pieces = (own_ref, right_ref, below_ref, corner_ref)

    def gathered(n):
        return jnp.concatenate([ref[n] for ref in pieces], axis=0).reshape(TOKENS, D)

    values = dot(to_order, gathered(0))
    cot = dot(to_order, gathered(1)).astype(BF16)
    gain = gain_ref[...]
    mean = jnp.mean(values, -1, keepdims=True)
    centred = values - mean
    inv_std = lax.rsqrt(jnp.mean(centred * centred, -1, keepdims=True) + EPS)
    normed = centred * inv_std
    hidden = (normed * gain).astype(BF16)
    projected = dot(hidden, qkv_ref[...]).astype(BF16)
    grad_att = dot_last(cot, proj_ref[...]).astype(BF16)
    normed_ref[...] = normed
    inv_ref[...] = inv_std
    left_ref[0] = hidden.T
    rows_ref[3] = cot

    lane = lax.broadcasted_iota(jnp.int32, (COUNT, 2 * HEAD), 1)
    low = lane < HEAD
    zero = jnp.zeros((COUNT, 2 * HEAD), BF16)

    def both(pair):
        return jnp.concatenate([jnp.where(low, pair, zero), jnp.where(low, zero, pair)], axis=0)

    def merged(stacked):
        return jnp.where(low, stacked[:COUNT], stacked[COUNT:])

    factor = HEAD ** (-0.5)
    biases = [jnp.concatenate([bias_ref[w]] * 2, axis=1) for w in range(WINDOWS)]
    spots = [(w, p) for w in range(WINDOWS) for p in range(PAIRS)]
    for at in range(0, len(spots), TOGETHER):
        here, cols, bias = [], [], []
        for window, pair in spots[at : at + TOGETHER]:
            here.append(slice(window * COUNT, (window + 1) * COUNT))
            cols.append(slice(pair * 2 * HEAD, (pair + 1) * 2 * HEAD))
            bias.append(biases[window])
        each = range(len(here))
        query = [both(projected[here[i], cols[i]] * jnp.asarray(factor, BF16)) for i in each]
        keys = [projected[here[i], D + cols[i].start : D + cols[i].stop] for i in each]
        vals = [projected[here[i], 2 * D + cols[i].start : 2 * D + cols[i].stop] for i in each]
        grad_out = [both(grad_att[here[i], cols[i]]) for i in each]
        scores = [dot_last(keys[i], query[i]) + bias[i] for i in each]
        grad_weights = [dot_last(vals[i], grad_out[i]) for i in each]
        numer = [jnp.exp(s - jnp.max(s, 0, keepdims=True)) for s in scores]
        weights = [n * (1.0 / jnp.sum(n, 0, keepdims=True)) for n in numer]
        weights_low = [w.astype(BF16) for w in weights]
        inner = [jnp.sum(g * w, 0, keepdims=True) for g, w in zip(grad_weights, weights)]
        grad_scores = [
            (w * (g - i)).astype(BF16) for w, g, i in zip(weights, grad_weights, inner)
        ]
        for i in each:
            att_ref[here[i], cols[i]] = merged(dot_first(weights_low[i], vals[i])).astype(BF16)
            rows_ref[2, here[i], cols[i]] = dot(weights_low[i], grad_out[i]).astype(BF16)
        for i in each:
            grad_query = merged(dot_first(grad_scores[i], keys[i])) * factor
            rows_ref[0, here[i], cols[i]] = grad_query.astype(BF16)
            rows_ref[1, here[i], cols[i]] = dot(grad_scores[i], query[i]).astype(BF16)

    left_ref[1] = att_ref[...].T
    half_grads(1 - lax.axis_index("c"), left_ref, rows_ref, send_ref)


def half_grads(half, left_ref, rows_ref, out_ref):
    here = pl.ds(pl.multiple_of(half * HALF_D, HALF_D), HALF_D)
    for block in range(4):
        out_ref[block] = dot(left_ref[block // 3, here], rows_ref[block]).astype(BF16)


def rest_kernel(
    left_ref, rows_ref, att_ref, normed_ref, inv_ref, gain_ref, qkv_ref, proj_ref,
    keep_ref, own_out, right_out, lower_out,
):
    half_grads(lax.axis_index("c"), left_ref, rows_ref, keep_ref)
    first = lax.broadcasted_iota(jnp.int32, (TOKENS, TOKENS), 0)
    second = lax.broadcasted_iota(jnp.int32, (1, TOKENS), 1)
    from_order = (first == source_of(second)).astype(BF16)
    normed = normed_ref[...]
    inv_std = inv_ref[...]
    attended = att_ref[...]
    gain = gain_ref[...]
    branch = dot(attended, proj_ref[...]).astype(BF16)
    grad_hidden = dot_last(rows_ref[0], qkv_ref[:, :D])
    grad_hidden += dot_last(rows_ref[1], qkv_ref[:, D : 2 * D])
    grad_hidden += dot_last(rows_ref[2], qkv_ref[:, 2 * D :])
    grad_norm = grad_hidden * gain
    grad_shift = inv_std * (
        grad_norm
        - jnp.mean(grad_norm, -1, keepdims=True)
        - normed * jnp.mean(grad_norm * normed, -1, keepdims=True)
    )
    for n, result in enumerate((branch, grad_shift.astype(BF16))):
        back = dot(from_order, result).reshape(4, HALF_R, HALF_C, 4, D).astype(BF16)
        own_out[n] = back[0]
        right_out[n] = back[1]
        lower_out[0, n] = back[2]
        lower_out[1, n] = back[3]


def weights_kernel(qkv_ref, proj_ref, gain_ref, qkv_out, proj_out, gain_out, sems):
    copies = [
        pltpu.make_async_copy(ref, out, sems.at[n])
        for n, (ref, out) in enumerate(
            ((qkv_ref, qkv_out), (proj_ref, proj_out), (gain_ref, gain_out))
        )
    ]
    for copy in copies:
        copy.start()
    for copy in copies:
        copy.wait()


def side_kernel(lower_ref, right_ref, side_ref):
    side_ref[0] = right_ref[...]
    side_ref[1] = lower_ref[1]


def add_kernel(keep_ref, got_ref, side_ref, out_ref, held, sems):
    del side_ref
    copies = []
    for block in range(4):
        held[block] = (keep_ref[block].astype(F32) + got_ref[block].astype(F32)).astype(BF16)
        copy = pltpu.make_async_copy(held.at[block], out_ref.at[block], sems.at[block])
        copy.start()
        copies.append(copy)
    for copy in copies:
        copy.wait()


def sum_kernel(got_ref, lower_ref, right_ref, out_ref, side_ref):
    side_ref[0] = right_ref[...]
    side_ref[1] = lower_ref[1]
    total = got_ref[0].astype(F32)
    for n in range(1, got_ref.shape[0]):
        total += got_ref[n].astype(F32)
    out_ref[...] = total.astype(BF16)


def spread_kernel(own_ref, one_ref, two_ref, three_ref, side_ref, out_ref):
    del side_ref
    even = own_ref[...].astype(F32) + two_ref[...].astype(F32)
    odd = one_ref[...].astype(F32) + three_ref[...].astype(F32)
    total = (even + odd).astype(BF16)
    for n in range(out_ref.shape[0]):
        out_ref[n] = total


def finish_kernel(
    tok_ref, cot_ref, own_ref, lower_0, side_0, lower_1, side_1, mixed_ref, grad_ref
):
    def put(lower_ref, side_ref):
        right_ref, below_ref, corner_ref = side_ref.at[0], lower_ref.at[0], side_ref.at[1]
        for n, (ref, out) in enumerate(((tok_ref, mixed_ref), (cot_ref, grad_ref))):
            for rows, cols, piece in quadrants(own_ref, right_ref, below_ref, corner_ref):
                total = ref[rows, cols].astype(F32) + piece[n].astype(F32)
                out[rows, cols] = total.astype(BF16)

    for core, pieces in enumerate(((lower_0, side_0), (lower_1, side_1))):

        @pl.when(lax.axis_index("c") == core)
        def _():
            put(*pieces)


def grads_half(half, ref, qkv_ref, gain_ref, qkv_out, proj_out, gain_out, wide, sems):
    copies = []
    here = pl.ds(pl.multiple_of(half * HALF_D, HALF_D), HALF_D)
    total = jnp.zeros((HALF_D, 128), F32)
    for block in range(4):
        part = ref[block].astype(F32)
        wide[block] = part
        cols = pl.ds(block * D, D)
        out = proj_out.at[here] if block == 3 else qkv_out.at[here, cols]
        copy = pltpu.make_async_copy(wide.at[block], out, sems.at[block])
        copy.start()
        copies.append(copy)
        if block < 3:
            product = part * qkv_ref[here, cols].astype(F32)
            for q in range(4):
                total += product[:, q * 128 : (q + 1) * 128]
    sums = jnp.sum(total.T, axis=0, keepdims=True)
    gain_out[:, here] = sums / gain_ref[:, here]
    return copies


def mine_kernel(ref, qkv_ref, gain_ref, qkv_out, proj_out, gain_out, wide, sems):
    gain_out[...] = jnp.zeros_like(gain_out)
    core = lax.axis_index("c")
    copies = grads_half(core, ref, qkv_ref, gain_ref, qkv_out, proj_out, gain_out, wide, sems)
    for copy in copies:
        copy.wait()


def other_kernel(
    ref, qkv_ref, gain_ref, qkv_in, proj_in, gain_in, qkv_out, proj_out, gain_out, wide, sems,
    held, gain_sem,
):
    del qkv_in, proj_in
    held[...] = gain_in[...]
    half = 1 - lax.axis_index("c")
    copies = grads_half(half, ref, qkv_ref, gain_ref, qkv_out, proj_out, held, wide, sems)
    copies.append(pltpu.make_async_copy(held, gain_out, gain_sem))
    copies[-1].start()
    for copy in copies:
        copy.wait()


def call(kernel, outs, scratch=(), ins=None, out_specs=None, mib=8, aliases=None):
    more = {"input_output_aliases": aliases or {}}
    if ins is not None:
        more["in_specs"] = ins
    if out_specs is not None:
        more["out_specs"] = out_specs
    return pl.pallas_call(
        kernel,
        out_shape=outs,
        scratch_shapes=list(scratch),
        compiler_params=pltpu.CompilerParams(vmem_limit_bytes=mib * 1024 * 1024),
        **more,
    )


def in_hbm(array):
    return pltpu.with_memory_space_constraint(array, pltpu.HBM)


def shaped(shape, dtype):
    return jax.ShapeDtypeStruct(shape, dtype)


def moved(block, lat_step, lon_step, cores=(0, 1)):
    route = [
        (lat * 8 + lon, (lat + lat_step) % 32 * 8 + (lon + lon_step) % 8)
        for lat in range(32)
        if lat % 2 in cores
        for lon in range(8)
    ]
    return lax.ppermute(block, AXES, route)


def swapped(block):
    return lax.ppermute(block, "c", [(0, 1), (1, 0)])


def on_device(tokens, cotangent, region, gain, qkv_weight, proj_weight):
    tok = tokens.transpose(1, 2, 0, 3)
    cot = cotangent.transpose(1, 2, 0, 3)
    anywhere = pl.BlockSpec(memory_space=pl.ANY)
    vmem = pl.BlockSpec(memory_space=pltpu.VMEM)
    hbm = pl.BlockSpec(memory_space=pltpu.HBM)
    own, right, below, corner = call(
        pack_kernel,
        [shaped(PIECE, BF16)] * 4,
        [pltpu.SemaphoreType.DMA((8,))],
        [hbm] * 2,
        [vmem] * 4,
        mib=2,
    )(in_hbm(tok), in_hbm(cot))
    corner = moved(corner, -1, -1)
    right = moved(right, 0, -1)
    below = moved(below, -1, 0)
    ids = region.reshape(2, 2, 2, HALF_R, 2, HALF_C).transpose(0, 2, 4, 3, 5, 1).reshape(2, COUNT)
    bias = jnp.where(ids[:, :, None] == ids[:, None, :], 0.0, -1e30).astype(F32)
    gain = gain.reshape(1, D)
    qkv_weight, proj_weight, gain = call(
        weights_kernel,
        [shaped((D, 3 * D), BF16), shaped((D, D), BF16), shaped((1, D), F32)],
        [pltpu.SemaphoreType.DMA((3,))],
        [hbm] * 3,
        [vmem] * 3,
        mib=1,
    )(in_hbm(qkv_weight), in_hbm(proj_weight), in_hbm(gain))
    send, *state = call(
        attend_kernel,
        [
            shaped((4, HALF_D, D), BF16),
            shaped((2, D, TOKENS), BF16),
            shaped((4, TOKENS, D), BF16),
            shaped((TOKENS, D), BF16),
            shaped((TOKENS, D), F32),
            shaped((TOKENS, 1), F32),
        ],
        mib=16,
    )(corner, right, below, own, bias, gain, qkv_weight, proj_weight)
    got = swapped(send)
    pair = shaped((2,) + PIECE, BF16)
    keep, own_back, right_back, lower_back = call(
        rest_kernel,
        [shaped((4, HALF_D, D), BF16), shaped(PIECE, BF16), shaped(PIECE, BF16), pair],
        mib=16,
    )(*state, gain, qkv_weight, proj_weight)
    lower_1 = moved(lower_back, 1, 0, cores=[0])
    lower_0 = moved(lower_back, 1, 0, cores=[1])
    side_1 = moved(call(side_kernel, pair, mib=4)(lower_1, right_back), 0, 1, cores=[1])
    half = call(
        add_kernel,
        shaped((4, HALF_D, D), BF16),
        [pltpu.VMEM((4, HALF_D, D), BF16), pltpu.SemaphoreType.DMA((4,))],
        [vmem] * 2 + [anywhere],
        anywhere,
        mib=4,
    )(keep, got, side_1)
    got = lax.all_to_all(half.reshape(N_NEAR, CHUNK, D), NEAR, 0, 0)
    part, side_back = call(
        sum_kernel, [shaped((CHUNK, D), BF16), pair], ins=[vmem] * 3, out_specs=[vmem] * 2, mib=6
    )(got, lower_0, right_back)
    others = [
        lax.ppermute(part, FAR, [(n, (n - step) % N_FAR) for n in range(N_FAR)])
        for step in range(1, N_FAR)
    ]
    side_0 = moved(side_back, 0, 1, cores=[0])
    parts = call(
        spread_kernel,
        shaped((N_NEAR, CHUNK, D), BF16),
        ins=[vmem] * 4 + [anywhere],
        out_specs=vmem,
        mib=4,
    )(part, *others, side_0)
    mine = lax.all_to_all(parts, NEAR, 0, 0)
    mine = mine.reshape(4, HALF_D, D)
    other = swapped(mine)
    grads = call(
        mine_kernel,
        [shaped((D, 3 * D), F32), shaped((D, D), F32), shaped((1, D), F32)],
        [pltpu.VMEM((4, HALF_D, D), F32), pltpu.SemaphoreType.DMA((4,))],
        [vmem] * 3,
        [anywhere, anywhere, vmem],
        mib=6,
    )(mine, qkv_weight, gain)
    grad_qkv, grad_proj, grad_gain = call(
        other_kernel,
        [shaped((D, 3 * D), F32), shaped((D, D), F32), shaped((1, D), F32)],
        [
            pltpu.VMEM((4, HALF_D, D), F32),
            pltpu.SemaphoreType.DMA((4,)),
            pltpu.VMEM((1, D), F32),
            pltpu.SemaphoreType.DMA,
        ],
        [vmem] * 3 + [anywhere] * 2 + [vmem],
        [anywhere] * 3,
        mib=6,
        aliases={3: 0, 4: 1},
    )(other, qkv_weight, gain, *grads)
    mixed, grad_tokens = call(finish_kernel, [shaped((6, 12, 4, D), BF16)] * 2, mib=6)(
        tok, cot, own_back, lower_0, side_0, lower_1, side_1
    )
    return (
        mixed.transpose(2, 0, 1, 3),
        grad_tokens.transpose(2, 0, 1, 3),
        grad_qkv,
        grad_proj,
        grad_gain.reshape(D),
    )


def solution(mesh):
    fine = Mesh(mesh.devices.reshape(tuple(SIZES.values())), AXES)
    grid = P(None, LAT, LON, None)
    return jax.shard_map(
        on_device,
        mesh=fine,
        in_specs=(grid, grid, P(None, LAT, LON), P(), P(), P()),
        out_specs=(grid, grid, P(), P(), P()),
        check_vma=False,
    )
```

```python
import jax
import jax.numpy as jnp
from jax import lax
from jax.experimental import pallas as pl
from jax.experimental.pallas import tpu as pltpu
from jax.sharding import Mesh, PartitionSpec as P

D = 512
HALF_D = D // 2
HEADS = 8
HEAD = 64
PAIRS = HEADS // 2
WINDOWS = 2
COUNT = 144
TOKENS = WINDOWS * COUNT
HALF_R = 3
HALF_C = 6
EPS = 1e-05
TOGETHER = 8
SIZES = {"xl": 2, "zh": 4, "zl": 2, "c": 2, "y": 4, "xh": 2}
AXES = tuple(SIZES)
LAT = AXES[:4]
LON = AXES[4:]
N_NEAR = 32
FAR = "zh"
N_FAR = 4
CHUNK = 2 * D // N_NEAR
PIECE = (2, HALF_R, HALF_C, 4, D)
F32 = jnp.float32
BF16 = jnp.bfloat16


def spot(x, y, z, core):
    return ((x % 2) * 16 + z * 2 + core) * 8 + y * 2 + x // 2


FOUR, EIGHT, TWO = range(4), range(8), range(2)
LINES = [[spot(x, y, z, 0) for x in FOUR] for y in FOUR for z in EIGHT]
LINES += [[spot(x, y, z, 1) for y in FOUR] for x in FOUR for z in EIGHT]
SHEETS = [[spot(x, y, 2 * f + z, 0) for y in FOUR for z in TWO] for x in FOUR for f in FOUR]
SHEETS += [[spot(x, y, 2 * f + z, 1) for x in FOUR for z in TWO] for y in FOUR for f in FOUR]
NEAR = [[spot(x, y, 2 * f + z, 0) for x in FOUR for y in FOUR for z in TWO] for f in FOUR]
NEAR += [[spot(x, y, 2 * f + z, 1) for y in FOUR for x in FOUR for z in TWO] for f in FOUR]


def exchanged(parts, groups):
    return lax.all_to_all(parts, AXES, 0, 0, axis_index_groups=groups)


def dot(left, right):
    return jnp.dot(left, right, preferred_element_type=F32)


def dot_first(left, right):
    return lax.dot_general(left, right, (((0,), (0,)), ((), ())), preferred_element_type=F32)


def dot_last(left, right):
    return lax.dot_general(left, right, (((1,), (1,)), ((), ())), preferred_element_type=F32)


def pack_kernel(tok_ref, cot_ref, own_ref, right_ref, below_ref, corner_ref, sems):
    copies = []
    for n, ref in enumerate((tok_ref, cot_ref)):
        for rows, cols, piece in quadrants(own_ref, right_ref, below_ref, corner_ref):
            sem = sems.at[len(copies)]
            copies.append(pltpu.make_async_copy(ref.at[rows, cols], piece.at[n], sem))
    for copy in copies:
        copy.start()
    for copy in copies:
        copy.wait()


def quadrants(own, right, below, corner):
    late_r, early_r = pl.ds(HALF_R, HALF_R), pl.ds(0, HALF_R)
    late_c, early_c = pl.ds(HALF_C, HALF_C), pl.ds(0, HALF_C)
    return (
        (late_r, late_c, own),
        (late_r, early_c, right),
        (early_r, late_c, below),
        (early_r, early_c, corner),
    )


def source_of(place):
    window = place // COUNT
    rest = place - window * COUNT
    level = (1 + 2 * window + rest % 2) % 4
    return (rest // 2) * 4 + level


def attend_kernel(
    corner_ref, right_ref, below_ref, own_ref, bias_ref, gain_ref, qkv_ref, proj_ref,
    send_ref, left_ref, rows_ref, att_ref, normed_ref, inv_ref,
):
    first = lax.broadcasted_iota(jnp.int32, (TOKENS, 1), 0)
    second = lax.broadcasted_iota(jnp.int32, (TOKENS, TOKENS), 1)
    to_order = (second == source_of(first)).astype(BF16)
    pieces = (own_ref, right_ref, below_ref, corner_ref)

    def gathered(n):
        return jnp.concatenate([ref[n] for ref in pieces], axis=0).reshape(TOKENS, D)

    values = dot(to_order, gathered(0))
    cot = dot(to_order, gathered(1)).astype(BF16)
    gain = gain_ref[...]
    mean = jnp.mean(values, -1, keepdims=True)
    centred = values - mean
    inv_std = lax.rsqrt(jnp.mean(centred * centred, -1, keepdims=True) + EPS)
    normed = centred * inv_std
    hidden = (normed * gain).astype(BF16)
    projected = dot(hidden, qkv_ref[...]).astype(BF16)
    grad_att = dot_last(cot, proj_ref[...]).astype(BF16)
    normed_ref[...] = normed
    inv_ref[...] = inv_std
    left_ref[0] = hidden.T
    rows_ref[3] = cot

    lane = lax.broadcasted_iota(jnp.int32, (COUNT, 2 * HEAD), 1)
    low = lane < HEAD
    zero = jnp.zeros((COUNT, 2 * HEAD), BF16)

    def both(pair):
        return jnp.concatenate([jnp.where(low, pair, zero), jnp.where(low, zero, pair)], axis=0)

    def merged(stacked):
        return jnp.where(low, stacked[:COUNT], stacked[COUNT:])

    factor = HEAD ** (-0.5)
    biases = [jnp.concatenate([bias_ref[w]] * 2, axis=1) for w in range(WINDOWS)]
    spots = [(w, p) for w in range(WINDOWS) for p in range(PAIRS)]
    for at in range(0, len(spots), TOGETHER):
        here, cols, bias = [], [], []
        for window, pair in spots[at : at + TOGETHER]:
            here.append(slice(window * COUNT, (window + 1) * COUNT))
            cols.append(slice(pair * 2 * HEAD, (pair + 1) * 2 * HEAD))
            bias.append(biases[window])
        each = range(len(here))
        query = [both(projected[here[i], cols[i]] * jnp.asarray(factor, BF16)) for i in each]
        keys = [projected[here[i], D + cols[i].start : D + cols[i].stop] for i in each]
        vals = [projected[here[i], 2 * D + cols[i].start : 2 * D + cols[i].stop] for i in each]
        grad_out = [both(grad_att[here[i], cols[i]]) for i in each]
        scores = [dot_last(keys[i], query[i]) + bias[i] for i in each]
        grad_weights = [dot_last(vals[i], grad_out[i]) for i in each]
        numer = [jnp.exp(s - jnp.max(s, 0, keepdims=True)) for s in scores]
        weights = [n * (1.0 / jnp.sum(n, 0, keepdims=True)) for n in numer]
        weights_low = [w.astype(BF16) for w in weights]
        inner = [jnp.sum(g * w, 0, keepdims=True) for g, w in zip(grad_weights, weights)]
        grad_scores = [
            (w * (g - i)).astype(BF16) for w, g, i in zip(weights, grad_weights, inner)
        ]
        for i in each:
            att_ref[here[i], cols[i]] = merged(dot_first(weights_low[i], vals[i])).astype(BF16)
            rows_ref[2, here[i], cols[i]] = dot(weights_low[i], grad_out[i]).astype(BF16)
        for i in each:
            grad_query = merged(dot_first(grad_scores[i], keys[i])) * factor
            rows_ref[0, here[i], cols[i]] = grad_query.astype(BF16)
            rows_ref[1, here[i], cols[i]] = dot(grad_scores[i], query[i]).astype(BF16)

    left_ref[1] = att_ref[...].T
    half_grads(1 - lax.axis_index("c"), left_ref, rows_ref, send_ref)


def half_grads(half, left_ref, rows_ref, out_ref):
    here = pl.ds(pl.multiple_of(half * HALF_D, HALF_D), HALF_D)
    for block in range(4):
        out_ref[block] = dot(left_ref[block // 3, here], rows_ref[block]).astype(BF16)


def rest_kernel(
    left_ref, rows_ref, att_ref, normed_ref, inv_ref, gain_ref, qkv_ref, proj_ref,
    keep_ref, own_out, right_out, lower_out,
):
    half_grads(lax.axis_index("c"), left_ref, rows_ref, keep_ref)
    first = lax.broadcasted_iota(jnp.int32, (TOKENS, TOKENS), 0)
    second = lax.broadcasted_iota(jnp.int32, (1, TOKENS), 1)
    from_order = (first == source_of(second)).astype(BF16)
    normed = normed_ref[...]
    inv_std = inv_ref[...]
    attended = att_ref[...]
    gain = gain_ref[...]
    branch = dot(attended, proj_ref[...]).astype(BF16)
    grad_hidden = dot_last(rows_ref[0], qkv_ref[:, :D])
    grad_hidden += dot_last(rows_ref[1], qkv_ref[:, D : 2 * D])
    grad_hidden += dot_last(rows_ref[2], qkv_ref[:, 2 * D :])
    grad_norm = grad_hidden * gain
    grad_shift = inv_std * (
        grad_norm
        - jnp.mean(grad_norm, -1, keepdims=True)
        - normed * jnp.mean(grad_norm * normed, -1, keepdims=True)
    )
    for n, result in enumerate((branch, grad_shift.astype(BF16))):
        back = dot(from_order, result).reshape(4, HALF_R, HALF_C, 4, D).astype(BF16)
        own_out[n] = back[0]
        right_out[n] = back[1]
        lower_out[0, n] = back[2]
        lower_out[1, n] = back[3]


def weights_kernel(qkv_ref, proj_ref, gain_ref, qkv_out, proj_out, gain_out, sems):
    copies = [
        pltpu.make_async_copy(ref, out, sems.at[n])
        for n, (ref, out) in enumerate(
            ((qkv_ref, qkv_out), (proj_ref, proj_out), (gain_ref, gain_out))
        )
    ]
    for copy in copies:
        copy.start()
    for copy in copies:
        copy.wait()


def add_kernel(keep_ref, got_ref, out_ref, held, sems):
    copies = []
    for block in range(4):
        held[block] = (keep_ref[block].astype(F32) + got_ref[block].astype(F32)).astype(BF16)
        copy = pltpu.make_async_copy(held.at[block], out_ref.at[block], sems.at[block])
        copy.start()
        copies.append(copy)
    for copy in copies:
        copy.wait()


def line_kernel(got_ref, out_ref):
    for n in range(8):
        rows = slice(n * CHUNK, (n + 1) * CHUNK)
        total = got_ref[0, rows].astype(F32)
        for line in range(1, 4):
            total += got_ref[line, rows].astype(F32)
        out_ref[n] = total.astype(BF16)


def sum_kernel(got_ref, lower_ref, right_ref, out_ref, side_ref):
    side_ref[0] = right_ref[...]
    side_ref[1] = lower_ref[1]
    total = got_ref[0].astype(F32)
    for n in range(1, got_ref.shape[0]):
        total += got_ref[n].astype(F32)
    out_ref[...] = total.astype(BF16)


def spread_kernel(own_ref, one_ref, two_ref, three_ref, side_ref, out_ref):
    del side_ref
    even = own_ref[...].astype(F32) + two_ref[...].astype(F32)
    odd = one_ref[...].astype(F32) + three_ref[...].astype(F32)
    total = (even + odd).astype(BF16)
    for n in range(out_ref.shape[0]):
        out_ref[n] = total


def finish_kernel(tok_ref, cot_ref, own_ref, lower_ref, side_ref, mixed_ref, grad_ref):
    right_ref, below_ref, corner_ref = side_ref.at[0], lower_ref.at[0], side_ref.at[1]
    for n, (ref, out) in enumerate(((tok_ref, mixed_ref), (cot_ref, grad_ref))):
        for rows, cols, piece in quadrants(own_ref, right_ref, below_ref, corner_ref):
            out[rows, cols] = (ref[rows, cols].astype(F32) + piece[n].astype(F32)).astype(BF16)


def grads_half(half, ref, qkv_ref, gain_ref, qkv_out, proj_out, gain_out, wide, sems):
    copies = []
    here = pl.ds(pl.multiple_of(half * HALF_D, HALF_D), HALF_D)
    total = jnp.zeros((HALF_D, 128), F32)
    for block in range(4):
        part = ref[block].astype(F32)
        wide[block] = part
        cols = pl.ds(block * D, D)
        out = proj_out.at[here] if block == 3 else qkv_out.at[here, cols]
        copy = pltpu.make_async_copy(wide.at[block], out, sems.at[block])
        copy.start()
        copies.append(copy)
        if block < 3:
            product = part * qkv_ref[here, cols].astype(F32)
            for q in range(4):
                total += product[:, q * 128 : (q + 1) * 128]
    sums = jnp.sum(total.T, axis=0, keepdims=True)
    gain_out[:, here] = sums / gain_ref[:, here]
    return copies


def mine_kernel(ref, qkv_ref, gain_ref, qkv_out, proj_out, gain_out, wide, sems):
    gain_out[...] = jnp.zeros_like(gain_out)
    core = lax.axis_index("c")
    copies = grads_half(core, ref, qkv_ref, gain_ref, qkv_out, proj_out, gain_out, wide, sems)
    for copy in copies:
        copy.wait()


def other_kernel(
    ref, qkv_ref, gain_ref, qkv_in, proj_in, gain_in, qkv_out, proj_out, gain_out, wide, sems,
    held, gain_sem,
):
    del qkv_in, proj_in
    held[...] = gain_in[...]
    half = 1 - lax.axis_index("c")
    copies = grads_half(half, ref, qkv_ref, gain_ref, qkv_out, proj_out, held, wide, sems)
    copies.append(pltpu.make_async_copy(held, gain_out, gain_sem))
    copies[-1].start()
    for copy in copies:
        copy.wait()


def call(kernel, outs, scratch=(), ins=None, out_specs=None, mib=8, aliases=None):
    more = {"input_output_aliases": aliases or {}}
    if ins is not None:
        more["in_specs"] = ins
    if out_specs is not None:
        more["out_specs"] = out_specs
    return pl.pallas_call(
        kernel,
        out_shape=outs,
        scratch_shapes=list(scratch),
        compiler_params=pltpu.CompilerParams(vmem_limit_bytes=mib * 1024 * 1024),
        **more,
    )


def in_hbm(array):
    return pltpu.with_memory_space_constraint(array, pltpu.HBM)


def shaped(shape, dtype):
    return jax.ShapeDtypeStruct(shape, dtype)


def moved(block, lat_step, lon_step):
    route = [
        (lat * 8 + lon, (lat + lat_step) % 32 * 8 + (lon + lon_step) % 8)
        for lat in range(32)
        for lon in range(8)
    ]
    return lax.ppermute(block, AXES, route)


def swapped(block):
    return lax.ppermute(block, "c", [(0, 1), (1, 0)])


def on_device(tokens, cotangent, region, gain, qkv_weight, proj_weight):
    tok = tokens.transpose(1, 2, 0, 3)
    cot = cotangent.transpose(1, 2, 0, 3)
    anywhere = pl.BlockSpec(memory_space=pl.ANY)
    vmem = pl.BlockSpec(memory_space=pltpu.VMEM)
    hbm = pl.BlockSpec(memory_space=pltpu.HBM)
    own, right, below, corner = call(
        pack_kernel,
        [shaped(PIECE, BF16)] * 4,
        [pltpu.SemaphoreType.DMA((8,))],
        [hbm] * 2,
        [vmem] * 4,
        mib=2,
    )(in_hbm(tok), in_hbm(cot))
    corner = moved(corner, -1, -1)
    right = moved(right, 0, -1)
    below = moved(below, -1, 0)
    ids = region.reshape(2, 2, 2, HALF_R, 2, HALF_C).transpose(0, 2, 4, 3, 5, 1).reshape(2, COUNT)
    bias = jnp.where(ids[:, :, None] == ids[:, None, :], 0.0, -1e30).astype(F32)
    gain = gain.reshape(1, D)
    qkv_weight, proj_weight, gain = call(
        weights_kernel,
        [shaped((D, 3 * D), BF16), shaped((D, D), BF16), shaped((1, D), F32)],
        [pltpu.SemaphoreType.DMA((3,))],
        [hbm] * 3,
        [vmem] * 3,
        mib=1,
    )(in_hbm(qkv_weight), in_hbm(proj_weight), in_hbm(gain))
    send, *state = call(
        attend_kernel,
        [
            shaped((4, HALF_D, D), BF16),
            shaped((2, D, TOKENS), BF16),
            shaped((4, TOKENS, D), BF16),
            shaped((TOKENS, D), BF16),
            shaped((TOKENS, D), F32),
            shaped((TOKENS, 1), F32),
        ],
        mib=16,
    )(corner, right, below, own, bias, gain, qkv_weight, proj_weight)
    got = swapped(send)
    pair = shaped((2,) + PIECE, BF16)
    keep, own_back, right_back, lower_back = call(
        rest_kernel,
        [shaped((4, HALF_D, D), BF16), shaped(PIECE, BF16), shaped(PIECE, BF16), pair],
        mib=16,
    )(*state, gain, qkv_weight, proj_weight)
    half = call(
        add_kernel,
        shaped((4, HALF_D, D), BF16),
        [pltpu.VMEM((4, HALF_D, D), BF16), pltpu.SemaphoreType.DMA((4,))],
        [vmem] * 2,
        anywhere,
        mib=4,
    )(keep, got)
    got = exchanged(half.reshape(4, 8 * CHUNK, D), LINES)
    part = call(line_kernel, shaped((8, CHUNK, D), BF16), mib=6)(got)
    got = exchanged(part, SHEETS)
    lower_back = moved(lower_back, 1, 0)
    part, side_back = call(
        sum_kernel, [shaped((CHUNK, D), BF16), pair], ins=[vmem] * 3, out_specs=[vmem] * 2, mib=6
    )(got, lower_back, right_back)
    others = [
        lax.ppermute(part, FAR, [(n, (n - step) % N_FAR) for n in range(N_FAR)])
        for step in range(1, N_FAR)
    ]
    side_back = moved(side_back, 0, 1)
    parts = call(
        spread_kernel,
        shaped((N_NEAR, CHUNK, D), BF16),
        ins=[vmem] * 4 + [anywhere],
        out_specs=vmem,
        mib=4,
    )(part, *others, side_back)
    mine = exchanged(parts, NEAR)
    mine = mine.reshape(4, HALF_D, D)
    other = swapped(mine)
    grads = call(
        mine_kernel,
        [shaped((D, 3 * D), F32), shaped((D, D), F32), shaped((1, D), F32)],
        [pltpu.VMEM((4, HALF_D, D), F32), pltpu.SemaphoreType.DMA((4,))],
        [vmem] * 3,
        [anywhere, anywhere, vmem],
        mib=6,
    )(mine, qkv_weight, gain)
    grad_qkv, grad_proj, grad_gain = call(
        other_kernel,
        [shaped((D, 3 * D), F32), shaped((D, D), F32), shaped((1, D), F32)],
        [
            pltpu.VMEM((4, HALF_D, D), F32),
            pltpu.SemaphoreType.DMA((4,)),
            pltpu.VMEM((1, D), F32),
            pltpu.SemaphoreType.DMA,
        ],
        [vmem] * 3 + [anywhere] * 2 + [vmem],
        [anywhere] * 3,
        mib=6,
        aliases={3: 0, 4: 1},
    )(other, qkv_weight, gain, *grads)
    mixed, grad_tokens = call(finish_kernel, [shaped((6, 12, 4, D), BF16)] * 2, mib=6)(
        tok, cot, own_back, lower_back, side_back
    )
    return (
        mixed.transpose(2, 0, 1, 3),
        grad_tokens.transpose(2, 0, 1, 3),
        grad_qkv,
        grad_proj,
        grad_gain.reshape(D),
    )


def solution(mesh):
    fine = Mesh(mesh.devices.reshape(tuple(SIZES.values())), AXES)
    grid = P(None, LAT, LON, None)
    return jax.shard_map(
        on_device,
        mesh=fine,
        in_specs=(grid, grid, P(None, LAT, LON), P(), P(), P()),
        out_specs=(grid, grid, P(), P(), P()),
        check_vma=False,
    )
```

```python
import jax
import jax.numpy as jnp
from jax import lax
from jax.experimental import pallas as pl
from jax.experimental.pallas import tpu as pltpu
from jax.sharding import Mesh, PartitionSpec as P

D = 512
HALF_D = D // 2
HEADS = 8
HEAD = 64
PAIRS = HEADS // 2
WINDOWS = 2
COUNT = 144
TOKENS = WINDOWS * COUNT
HALF_R = 3
HALF_C = 6
EPS = 1e-05
TOGETHER = 8
SIZES = {"xl": 2, "zh": 4, "zl": 2, "c": 2, "y": 4, "xh": 2}
AXES = tuple(SIZES)
LAT = AXES[:4]
LON = AXES[4:]
N_NEAR = 32
FAR = "zh"
N_FAR = 4
CHUNK = 2 * D // N_NEAR
PIECE = (2, HALF_R, HALF_C, 4, D)
F32 = jnp.float32
BF16 = jnp.bfloat16


def spot(x, y, z, core):
    return ((x % 2) * 16 + z * 2 + core) * 8 + y * 2 + x // 2


FOUR, EIGHT, TWO = range(4), range(8), range(2)
LINES = [[spot(x, y, z, 0) for x in FOUR] for y in FOUR for z in EIGHT]
LINES += [[spot(x, y, z, 1) for y in FOUR] for x in FOUR for z in EIGHT]
SHEETS = [[spot(x, y, 2 * f + z, 0) for y in FOUR for z in TWO] for x in FOUR for f in FOUR]
SHEETS += [[spot(x, y, 2 * f + z, 1) for x in FOUR for z in TWO] for y in FOUR for f in FOUR]
NEAR = [[spot(x, y, 2 * f + z, 0) for x in FOUR for y in FOUR for z in TWO] for f in FOUR]
NEAR += [[spot(x, y, 2 * f + z, 1) for y in FOUR for x in FOUR for z in TWO] for f in FOUR]


def exchanged(parts, groups):
    return lax.all_to_all(parts, AXES, 0, 0, axis_index_groups=groups)


def dot(left, right):
    return jnp.dot(left, right, preferred_element_type=F32)


def dot_first(left, right):
    return lax.dot_general(left, right, (((0,), (0,)), ((), ())), preferred_element_type=F32)


def dot_last(left, right):
    return lax.dot_general(left, right, (((1,), (1,)), ((), ())), preferred_element_type=F32)


def pack_kernel(tok_ref, cot_ref, own_ref, right_ref, below_ref, corner_ref, sems):
    copies = []
    for n, ref in enumerate((tok_ref, cot_ref)):
        for rows, cols, piece in quadrants(own_ref, right_ref, below_ref, corner_ref):
            sem = sems.at[len(copies)]
            copies.append(pltpu.make_async_copy(ref.at[rows, cols], piece.at[n], sem))
    for copy in copies:
        copy.start()
    for copy in copies:
        copy.wait()


def quadrants(own, right, below, corner):
    late_r, early_r = pl.ds(HALF_R, HALF_R), pl.ds(0, HALF_R)
    late_c, early_c = pl.ds(HALF_C, HALF_C), pl.ds(0, HALF_C)
    return (
        (late_r, late_c, own),
        (late_r, early_c, right),
        (early_r, late_c, below),
        (early_r, early_c, corner),
    )


def source_of(place):
    window = place // COUNT
    rest = place - window * COUNT
    level = (1 + 2 * window + rest % 2) % 4
    return (rest // 2) * 4 + level


def attend_kernel(
    corner_ref, right_ref, below_ref, own_ref, bias_ref, gain_ref, qkv_ref, proj_ref,
    send_ref, left_ref, rows_ref, att_ref, normed_ref, inv_ref,
):
    first = lax.broadcasted_iota(jnp.int32, (TOKENS, 1), 0)
    second = lax.broadcasted_iota(jnp.int32, (TOKENS, TOKENS), 1)
    to_order = (second == source_of(first)).astype(BF16)
    pieces = (own_ref, right_ref, below_ref, corner_ref)

    def gathered(n):
        return jnp.concatenate([ref[n] for ref in pieces], axis=0).reshape(TOKENS, D)

    values = dot(to_order, gathered(0))
    cot = dot(to_order, gathered(1)).astype(BF16)
    gain = gain_ref[...]
    mean = jnp.mean(values, -1, keepdims=True)
    centred = values - mean
    inv_std = lax.rsqrt(jnp.mean(centred * centred, -1, keepdims=True) + EPS)
    normed = centred * inv_std
    hidden = (normed * gain).astype(BF16)
    projected = dot(hidden, qkv_ref[...]).astype(BF16)
    grad_att = dot_last(cot, proj_ref[...]).astype(BF16)
    normed_ref[...] = normed
    inv_ref[...] = inv_std
    left_ref[0] = hidden.T
    rows_ref[3] = cot

    lane = lax.broadcasted_iota(jnp.int32, (COUNT, 2 * HEAD), 1)
    low = lane < HEAD
    zero = jnp.zeros((COUNT, 2 * HEAD), BF16)

    def both(pair):
        return jnp.concatenate([jnp.where(low, pair, zero), jnp.where(low, zero, pair)], axis=0)

    def merged(stacked):
        return jnp.where(low, stacked[:COUNT], stacked[COUNT:])

    factor = HEAD ** (-0.5)
    biases = [jnp.concatenate([bias_ref[w]] * 2, axis=1) for w in range(WINDOWS)]
    spots = [(w, p) for w in range(WINDOWS) for p in range(PAIRS)]
    for at in range(0, len(spots), TOGETHER):
        here, cols, bias = [], [], []
        for window, pair in spots[at : at + TOGETHER]:
            here.append(slice(window * COUNT, (window + 1) * COUNT))
            cols.append(slice(pair * 2 * HEAD, (pair + 1) * 2 * HEAD))
            bias.append(biases[window])
        each = range(len(here))
        query = [both(projected[here[i], cols[i]] * jnp.asarray(factor, BF16)) for i in each]
        keys = [projected[here[i], D + cols[i].start : D + cols[i].stop] for i in each]
        vals = [projected[here[i], 2 * D + cols[i].start : 2 * D + cols[i].stop] for i in each]
        grad_out = [both(grad_att[here[i], cols[i]]) for i in each]
        scores = [dot_last(keys[i], query[i]) + bias[i] for i in each]
        grad_weights = [dot_last(vals[i], grad_out[i]) for i in each]
        numer = [jnp.exp(s - jnp.max(s, 0, keepdims=True)) for s in scores]
        weights = [n * (1.0 / jnp.sum(n, 0, keepdims=True)) for n in numer]
        weights_low = [w.astype(BF16) for w in weights]
        inner = [jnp.sum(g * w, 0, keepdims=True) for g, w in zip(grad_weights, weights)]
        grad_scores = [
            (w * (g - i)).astype(BF16) for w, g, i in zip(weights, grad_weights, inner)
        ]
        for i in each:
            att_ref[here[i], cols[i]] = merged(dot_first(weights_low[i], vals[i])).astype(BF16)
            rows_ref[2, here[i], cols[i]] = dot(weights_low[i], grad_out[i]).astype(BF16)
        for i in each:
            grad_query = merged(dot_first(grad_scores[i], keys[i])) * factor
            rows_ref[0, here[i], cols[i]] = grad_query.astype(BF16)
            rows_ref[1, here[i], cols[i]] = dot(grad_scores[i], query[i]).astype(BF16)

    left_ref[1] = att_ref[...].T
    half_grads(1 - lax.axis_index("c"), left_ref, rows_ref, send_ref)


def half_grads(half, left_ref, rows_ref, out_ref):
    here = pl.ds(pl.multiple_of(half * HALF_D, HALF_D), HALF_D)
    for block in range(4):
        out_ref[block] = dot(left_ref[block // 3, here], rows_ref[block]).astype(BF16)


def rest_kernel(
    left_ref, rows_ref, att_ref, normed_ref, inv_ref, gain_ref, qkv_ref, proj_ref,
    keep_ref, own_out, right_out, lower_out,
):
    half_grads(lax.axis_index("c"), left_ref, rows_ref, keep_ref)
    first = lax.broadcasted_iota(jnp.int32, (TOKENS, TOKENS), 0)
    second = lax.broadcasted_iota(jnp.int32, (1, TOKENS), 1)
    from_order = (first == source_of(second)).astype(BF16)
    normed = normed_ref[...]
    inv_std = inv_ref[...]
    attended = att_ref[...]
    gain = gain_ref[...]
    branch = dot(attended, proj_ref[...]).astype(BF16)
    grad_hidden = dot_last(rows_ref[0], qkv_ref[:, :D])
    grad_hidden += dot_last(rows_ref[1], qkv_ref[:, D : 2 * D])
    grad_hidden += dot_last(rows_ref[2], qkv_ref[:, 2 * D :])
    grad_norm = grad_hidden * gain
    grad_shift = inv_std * (
        grad_norm
        - jnp.mean(grad_norm, -1, keepdims=True)
        - normed * jnp.mean(grad_norm * normed, -1, keepdims=True)
    )
    for n, result in enumerate((branch, grad_shift.astype(BF16))):
        back = dot(from_order, result).reshape(4, HALF_R, HALF_C, 4, D).astype(BF16)
        own_out[n] = back[0]
        right_out[n] = back[1]
        lower_out[0, n] = back[2]
        lower_out[1, n] = back[3]


def weights_kernel(qkv_ref, proj_ref, gain_ref, qkv_out, proj_out, gain_out, sems):
    copies = [
        pltpu.make_async_copy(ref, out, sems.at[n])
        for n, (ref, out) in enumerate(
            ((qkv_ref, qkv_out), (proj_ref, proj_out), (gain_ref, gain_out))
        )
    ]
    for copy in copies:
        copy.start()
    for copy in copies:
        copy.wait()


def add_kernel(keep_ref, got_ref, out_ref, held, sems):
    copies = []
    for block in range(4):
        held[block] = (keep_ref[block].astype(F32) + got_ref[block].astype(F32)).astype(BF16)
        copy = pltpu.make_async_copy(held.at[block], out_ref.at[block], sems.at[block])
        copy.start()
        copies.append(copy)
    for copy in copies:
        copy.wait()


def line_kernel(got_ref, lower_ref, out_ref):
    del lower_ref
    for n in range(8):
        rows = slice(n * CHUNK, (n + 1) * CHUNK)
        total = got_ref[0, rows].astype(F32)
        for line in range(1, 4):
            total += got_ref[line, rows].astype(F32)
        out_ref[n] = total.astype(BF16)


def sum_kernel(got_ref, lower_ref, right_ref, out_ref, side_ref):
    side_ref[0] = right_ref[...]
    side_ref[1] = lower_ref[1]
    total = got_ref[0].astype(F32)
    for n in range(1, got_ref.shape[0]):
        total += got_ref[n].astype(F32)
    out_ref[...] = total.astype(BF16)


def spread_kernel(own_ref, one_ref, two_ref, three_ref, side_ref, out_ref):
    del side_ref
    even = own_ref[...].astype(F32) + two_ref[...].astype(F32)
    odd = one_ref[...].astype(F32) + three_ref[...].astype(F32)
    total = (even + odd).astype(BF16)
    for n in range(out_ref.shape[0]):
        out_ref[n] = total


def finish_kernel(tok_ref, cot_ref, own_ref, lower_ref, side_ref, mixed_ref, grad_ref):
    right_ref, below_ref, corner_ref = side_ref.at[0], lower_ref.at[0], side_ref.at[1]
    for n, (ref, out) in enumerate(((tok_ref, mixed_ref), (cot_ref, grad_ref))):
        for rows, cols, piece in quadrants(own_ref, right_ref, below_ref, corner_ref):
            out[rows, cols] = (ref[rows, cols].astype(F32) + piece[n].astype(F32)).astype(BF16)


def grads_half(half, ref, qkv_ref, gain_ref, qkv_out, proj_out, gain_out, wide, sems):
    copies = []
    here = pl.ds(pl.multiple_of(half * HALF_D, HALF_D), HALF_D)
    total = jnp.zeros((HALF_D, 128), F32)
    for block in range(4):
        part = ref[block].astype(F32)
        wide[block] = part
        cols = pl.ds(block * D, D)
        out = proj_out.at[here] if block == 3 else qkv_out.at[here, cols]
        copy = pltpu.make_async_copy(wide.at[block], out, sems.at[block])
        copy.start()
        copies.append(copy)
        if block < 3:
            product = part * qkv_ref[here, cols].astype(F32)
            for q in range(4):
                total += product[:, q * 128 : (q + 1) * 128]
    sums = jnp.sum(total.T, axis=0, keepdims=True)
    gain_out[:, here] = sums / gain_ref[:, here]
    return copies


def mine_kernel(ref, qkv_ref, gain_ref, qkv_out, proj_out, gain_out, wide, sems):
    gain_out[...] = jnp.zeros_like(gain_out)
    core = lax.axis_index("c")
    copies = grads_half(core, ref, qkv_ref, gain_ref, qkv_out, proj_out, gain_out, wide, sems)
    for copy in copies:
        copy.wait()


def other_kernel(
    ref, qkv_ref, gain_ref, qkv_in, proj_in, gain_in, qkv_out, proj_out, gain_out, wide, sems,
    held, gain_sem,
):
    del qkv_in, proj_in
    held[...] = gain_in[...]
    half = 1 - lax.axis_index("c")
    copies = grads_half(half, ref, qkv_ref, gain_ref, qkv_out, proj_out, held, wide, sems)
    copies.append(pltpu.make_async_copy(held, gain_out, gain_sem))
    copies[-1].start()
    for copy in copies:
        copy.wait()


def call(kernel, outs, scratch=(), ins=None, out_specs=None, mib=8, aliases=None):
    more = {"input_output_aliases": aliases or {}}
    if ins is not None:
        more["in_specs"] = ins
    if out_specs is not None:
        more["out_specs"] = out_specs
    return pl.pallas_call(
        kernel,
        out_shape=outs,
        scratch_shapes=list(scratch),
        compiler_params=pltpu.CompilerParams(vmem_limit_bytes=mib * 1024 * 1024),
        **more,
    )


def in_hbm(array):
    return pltpu.with_memory_space_constraint(array, pltpu.HBM)


def shaped(shape, dtype):
    return jax.ShapeDtypeStruct(shape, dtype)


def moved(block, lat_step, lon_step):
    route = [
        (lat * 8 + lon, (lat + lat_step) % 32 * 8 + (lon + lon_step) % 8)
        for lat in range(32)
        for lon in range(8)
    ]
    return lax.ppermute(block, AXES, route)


def swapped(block):
    return lax.ppermute(block, "c", [(0, 1), (1, 0)])


def on_device(tokens, cotangent, region, gain, qkv_weight, proj_weight):
    tok = tokens.transpose(1, 2, 0, 3)
    cot = cotangent.transpose(1, 2, 0, 3)
    anywhere = pl.BlockSpec(memory_space=pl.ANY)
    vmem = pl.BlockSpec(memory_space=pltpu.VMEM)
    hbm = pl.BlockSpec(memory_space=pltpu.HBM)
    own, right, below, corner = call(
        pack_kernel,
        [shaped(PIECE, BF16)] * 4,
        [pltpu.SemaphoreType.DMA((8,))],
        [hbm] * 2,
        [vmem] * 4,
        mib=2,
    )(in_hbm(tok), in_hbm(cot))
    corner = moved(corner, -1, -1)
    right = moved(right, 0, -1)
    below = moved(below, -1, 0)
    ids = region.reshape(2, 2, 2, HALF_R, 2, HALF_C).transpose(0, 2, 4, 3, 5, 1).reshape(2, COUNT)
    bias = jnp.where(ids[:, :, None] == ids[:, None, :], 0.0, -1e30).astype(F32)
    gain = gain.reshape(1, D)
    qkv_weight, proj_weight, gain = call(
        weights_kernel,
        [shaped((D, 3 * D), BF16), shaped((D, D), BF16), shaped((1, D), F32)],
        [pltpu.SemaphoreType.DMA((3,))],
        [hbm] * 3,
        [vmem] * 3,
        mib=1,
    )(in_hbm(qkv_weight), in_hbm(proj_weight), in_hbm(gain))
    send, *state = call(
        attend_kernel,
        [
            shaped((4, HALF_D, D), BF16),
            shaped((2, D, TOKENS), BF16),
            shaped((4, TOKENS, D), BF16),
            shaped((TOKENS, D), BF16),
            shaped((TOKENS, D), F32),
            shaped((TOKENS, 1), F32),
        ],
        mib=16,
    )(corner, right, below, own, bias, gain, qkv_weight, proj_weight)
    got = swapped(send)
    pair = shaped((2,) + PIECE, BF16)
    keep, own_back, right_back, lower_back = call(
        rest_kernel,
        [shaped((4, HALF_D, D), BF16), shaped(PIECE, BF16), shaped(PIECE, BF16), pair],
        mib=16,
    )(*state, gain, qkv_weight, proj_weight)
    half = call(
        add_kernel,
        shaped((4, HALF_D, D), BF16),
        [pltpu.VMEM((4, HALF_D, D), BF16), pltpu.SemaphoreType.DMA((4,))],
        [vmem] * 2,
        anywhere,
        mib=4,
    )(keep, got)
    got = exchanged(half.reshape(4, 8 * CHUNK, D), LINES)
    lower_back = moved(lower_back, 1, 0)
    part = call(
        line_kernel, shaped((8, CHUNK, D), BF16), ins=[vmem, anywhere], out_specs=vmem, mib=6
    )(got, lower_back)
    got = exchanged(part, SHEETS)
    part, side_back = call(
        sum_kernel, [shaped((CHUNK, D), BF16), pair], ins=[vmem] * 3, out_specs=[vmem] * 2, mib=6
    )(got, lower_back, right_back)
    others = [
        lax.ppermute(part, FAR, [(n, (n - step) % N_FAR) for n in range(N_FAR)])
        for step in range(1, N_FAR)
    ]
    side_back = moved(side_back, 0, 1)
    parts = call(
        spread_kernel,
        shaped((N_NEAR, CHUNK, D), BF16),
        ins=[vmem] * 4 + [anywhere],
        out_specs=vmem,
        mib=4,
    )(part, *others, side_back)
    mine = exchanged(parts, NEAR)
    mine = mine.reshape(4, HALF_D, D)
    other = swapped(mine)
    grads = call(
        mine_kernel,
        [shaped((D, 3 * D), F32), shaped((D, D), F32), shaped((1, D), F32)],
        [pltpu.VMEM((4, HALF_D, D), F32), pltpu.SemaphoreType.DMA((4,))],
        [vmem] * 3,
        [anywhere, anywhere, vmem],
        mib=6,
    )(mine, qkv_weight, gain)
    grad_qkv, grad_proj, grad_gain = call(
        other_kernel,
        [shaped((D, 3 * D), F32), shaped((D, D), F32), shaped((1, D), F32)],
        [
            pltpu.VMEM((4, HALF_D, D), F32),
            pltpu.SemaphoreType.DMA((4,)),
            pltpu.VMEM((1, D), F32),
            pltpu.SemaphoreType.DMA,
        ],
        [vmem] * 3 + [anywhere] * 2 + [vmem],
        [anywhere] * 3,
        mib=6,
        aliases={3: 0, 4: 1},
    )(other, qkv_weight, gain, *grads)
    mixed, grad_tokens = call(finish_kernel, [shaped((6, 12, 4, D), BF16)] * 2, mib=6)(
        tok, cot, own_back, lower_back, side_back
    )
    return (
        mixed.transpose(2, 0, 1, 3),
        grad_tokens.transpose(2, 0, 1, 3),
        grad_qkv,
        grad_proj,
        grad_gain.reshape(D),
    )


def solution(mesh):
    fine = Mesh(mesh.devices.reshape(tuple(SIZES.values())), AXES)
    grid = P(None, LAT, LON, None)
    return jax.shard_map(
        on_device,
        mesh=fine,
        in_specs=(grid, grid, P(None, LAT, LON), P(), P(), P()),
        out_specs=(grid, grid, P(), P(), P()),
        check_vma=False,
    )
```

```python
import jax
import jax.numpy as jnp
from jax import lax
from jax.experimental import pallas as pl
from jax.experimental.pallas import tpu as pltpu
from jax.sharding import Mesh, PartitionSpec as P

D = 512
HALF_D = D // 2
HEADS = 8
HEAD = 64
PAIRS = HEADS // 2
WINDOWS = 2
COUNT = 144
TOKENS = WINDOWS * COUNT
HALF_R = 3
HALF_C = 6
EPS = 1e-05
TOGETHER = 8
SIZES = {"xl": 2, "zh": 4, "zl": 2, "c": 2, "y": 4, "xh": 2}
AXES = tuple(SIZES)
LAT = AXES[:4]
LON = AXES[4:]
N_NEAR = 32
FAR = "zh"
N_FAR = 4
CHUNK = 2 * D // N_NEAR
PIECE = (2, HALF_R, HALF_C, 4, D)
F32 = jnp.float32
BF16 = jnp.bfloat16


def spot(x, y, z, core):
    return ((x % 2) * 16 + z * 2 + core) * 8 + y * 2 + x // 2


FOUR, EIGHT, TWO = range(4), range(8), range(2)
LINES = [[spot(x, y, z, 0) for x in FOUR] for y in FOUR for z in EIGHT]
LINES += [[spot(x, y, z, 1) for y in FOUR] for x in FOUR for z in EIGHT]
SHEETS = [[spot(x, y, 2 * f + z, 0) for y in FOUR for z in TWO] for x in FOUR for f in FOUR]
SHEETS += [[spot(x, y, 2 * f + z, 1) for x in FOUR for z in TWO] for y in FOUR for f in FOUR]
NEAR = [[spot(x, y, 2 * f + z, 0) for x in FOUR for y in FOUR for z in TWO] for f in FOUR]
NEAR += [[spot(x, y, 2 * f + z, 1) for x in FOUR for y in FOUR for z in TWO] for f in FOUR]


def exchanged(parts, groups):
    return lax.all_to_all(parts, AXES, 0, 0, axis_index_groups=groups)


def dot(left, right):
    return jnp.dot(left, right, preferred_element_type=F32)


def dot_first(left, right):
    return lax.dot_general(left, right, (((0,), (0,)), ((), ())), preferred_element_type=F32)


def dot_last(left, right):
    return lax.dot_general(left, right, (((1,), (1,)), ((), ())), preferred_element_type=F32)


def pack_kernel(tok_ref, cot_ref, own_ref, right_ref, below_ref, corner_ref, sems):
    copies = []
    for n, ref in enumerate((tok_ref, cot_ref)):
        for rows, cols, piece in quadrants(own_ref, right_ref, below_ref, corner_ref):
            sem = sems.at[len(copies)]
            copies.append(pltpu.make_async_copy(ref.at[rows, cols], piece.at[n], sem))
    for copy in copies:
        copy.start()
    for copy in copies:
        copy.wait()


def quadrants(own, right, below, corner):
    late_r, early_r = pl.ds(HALF_R, HALF_R), pl.ds(0, HALF_R)
    late_c, early_c = pl.ds(HALF_C, HALF_C), pl.ds(0, HALF_C)
    return (
        (late_r, late_c, own),
        (late_r, early_c, right),
        (early_r, late_c, below),
        (early_r, early_c, corner),
    )


def source_of(place):
    window = place // COUNT
    rest = place - window * COUNT
    level = (1 + 2 * window + rest % 2) % 4
    return (rest // 2) * 4 + level


def attend_kernel(
    corner_ref, right_ref, below_ref, own_ref, bias_ref, gain_ref, qkv_ref, proj_ref,
    send_ref, left_ref, rows_ref, att_ref, normed_ref, inv_ref,
):
    first = lax.broadcasted_iota(jnp.int32, (TOKENS, 1), 0)
    second = lax.broadcasted_iota(jnp.int32, (TOKENS, TOKENS), 1)
    to_order = (second == source_of(first)).astype(BF16)
    pieces = (own_ref, right_ref, below_ref, corner_ref)

    def gathered(n):
        return jnp.concatenate([ref[n] for ref in pieces], axis=0).reshape(TOKENS, D)

    values = dot(to_order, gathered(0))
    cot = dot(to_order, gathered(1)).astype(BF16)
    gain = gain_ref[...]
    mean = jnp.mean(values, -1, keepdims=True)
    centred = values - mean
    inv_std = lax.rsqrt(jnp.mean(centred * centred, -1, keepdims=True) + EPS)
    normed = centred * inv_std
    hidden = (normed * gain).astype(BF16)
    projected = dot(hidden, qkv_ref[...]).astype(BF16)
    grad_att = dot_last(cot, proj_ref[...]).astype(BF16)
    normed_ref[...] = normed
    inv_ref[...] = inv_std
    left_ref[0] = hidden.T
    rows_ref[3] = cot

    lane = lax.broadcasted_iota(jnp.int32, (COUNT, 2 * HEAD), 1)
    low = lane < HEAD
    zero = jnp.zeros((COUNT, 2 * HEAD), BF16)

    def both(pair):
        return jnp.concatenate([jnp.where(low, pair, zero), jnp.where(low, zero, pair)], axis=0)

    def merged(stacked):
        return jnp.where(low, stacked[:COUNT], stacked[COUNT:])

    factor = HEAD ** (-0.5)
    biases = [jnp.concatenate([bias_ref[w]] * 2, axis=1) for w in range(WINDOWS)]
    spots = [(w, p) for w in range(WINDOWS) for p in range(PAIRS)]
    for at in range(0, len(spots), TOGETHER):
        here, cols, bias = [], [], []
        for window, pair in spots[at : at + TOGETHER]:
            here.append(slice(window * COUNT, (window + 1) * COUNT))
            cols.append(slice(pair * 2 * HEAD, (pair + 1) * 2 * HEAD))
            bias.append(biases[window])
        each = range(len(here))
        query = [both(projected[here[i], cols[i]] * jnp.asarray(factor, BF16)) for i in each]
        keys = [projected[here[i], D + cols[i].start : D + cols[i].stop] for i in each]
        vals = [projected[here[i], 2 * D + cols[i].start : 2 * D + cols[i].stop] for i in each]
        grad_out = [both(grad_att[here[i], cols[i]]) for i in each]
        scores = [dot_last(keys[i], query[i]) + bias[i] for i in each]
        grad_weights = [dot_last(vals[i], grad_out[i]) for i in each]
        numer = [jnp.exp(s - jnp.max(s, 0, keepdims=True)) for s in scores]
        weights = [n * (1.0 / jnp.sum(n, 0, keepdims=True)) for n in numer]
        weights_low = [w.astype(BF16) for w in weights]
        inner = [jnp.sum(g * w, 0, keepdims=True) for g, w in zip(grad_weights, weights)]
        grad_scores = [
            (w * (g - i)).astype(BF16) for w, g, i in zip(weights, grad_weights, inner)
        ]
        for i in each:
            att_ref[here[i], cols[i]] = merged(dot_first(weights_low[i], vals[i])).astype(BF16)
            rows_ref[2, here[i], cols[i]] = dot(weights_low[i], grad_out[i]).astype(BF16)
        for i in each:
            grad_query = merged(dot_first(grad_scores[i], keys[i])) * factor
            rows_ref[0, here[i], cols[i]] = grad_query.astype(BF16)
            rows_ref[1, here[i], cols[i]] = dot(grad_scores[i], query[i]).astype(BF16)

    left_ref[1] = att_ref[...].T
    half_grads(1 - lax.axis_index("c"), left_ref, rows_ref, send_ref)


def half_grads(half, left_ref, rows_ref, out_ref):
    here = pl.ds(pl.multiple_of(half * HALF_D, HALF_D), HALF_D)
    for block in range(4):
        out_ref[block] = dot(left_ref[block // 3, here], rows_ref[block]).astype(BF16)


def rest_kernel(
    left_ref, rows_ref, att_ref, normed_ref, inv_ref, gain_ref, qkv_ref, proj_ref,
    keep_ref, own_out, right_out, lower_out,
):
    half_grads(lax.axis_index("c"), left_ref, rows_ref, keep_ref)
    first = lax.broadcasted_iota(jnp.int32, (TOKENS, TOKENS), 0)
    second = lax.broadcasted_iota(jnp.int32, (1, TOKENS), 1)
    from_order = (first == source_of(second)).astype(BF16)
    normed = normed_ref[...]
    inv_std = inv_ref[...]
    attended = att_ref[...]
    gain = gain_ref[...]
    branch = dot(attended, proj_ref[...]).astype(BF16)
    grad_hidden = dot_last(rows_ref[0], qkv_ref[:, :D])
    grad_hidden += dot_last(rows_ref[1], qkv_ref[:, D : 2 * D])
    grad_hidden += dot_last(rows_ref[2], qkv_ref[:, 2 * D :])
    grad_norm = grad_hidden * gain
    grad_shift = inv_std * (
        grad_norm
        - jnp.mean(grad_norm, -1, keepdims=True)
        - normed * jnp.mean(grad_norm * normed, -1, keepdims=True)
    )
    for n, result in enumerate((branch, grad_shift.astype(BF16))):
        back = dot(from_order, result).reshape(4, HALF_R, HALF_C, 4, D).astype(BF16)
        own_out[n] = back[0]
        right_out[n] = back[1]
        lower_out[0, n] = back[2]
        lower_out[1, n] = back[3]


def weights_kernel(qkv_ref, proj_ref, gain_ref, qkv_out, proj_out, gain_out, sems):
    copies = [
        pltpu.make_async_copy(ref, out, sems.at[n])
        for n, (ref, out) in enumerate(
            ((qkv_ref, qkv_out), (proj_ref, proj_out), (gain_ref, gain_out))
        )
    ]
    for copy in copies:
        copy.start()
    for copy in copies:
        copy.wait()


def add_kernel(keep_ref, got_ref, out_ref, held, sems):
    core = lax.axis_index("c")
    copies = []
    for x in range(4):
        held[x] = (keep_ref[x].astype(F32) + got_ref[x].astype(F32)).astype(BF16)
        for y in range(4):
            place = (4 * x + y) * (1 - core) + (4 * y + x) * core
            group = held.at[x, pl.ds(y * 2 * CHUNK, 2 * CHUNK)]
            copies.append(pltpu.make_async_copy(group, out_ref.at[place], sems.at[4 * x + y]))
            copies[-1].start()
    for copy in copies:
        copy.wait()


def line_kernel(got_ref, lower_ref, out_ref):
    del lower_ref
    for n in range(8):
        rows = slice(n * CHUNK, (n + 1) * CHUNK)
        total = got_ref[0, rows].astype(F32)
        for line in range(1, 4):
            total += got_ref[line, rows].astype(F32)
        out_ref[n] = total.astype(BF16)


def sum_kernel(got_ref, lower_ref, right_ref, out_ref, side_ref):
    side_ref[0] = right_ref[...]
    side_ref[1] = lower_ref[1]
    total = got_ref[0].astype(F32)
    for n in range(1, got_ref.shape[0]):
        total += got_ref[n].astype(F32)
    out_ref[...] = total.astype(BF16)


def spread_kernel(own_ref, one_ref, two_ref, three_ref, side_ref, out_ref):
    del side_ref
    even = own_ref[...].astype(F32) + two_ref[...].astype(F32)
    odd = one_ref[...].astype(F32) + three_ref[...].astype(F32)
    total = (even + odd).astype(BF16)
    for n in range(out_ref.shape[0]):
        out_ref[n] = total


def finish_kernel(tok_ref, cot_ref, own_ref, lower_ref, side_ref, mixed_ref, grad_ref):
    right_ref, below_ref, corner_ref = side_ref.at[0], lower_ref.at[0], side_ref.at[1]
    for n, (ref, out) in enumerate(((tok_ref, mixed_ref), (cot_ref, grad_ref))):
        for rows, cols, piece in quadrants(own_ref, right_ref, below_ref, corner_ref):
            out[rows, cols] = (ref[rows, cols].astype(F32) + piece[n].astype(F32)).astype(BF16)


def grads_half(half, ref, qkv_ref, gain_ref, qkv_out, proj_out, gain_out, wide, sems):
    copies = []
    here = pl.ds(pl.multiple_of(half * HALF_D, HALF_D), HALF_D)
    total = jnp.zeros((HALF_D, 128), F32)
    for block in range(4):
        part = ref[block].astype(F32)
        wide[block] = part
        cols = pl.ds(block * D, D)
        out = proj_out.at[here] if block == 3 else qkv_out.at[here, cols]
        copy = pltpu.make_async_copy(wide.at[block], out, sems.at[block])
        copy.start()
        copies.append(copy)
        if block < 3:
            product = part * qkv_ref[here, cols].astype(F32)
            for q in range(4):
                total += product[:, q * 128 : (q + 1) * 128]
    sums = jnp.sum(total.T, axis=0, keepdims=True)
    gain_out[:, here] = sums / gain_ref[:, here]
    return copies


def mine_kernel(ref, qkv_ref, gain_ref, qkv_out, proj_out, gain_out, wide, sems):
    gain_out[...] = jnp.zeros_like(gain_out)
    core = lax.axis_index("c")
    copies = grads_half(core, ref, qkv_ref, gain_ref, qkv_out, proj_out, gain_out, wide, sems)
    for copy in copies:
        copy.wait()


def other_kernel(
    ref, qkv_ref, gain_ref, qkv_in, proj_in, gain_in, qkv_out, proj_out, gain_out, wide, sems,
    held, gain_sem,
):
    del qkv_in, proj_in
    held[...] = gain_in[...]
    half = 1 - lax.axis_index("c")
    copies = grads_half(half, ref, qkv_ref, gain_ref, qkv_out, proj_out, held, wide, sems)
    copies.append(pltpu.make_async_copy(held, gain_out, gain_sem))
    copies[-1].start()
    for copy in copies:
        copy.wait()


def call(kernel, outs, scratch=(), ins=None, out_specs=None, mib=8, aliases=None):
    more = {"input_output_aliases": aliases or {}}
    if ins is not None:
        more["in_specs"] = ins
    if out_specs is not None:
        more["out_specs"] = out_specs
    return pl.pallas_call(
        kernel,
        out_shape=outs,
        scratch_shapes=list(scratch),
        compiler_params=pltpu.CompilerParams(vmem_limit_bytes=mib * 1024 * 1024),
        **more,
    )


def in_hbm(array):
    return pltpu.with_memory_space_constraint(array, pltpu.HBM)


def shaped(shape, dtype):
    return jax.ShapeDtypeStruct(shape, dtype)


def moved(block, lat_step, lon_step):
    route = [
        (lat * 8 + lon, (lat + lat_step) % 32 * 8 + (lon + lon_step) % 8)
        for lat in range(32)
        for lon in range(8)
    ]
    return lax.ppermute(block, AXES, route)


def swapped(block):
    return lax.ppermute(block, "c", [(0, 1), (1, 0)])


def on_device(tokens, cotangent, region, gain, qkv_weight, proj_weight):
    tok = tokens.transpose(1, 2, 0, 3)
    cot = cotangent.transpose(1, 2, 0, 3)
    anywhere = pl.BlockSpec(memory_space=pl.ANY)
    vmem = pl.BlockSpec(memory_space=pltpu.VMEM)
    hbm = pl.BlockSpec(memory_space=pltpu.HBM)
    own, right, below, corner = call(
        pack_kernel,
        [shaped(PIECE, BF16)] * 4,
        [pltpu.SemaphoreType.DMA((8,))],
        [hbm] * 2,
        [vmem] * 4,
        mib=2,
    )(in_hbm(tok), in_hbm(cot))
    corner = moved(corner, -1, -1)
    right = moved(right, 0, -1)
    below = moved(below, -1, 0)
    ids = region.reshape(2, 2, 2, HALF_R, 2, HALF_C).transpose(0, 2, 4, 3, 5, 1).reshape(2, COUNT)
    bias = jnp.where(ids[:, :, None] == ids[:, None, :], 0.0, -1e30).astype(F32)
    gain = gain.reshape(1, D)
    qkv_weight, proj_weight, gain = call(
        weights_kernel,
        [shaped((D, 3 * D), BF16), shaped((D, D), BF16), shaped((1, D), F32)],
        [pltpu.SemaphoreType.DMA((3,))],
        [hbm] * 3,
        [vmem] * 3,
        mib=1,
    )(in_hbm(qkv_weight), in_hbm(proj_weight), in_hbm(gain))
    send, *state = call(
        attend_kernel,
        [
            shaped((4, HALF_D, D), BF16),
            shaped((2, D, TOKENS), BF16),
            shaped((4, TOKENS, D), BF16),
            shaped((TOKENS, D), BF16),
            shaped((TOKENS, D), F32),
            shaped((TOKENS, 1), F32),
        ],
        mib=16,
    )(corner, right, below, own, bias, gain, qkv_weight, proj_weight)
    got = swapped(send)
    pair = shaped((2,) + PIECE, BF16)
    keep, own_back, right_back, lower_back = call(
        rest_kernel,
        [shaped((4, HALF_D, D), BF16), shaped(PIECE, BF16), shaped(PIECE, BF16), pair],
        mib=16,
    )(*state, gain, qkv_weight, proj_weight)
    half = call(
        add_kernel,
        shaped((16, 2 * CHUNK, D), BF16),
        [pltpu.VMEM((4, HALF_D, D), BF16), pltpu.SemaphoreType.DMA((16,))],
        [vmem] * 2,
        anywhere,
        mib=4,
    )(keep, got)
    got = exchanged(half.reshape(4, 8 * CHUNK, D), LINES)
    lower_back = moved(lower_back, 1, 0)
    part = call(
        line_kernel, shaped((8, CHUNK, D), BF16), ins=[vmem, anywhere], out_specs=vmem, mib=6
    )(got, lower_back)
    got = exchanged(part, SHEETS)
    part, side_back = call(
        sum_kernel, [shaped((CHUNK, D), BF16), pair], ins=[vmem] * 3, out_specs=[vmem] * 2, mib=6
    )(got, lower_back, right_back)
    others = [
        lax.ppermute(part, FAR, [(n, (n - step) % N_FAR) for n in range(N_FAR)])
        for step in range(1, N_FAR)
    ]
    side_back = moved(side_back, 0, 1)
    parts = call(
        spread_kernel,
        shaped((N_NEAR, CHUNK, D), BF16),
        ins=[vmem] * 4 + [anywhere],
        out_specs=vmem,
        mib=4,
    )(part, *others, side_back)
    mine = exchanged(parts, NEAR)
    mine = mine.reshape(4, HALF_D, D)
    other = swapped(mine)
    grads = call(
        mine_kernel,
        [shaped((D, 3 * D), F32), shaped((D, D), F32), shaped((1, D), F32)],
        [pltpu.VMEM((4, HALF_D, D), F32), pltpu.SemaphoreType.DMA((4,))],
        [vmem] * 3,
        [anywhere, anywhere, vmem],
        mib=6,
    )(mine, qkv_weight, gain)
    grad_qkv, grad_proj, grad_gain = call(
        other_kernel,
        [shaped((D, 3 * D), F32), shaped((D, D), F32), shaped((1, D), F32)],
        [
            pltpu.VMEM((4, HALF_D, D), F32),
            pltpu.SemaphoreType.DMA((4,)),
            pltpu.VMEM((1, D), F32),
            pltpu.SemaphoreType.DMA,
        ],
        [vmem] * 3 + [anywhere] * 2 + [vmem],
        [anywhere] * 3,
        mib=6,
        aliases={3: 0, 4: 1},
    )(other, qkv_weight, gain, *grads)
    mixed, grad_tokens = call(finish_kernel, [shaped((6, 12, 4, D), BF16)] * 2, mib=6)(
        tok, cot, own_back, lower_back, side_back
    )
    return (
        mixed.transpose(2, 0, 1, 3),
        grad_tokens.transpose(2, 0, 1, 3),
        grad_qkv,
        grad_proj,
        grad_gain.reshape(D),
    )


def solution(mesh):
    fine = Mesh(mesh.devices.reshape(tuple(SIZES.values())), AXES)
    grid = P(None, LAT, LON, None)
    return jax.shard_map(
        on_device,
        mesh=fine,
        in_specs=(grid, grid, P(None, LAT, LON), P(), P(), P()),
        out_specs=(grid, grid, P(), P(), P()),
        check_vma=False,
    )
```

```python
import jax
import jax.numpy as jnp
from jax import lax
from jax.experimental import pallas as pl
from jax.experimental.pallas import tpu as pltpu
from jax.sharding import Mesh, PartitionSpec as P

D = 512
HALF_D = D // 2
HEADS = 8
HEAD = 64
PAIRS = HEADS // 2
WINDOWS = 2
COUNT = 144
TOKENS = WINDOWS * COUNT
HALF_R = 3
HALF_C = 6
EPS = 1e-05
TOGETHER = 8
SIZES = {"xl": 2, "zh": 4, "zl": 2, "c": 2, "y": 4, "xh": 2}
AXES = tuple(SIZES)
LAT = AXES[:4]
LON = AXES[4:]
NEAR = ("xh", "xl", "y", "zl")
N_NEAR = 32
FAR = "zh"
N_FAR = 4
CHUNK = 2 * D // N_NEAR
PIECE = (2, HALF_R, HALF_C, 4, D)
F32 = jnp.float32
BF16 = jnp.bfloat16


def dot(left, right):
    return jnp.dot(left, right, preferred_element_type=F32)


def dot_first(left, right):
    return lax.dot_general(left, right, (((0,), (0,)), ((), ())), preferred_element_type=F32)


def dot_last(left, right):
    return lax.dot_general(left, right, (((1,), (1,)), ((), ())), preferred_element_type=F32)


def pack_kernel(tok_ref, cot_ref, own_ref, right_ref, below_ref, corner_ref, sems):
    copies = []
    for n, ref in enumerate((tok_ref, cot_ref)):
        for rows, cols, piece in quadrants(own_ref, right_ref, below_ref, corner_ref):
            sem = sems.at[len(copies)]
            copies.append(pltpu.make_async_copy(ref.at[rows, cols], piece.at[n], sem))
    for copy in copies:
        copy.start()
    for copy in copies:
        copy.wait()


def quadrants(own, right, below, corner):
    late_r, early_r = pl.ds(HALF_R, HALF_R), pl.ds(0, HALF_R)
    late_c, early_c = pl.ds(HALF_C, HALF_C), pl.ds(0, HALF_C)
    return (
        (late_r, late_c, own),
        (late_r, early_c, right),
        (early_r, late_c, below),
        (early_r, early_c, corner),
    )


def source_of(place):
    window = place // COUNT
    rest = place - window * COUNT
    level = (1 + 2 * window + rest % 2) % 4
    return (rest // 2) * 4 + level


def attend_kernel(
    corner_ref, right_ref, below_ref, own_ref, bias_ref, gain_ref, qkv_ref, proj_ref,
    send_ref, left_ref, rows_ref, att_ref, normed_ref, inv_ref,
):
    first = lax.broadcasted_iota(jnp.int32, (TOKENS, 1), 0)
    second = lax.broadcasted_iota(jnp.int32, (TOKENS, TOKENS), 1)
    to_order = (second == source_of(first)).astype(BF16)
    pieces = (own_ref, right_ref, below_ref, corner_ref)

    def gathered(n):
        return jnp.concatenate([ref[n] for ref in pieces], axis=0).reshape(TOKENS, D)

    values = dot(to_order, gathered(0))
    cot = dot(to_order, gathered(1)).astype(BF16)
    gain = gain_ref[...]
    mean = jnp.mean(values, -1, keepdims=True)
    centred = values - mean
    inv_std = lax.rsqrt(jnp.mean(centred * centred, -1, keepdims=True) + EPS)
    normed = centred * inv_std
    hidden = (normed * gain).astype(BF16)
    projected = dot(hidden, qkv_ref[...]).astype(BF16)
    grad_att = dot_last(cot, proj_ref[...]).astype(BF16)
    normed_ref[...] = normed
    inv_ref[...] = inv_std
    left_ref[0] = hidden.T
    rows_ref[3] = cot

    lane = lax.broadcasted_iota(jnp.int32, (COUNT, 2 * HEAD), 1)
    low = lane < HEAD
    zero = jnp.zeros((COUNT, 2 * HEAD), BF16)

    def both(pair):
        return jnp.concatenate([jnp.where(low, pair, zero), jnp.where(low, zero, pair)], axis=0)

    def merged(stacked):
        return jnp.where(low, stacked[:COUNT], stacked[COUNT:])

    factor = HEAD ** (-0.5)
    biases = [jnp.concatenate([bias_ref[w]] * 2, axis=1) for w in range(WINDOWS)]
    spots = [(w, p) for w in range(WINDOWS) for p in range(PAIRS)]
    for at in range(0, len(spots), TOGETHER):
        here, cols, bias = [], [], []
        for window, pair in spots[at : at + TOGETHER]:
            here.append(slice(window * COUNT, (window + 1) * COUNT))
            cols.append(slice(pair * 2 * HEAD, (pair + 1) * 2 * HEAD))
            bias.append(biases[window])
        each = range(len(here))
        query = [both(projected[here[i], cols[i]] * jnp.asarray(factor, BF16)) for i in each]
        keys = [projected[here[i], D + cols[i].start : D + cols[i].stop] for i in each]
        vals = [projected[here[i], 2 * D + cols[i].start : 2 * D + cols[i].stop] for i in each]
        grad_out = [both(grad_att[here[i], cols[i]]) for i in each]
        scores = [dot_last(keys[i], query[i]) + bias[i] for i in each]
        grad_weights = [dot_last(vals[i], grad_out[i]) for i in each]
        numer = [jnp.exp(s - jnp.max(s, 0, keepdims=True)) for s in scores]
        weights = [n * (1.0 / jnp.sum(n, 0, keepdims=True)) for n in numer]
        weights_low = [w.astype(BF16) for w in weights]
        inner = [jnp.sum(g * w, 0, keepdims=True) for g, w in zip(grad_weights, weights)]
        grad_scores = [
            (w * (g - i)).astype(BF16) for w, g, i in zip(weights, grad_weights, inner)
        ]
        for i in each:
            att_ref[here[i], cols[i]] = merged(dot_first(weights_low[i], vals[i])).astype(BF16)
            rows_ref[2, here[i], cols[i]] = dot(weights_low[i], grad_out[i]).astype(BF16)
        for i in each:
            grad_query = merged(dot_first(grad_scores[i], keys[i])) * factor
            rows_ref[0, here[i], cols[i]] = grad_query.astype(BF16)
            rows_ref[1, here[i], cols[i]] = dot(grad_scores[i], query[i]).astype(BF16)

    left_ref[1] = att_ref[...].T
    half_grads(1 - lax.axis_index("c"), left_ref, rows_ref, send_ref)


def half_grads(half, left_ref, rows_ref, out_ref):
    here = pl.ds(pl.multiple_of(half * HALF_D, HALF_D), HALF_D)
    for block in range(4):
        out_ref[block] = dot(left_ref[block // 3, here], rows_ref[block]).astype(BF16)


def rest_kernel(
    left_ref, rows_ref, att_ref, normed_ref, inv_ref, gain_ref, qkv_ref, proj_ref,
    keep_ref, own_out, right_out, lower_out,
):
    half_grads(lax.axis_index("c"), left_ref, rows_ref, keep_ref)
    first = lax.broadcasted_iota(jnp.int32, (TOKENS, TOKENS), 0)
    second = lax.broadcasted_iota(jnp.int32, (1, TOKENS), 1)
    from_order = (first == source_of(second)).astype(BF16)
    normed = normed_ref[...]
    inv_std = inv_ref[...]
    attended = att_ref[...]
    gain = gain_ref[...]
    branch = dot(attended, proj_ref[...]).astype(BF16)
    grad_hidden = dot_last(rows_ref[0], qkv_ref[:, :D])
    grad_hidden += dot_last(rows_ref[1], qkv_ref[:, D : 2 * D])
    grad_hidden += dot_last(rows_ref[2], qkv_ref[:, 2 * D :])
    grad_norm = grad_hidden * gain
    grad_shift = inv_std * (
        grad_norm
        - jnp.mean(grad_norm, -1, keepdims=True)
        - normed * jnp.mean(grad_norm * normed, -1, keepdims=True)
    )
    for n, result in enumerate((branch, grad_shift.astype(BF16))):
        back = dot(from_order, result).reshape(4, HALF_R, HALF_C, 4, D).astype(BF16)
        own_out[n] = back[0]
        right_out[n] = back[1]
        lower_out[0, n] = back[2]
        lower_out[1, n] = back[3]


def weights_kernel(qkv_ref, proj_ref, gain_ref, qkv_out, proj_out, gain_out, sems):
    copies = [
        pltpu.make_async_copy(ref, out, sems.at[n])
        for n, (ref, out) in enumerate(
            ((qkv_ref, qkv_out), (proj_ref, proj_out), (gain_ref, gain_out))
        )
    ]
    for copy in copies:
        copy.start()
    for copy in copies:
        copy.wait()


def add_kernel(keep_ref, got_ref, out_ref, held, sems):
    copies = []
    for block in range(4):
        held[block] = (keep_ref[block].astype(F32) + got_ref[block].astype(F32)).astype(BF16)
        copy = pltpu.make_async_copy(held.at[block], out_ref.at[block], sems.at[block])
        copy.start()
        copies.append(copy)
    for copy in copies:
        copy.wait()


def sum_kernel(got_ref, lower_ref, right_ref, out_ref, side_ref):
    side_ref[0] = right_ref[...]
    side_ref[1] = lower_ref[1]
    total = got_ref[0].astype(F32)
    for n in range(1, got_ref.shape[0]):
        total += got_ref[n].astype(F32)
    out_ref[...] = total.astype(BF16)


def pair_kernel(own_ref, other_ref, out_ref):
    out_ref[...] = (own_ref[...].astype(F32) + other_ref[...].astype(F32)).astype(BF16)


def spread_kernel(own_ref, other_ref, side_ref, out_ref):
    del side_ref
    total = (own_ref[...].astype(F32) + other_ref[...].astype(F32)).astype(BF16)
    for n in range(out_ref.shape[0]):
        out_ref[n] = total


def finish_kernel(tok_ref, cot_ref, own_ref, lower_ref, side_ref, mixed_ref, grad_ref):
    right_ref, below_ref, corner_ref = side_ref.at[0], lower_ref.at[0], side_ref.at[1]
    for n, (ref, out) in enumerate(((tok_ref, mixed_ref), (cot_ref, grad_ref))):
        for rows, cols, piece in quadrants(own_ref, right_ref, below_ref, corner_ref):
            out[rows, cols] = (ref[rows, cols].astype(F32) + piece[n].astype(F32)).astype(BF16)


def grads_half(half, ref, qkv_ref, gain_ref, qkv_out, proj_out, gain_out, wide, sems):
    copies = []
    here = pl.ds(pl.multiple_of(half * HALF_D, HALF_D), HALF_D)
    total = jnp.zeros((HALF_D, 128), F32)
    for block in range(4):
        part = ref[block].astype(F32)
        wide[block] = part
        cols = pl.ds(block * D, D)
        out = proj_out.at[here] if block == 3 else qkv_out.at[here, cols]
        copy = pltpu.make_async_copy(wide.at[block], out, sems.at[block])
        copy.start()
        copies.append(copy)
        if block < 3:
            product = part * qkv_ref[here, cols].astype(F32)
            for q in range(4):
                total += product[:, q * 128 : (q + 1) * 128]
    sums = jnp.sum(total.T, axis=0, keepdims=True)
    gain_out[:, here] = sums / gain_ref[:, here]
    return copies


def mine_kernel(ref, qkv_ref, gain_ref, qkv_out, proj_out, gain_out, wide, sems):
    gain_out[...] = jnp.zeros_like(gain_out)
    core = lax.axis_index("c")
    copies = grads_half(core, ref, qkv_ref, gain_ref, qkv_out, proj_out, gain_out, wide, sems)
    for copy in copies:
        copy.wait()


def other_kernel(
    ref, qkv_ref, gain_ref, qkv_in, proj_in, gain_in, qkv_out, proj_out, gain_out, wide, sems,
    held, gain_sem,
):
    del qkv_in, proj_in
    held[...] = gain_in[...]
    half = 1 - lax.axis_index("c")
    copies = grads_half(half, ref, qkv_ref, gain_ref, qkv_out, proj_out, held, wide, sems)
    copies.append(pltpu.make_async_copy(held, gain_out, gain_sem))
    copies[-1].start()
    for copy in copies:
        copy.wait()


def call(kernel, outs, scratch=(), ins=None, out_specs=None, mib=8, aliases=None):
    more = {"input_output_aliases": aliases or {}}
    if ins is not None:
        more["in_specs"] = ins
    if out_specs is not None:
        more["out_specs"] = out_specs
    return pl.pallas_call(
        kernel,
        out_shape=outs,
        scratch_shapes=list(scratch),
        compiler_params=pltpu.CompilerParams(vmem_limit_bytes=mib * 1024 * 1024),
        **more,
    )


def in_hbm(array):
    return pltpu.with_memory_space_constraint(array, pltpu.HBM)


def shaped(shape, dtype):
    return jax.ShapeDtypeStruct(shape, dtype)


def moved(block, lat_step, lon_step):
    route = [
        (lat * 8 + lon, (lat + lat_step) % 32 * 8 + (lon + lon_step) % 8)
        for lat in range(32)
        for lon in range(8)
    ]
    return lax.ppermute(block, AXES, route)


def swapped(block):
    return lax.ppermute(block, "c", [(0, 1), (1, 0)])


def on_device(tokens, cotangent, region, gain, qkv_weight, proj_weight):
    tok = tokens.transpose(1, 2, 0, 3)
    cot = cotangent.transpose(1, 2, 0, 3)
    anywhere = pl.BlockSpec(memory_space=pl.ANY)
    vmem = pl.BlockSpec(memory_space=pltpu.VMEM)
    hbm = pl.BlockSpec(memory_space=pltpu.HBM)
    own, right, below, corner = call(
        pack_kernel,
        [shaped(PIECE, BF16)] * 4,
        [pltpu.SemaphoreType.DMA((8,))],
        [hbm] * 2,
        [vmem] * 4,
        mib=2,
    )(in_hbm(tok), in_hbm(cot))
    corner = moved(corner, -1, -1)
    right = moved(right, 0, -1)
    below = moved(below, -1, 0)
    ids = region.reshape(2, 2, 2, HALF_R, 2, HALF_C).transpose(0, 2, 4, 3, 5, 1).reshape(2, COUNT)
    bias = jnp.where(ids[:, :, None] == ids[:, None, :], 0.0, -1e30).astype(F32)
    gain = gain.reshape(1, D)
    qkv_weight, proj_weight, gain = call(
        weights_kernel,
        [shaped((D, 3 * D), BF16), shaped((D, D), BF16), shaped((1, D), F32)],
        [pltpu.SemaphoreType.DMA((3,))],
        [hbm] * 3,
        [vmem] * 3,
        mib=1,
    )(in_hbm(qkv_weight), in_hbm(proj_weight), in_hbm(gain))
    send, *state = call(
        attend_kernel,
        [
            shaped((4, HALF_D, D), BF16),
            shaped((2, D, TOKENS), BF16),
            shaped((4, TOKENS, D), BF16),
            shaped((TOKENS, D), BF16),
            shaped((TOKENS, D), F32),
            shaped((TOKENS, 1), F32),
        ],
        mib=16,
    )(corner, right, below, own, bias, gain, qkv_weight, proj_weight)
    got = swapped(send)
    pair = shaped((2,) + PIECE, BF16)
    keep, own_back, right_back, lower_back = call(
        rest_kernel,
        [shaped((4, HALF_D, D), BF16), shaped(PIECE, BF16), shaped(PIECE, BF16), pair],
        mib=16,
    )(*state, gain, qkv_weight, proj_weight)
    half = call(
        add_kernel,
        shaped((4, HALF_D, D), BF16),
        [pltpu.VMEM((4, HALF_D, D), BF16), pltpu.SemaphoreType.DMA((4,))],
        [vmem] * 2,
        anywhere,
        mib=4,
    )(keep, got)
    got = lax.all_to_all(half.reshape(N_NEAR, CHUNK, D), NEAR, 0, 0)
    lower_back = moved(lower_back, 1, 0)
    part, side_back = call(
        sum_kernel, [shaped((CHUNK, D), BF16), pair], ins=[vmem] * 3, out_specs=[vmem] * 2, mib=6
    )(got, lower_back, right_back)
    other = lax.ppermute(part, FAR, [(n, n ^ 1) for n in range(N_FAR)])
    part = call(pair_kernel, shaped((CHUNK, D), BF16), mib=1)(part, other)
    other = lax.ppermute(part, FAR, [(n, n ^ 2) for n in range(N_FAR)])
    side_back = moved(side_back, 0, 1)
    parts = call(
        spread_kernel,
        shaped((N_NEAR, CHUNK, D), BF16),
        ins=[vmem] * 2 + [anywhere],
        out_specs=vmem,
        mib=4,
    )(part, other, side_back)
    mine = lax.all_to_all(parts, NEAR, 0, 0)
    mine = mine.reshape(4, HALF_D, D)
    other = swapped(mine)
    grads = call(
        mine_kernel,
        [shaped((D, 3 * D), F32), shaped((D, D), F32), shaped((1, D), F32)],
        [pltpu.VMEM((4, HALF_D, D), F32), pltpu.SemaphoreType.DMA((4,))],
        [vmem] * 3,
        [anywhere, anywhere, vmem],
        mib=6,
    )(mine, qkv_weight, gain)
    grad_qkv, grad_proj, grad_gain = call(
        other_kernel,
        [shaped((D, 3 * D), F32), shaped((D, D), F32), shaped((1, D), F32)],
        [
            pltpu.VMEM((4, HALF_D, D), F32),
            pltpu.SemaphoreType.DMA((4,)),
            pltpu.VMEM((1, D), F32),
            pltpu.SemaphoreType.DMA,
        ],
        [vmem] * 3 + [anywhere] * 2 + [vmem],
        [anywhere] * 3,
        mib=6,
        aliases={3: 0, 4: 1},
    )(other, qkv_weight, gain, *grads)
    mixed, grad_tokens = call(finish_kernel, [shaped((6, 12, 4, D), BF16)] * 2, mib=6)(
        tok, cot, own_back, lower_back, side_back
    )
    return (
        mixed.transpose(2, 0, 1, 3),
        grad_tokens.transpose(2, 0, 1, 3),
        grad_qkv,
        grad_proj,
        grad_gain.reshape(D),
    )


def solution(mesh):
    fine = Mesh(mesh.devices.reshape(tuple(SIZES.values())), AXES)
    grid = P(None, LAT, LON, None)
    return jax.shard_map(
        on_device,
        mesh=fine,
        in_specs=(grid, grid, P(None, LAT, LON), P(), P(), P()),
        out_specs=(grid, grid, P(), P(), P()),
        check_vma=False,
    )
```

```python
import jax
import jax.numpy as jnp
from jax import lax
from jax.experimental import pallas as pl
from jax.experimental.pallas import tpu as pltpu
from jax.sharding import Mesh, PartitionSpec as P

D = 512
HALF_D = D // 2
HEADS = 8
HEAD = 64
PAIRS = HEADS // 2
WINDOWS = 2
COUNT = 144
TOKENS = WINDOWS * COUNT
HALF_R = 3
HALF_C = 6
EPS = 1e-05
TOGETHER = 8
SIZES = {"xl": 2, "zh": 4, "zl": 2, "c": 2, "y": 4, "xh": 2}
AXES = tuple(SIZES)
LAT = AXES[:4]
LON = AXES[4:]
NEAR = ("xh", "xl", "y", "zl")
N_NEAR = 32
FAR = "zh"
N_FAR = 4
CHUNK = 2 * D // N_NEAR
PIECE = (2, HALF_R, HALF_C, 4, D)
F32 = jnp.float32
BF16 = jnp.bfloat16


def dot(left, right):
    return jnp.dot(left, right, preferred_element_type=F32)


def dot_first(left, right):
    return lax.dot_general(left, right, (((0,), (0,)), ((), ())), preferred_element_type=F32)


def dot_last(left, right):
    return lax.dot_general(left, right, (((1,), (1,)), ((), ())), preferred_element_type=F32)


def pack_kernel(tok_ref, cot_ref, own_ref, right_ref, below_ref, corner_ref, sems):
    copies = []
    for n, ref in enumerate((tok_ref, cot_ref)):
        for rows, cols, piece in quadrants(own_ref, right_ref, below_ref, corner_ref):
            sem = sems.at[len(copies)]
            copies.append(pltpu.make_async_copy(ref.at[rows, cols], piece.at[n], sem))
    for copy in copies:
        copy.start()
    for copy in copies:
        copy.wait()


def quadrants(own, right, below, corner):
    late_r, early_r = pl.ds(HALF_R, HALF_R), pl.ds(0, HALF_R)
    late_c, early_c = pl.ds(HALF_C, HALF_C), pl.ds(0, HALF_C)
    return (
        (late_r, late_c, own),
        (late_r, early_c, right),
        (early_r, late_c, below),
        (early_r, early_c, corner),
    )


def source_of(place):
    window = place // COUNT
    rest = place - window * COUNT
    level = (1 + 2 * window + rest % 2) % 4
    return (rest // 2) * 4 + level


def attend_kernel(
    corner_ref, right_ref, below_ref, own_ref, bias_ref, gain_ref, qkv_ref, proj_ref,
    send_ref, left_ref, rows_ref, att_ref, normed_ref, inv_ref,
):
    first = lax.broadcasted_iota(jnp.int32, (TOKENS, 1), 0)
    second = lax.broadcasted_iota(jnp.int32, (TOKENS, TOKENS), 1)
    to_order = (second == source_of(first)).astype(BF16)
    pieces = (own_ref, right_ref, below_ref, corner_ref)

    def gathered(n):
        return jnp.concatenate([ref[n] for ref in pieces], axis=0).reshape(TOKENS, D)

    values = dot(to_order, gathered(0))
    cot = dot(to_order, gathered(1)).astype(BF16)
    gain = gain_ref[...]
    mean = jnp.mean(values, -1, keepdims=True)
    centred = values - mean
    inv_std = lax.rsqrt(jnp.mean(centred * centred, -1, keepdims=True) + EPS)
    normed = centred * inv_std
    hidden = (normed * gain).astype(BF16)
    projected = dot(hidden, qkv_ref[...]).astype(BF16)
    grad_att = dot_last(cot, proj_ref[...]).astype(BF16)
    normed_ref[...] = normed
    inv_ref[...] = inv_std
    left_ref[0] = hidden.T
    rows_ref[3] = cot

    lane = lax.broadcasted_iota(jnp.int32, (COUNT, 2 * HEAD), 1)
    low = lane < HEAD
    zero = jnp.zeros((COUNT, 2 * HEAD), BF16)

    def both(pair):
        return jnp.concatenate([jnp.where(low, pair, zero), jnp.where(low, zero, pair)], axis=0)

    def merged(stacked):
        return jnp.where(low, stacked[:COUNT], stacked[COUNT:])

    factor = HEAD ** (-0.5)
    biases = [jnp.concatenate([bias_ref[w]] * 2, axis=1) for w in range(WINDOWS)]
    spots = [(w, p) for w in range(WINDOWS) for p in range(PAIRS)]
    for at in range(0, len(spots), TOGETHER):
        here, cols, bias = [], [], []
        for window, pair in spots[at : at + TOGETHER]:
            here.append(slice(window * COUNT, (window + 1) * COUNT))
            cols.append(slice(pair * 2 * HEAD, (pair + 1) * 2 * HEAD))
            bias.append(biases[window])
        each = range(len(here))
        query = [both(projected[here[i], cols[i]] * jnp.asarray(factor, BF16)) for i in each]
        keys = [projected[here[i], D + cols[i].start : D + cols[i].stop] for i in each]
        vals = [projected[here[i], 2 * D + cols[i].start : 2 * D + cols[i].stop] for i in each]
        grad_out = [both(grad_att[here[i], cols[i]]) for i in each]
        scores = [dot_last(keys[i], query[i]) + bias[i] for i in each]
        grad_weights = [dot_last(vals[i], grad_out[i]) for i in each]
        numer = [jnp.exp(s - jnp.max(s, 0, keepdims=True)) for s in scores]
        weights = [n * (1.0 / jnp.sum(n, 0, keepdims=True)) for n in numer]
        weights_low = [w.astype(BF16) for w in weights]
        inner = [jnp.sum(g * w, 0, keepdims=True) for g, w in zip(grad_weights, weights)]
        grad_scores = [
            (w * (g - i)).astype(BF16) for w, g, i in zip(weights, grad_weights, inner)
        ]
        for i in each:
            att_ref[here[i], cols[i]] = merged(dot_first(weights_low[i], vals[i])).astype(BF16)
            rows_ref[2, here[i], cols[i]] = dot(weights_low[i], grad_out[i]).astype(BF16)
        for i in each:
            grad_query = merged(dot_first(grad_scores[i], keys[i])) * factor
            rows_ref[0, here[i], cols[i]] = grad_query.astype(BF16)
            rows_ref[1, here[i], cols[i]] = dot(grad_scores[i], query[i]).astype(BF16)

    left_ref[1] = att_ref[...].T
    half_grads(1 - lax.axis_index("c"), left_ref, rows_ref, send_ref)


def half_grads(half, left_ref, rows_ref, out_ref):
    here = pl.ds(pl.multiple_of(half * HALF_D, HALF_D), HALF_D)
    for block in range(4):
        out_ref[block] = dot(left_ref[block // 3, here], rows_ref[block]).astype(BF16)


def rest_kernel(
    left_ref, rows_ref, att_ref, normed_ref, inv_ref, gain_ref, qkv_ref, proj_ref,
    keep_ref, own_out, right_out, lower_out,
):
    half_grads(lax.axis_index("c"), left_ref, rows_ref, keep_ref)
    first = lax.broadcasted_iota(jnp.int32, (TOKENS, TOKENS), 0)
    second = lax.broadcasted_iota(jnp.int32, (1, TOKENS), 1)
    from_order = (first == source_of(second)).astype(BF16)
    normed = normed_ref[...]
    inv_std = inv_ref[...]
    attended = att_ref[...]
    gain = gain_ref[...]
    branch = dot(attended, proj_ref[...]).astype(BF16)
    grad_hidden = dot_last(rows_ref[0], qkv_ref[:, :D])
    grad_hidden += dot_last(rows_ref[1], qkv_ref[:, D : 2 * D])
    grad_hidden += dot_last(rows_ref[2], qkv_ref[:, 2 * D :])
    grad_norm = grad_hidden * gain
    grad_shift = inv_std * (
        grad_norm
        - jnp.mean(grad_norm, -1, keepdims=True)
        - normed * jnp.mean(grad_norm * normed, -1, keepdims=True)
    )
    for n, result in enumerate((branch, grad_shift.astype(BF16))):
        back = dot(from_order, result).reshape(4, HALF_R, HALF_C, 4, D).astype(BF16)
        own_out[n] = back[0]
        right_out[n] = back[1]
        lower_out[0, n] = back[2]
        lower_out[1, n] = back[3]


def weights_kernel(qkv_ref, proj_ref, gain_ref, qkv_out, proj_out, gain_out, sems):
    copies = [
        pltpu.make_async_copy(ref, out, sems.at[n])
        for n, (ref, out) in enumerate(
            ((qkv_ref, qkv_out), (proj_ref, proj_out), (gain_ref, gain_out))
        )
    ]
    for copy in copies:
        copy.start()
    for copy in copies:
        copy.wait()


def add_kernel(keep_ref, got_ref, out_ref):
    out_ref[...] = (keep_ref[...].astype(F32) + got_ref[...].astype(F32)).astype(BF16)


def sum_kernel(got_ref, lower_ref, right_ref, out_ref, side_ref):
    side_ref[0] = right_ref[...]
    side_ref[1] = lower_ref[1]
    total = got_ref[0].astype(F32)
    for n in range(1, got_ref.shape[0]):
        total += got_ref[n].astype(F32)
    out_ref[...] = total.astype(BF16)


def pair_kernel(own_ref, other_ref, out_ref):
    out_ref[...] = (own_ref[...].astype(F32) + other_ref[...].astype(F32)).astype(BF16)


def spread_kernel(own_ref, other_ref, side_ref, out_ref):
    del side_ref
    total = (own_ref[...].astype(F32) + other_ref[...].astype(F32)).astype(BF16)
    for n in range(out_ref.shape[0]):
        out_ref[n] = total


def finish_kernel(tok_ref, cot_ref, own_ref, lower_ref, side_ref, mixed_ref, grad_ref):
    right_ref, below_ref, corner_ref = side_ref.at[0], lower_ref.at[0], side_ref.at[1]
    for n, (ref, out) in enumerate(((tok_ref, mixed_ref), (cot_ref, grad_ref))):
        for rows, cols, piece in quadrants(own_ref, right_ref, below_ref, corner_ref):
            out[rows, cols] = (ref[rows, cols].astype(F32) + piece[n].astype(F32)).astype(BF16)


def grads_half(half, ref, qkv_ref, gain_ref, qkv_out, proj_out, gain_out, wide, sems):
    copies = []
    here = pl.ds(pl.multiple_of(half * HALF_D, HALF_D), HALF_D)
    total = jnp.zeros((HALF_D, 128), F32)
    for block in range(4):
        part = ref[block].astype(F32)
        wide[block] = part
        cols = pl.ds(block * D, D)
        out = proj_out.at[here] if block == 3 else qkv_out.at[here, cols]
        copy = pltpu.make_async_copy(wide.at[block], out, sems.at[block])
        copy.start()
        copies.append(copy)
        if block < 3:
            product = part * qkv_ref[here, cols].astype(F32)
            for q in range(4):
                total += product[:, q * 128 : (q + 1) * 128]
    sums = jnp.sum(total.T, axis=0, keepdims=True)
    gain_out[:, here] = sums / gain_ref[:, here]
    return copies


def mine_kernel(ref, qkv_ref, gain_ref, qkv_out, proj_out, gain_out, wide, sems):
    gain_out[...] = jnp.zeros_like(gain_out)
    core = lax.axis_index("c")
    copies = grads_half(core, ref, qkv_ref, gain_ref, qkv_out, proj_out, gain_out, wide, sems)
    for copy in copies:
        copy.wait()


def other_kernel(
    ref, qkv_ref, gain_ref, qkv_in, proj_in, gain_in, qkv_out, proj_out, gain_out, wide, sems,
    held, gain_sem,
):
    del qkv_in, proj_in
    held[...] = gain_in[...]
    half = 1 - lax.axis_index("c")
    copies = grads_half(half, ref, qkv_ref, gain_ref, qkv_out, proj_out, held, wide, sems)
    copies.append(pltpu.make_async_copy(held, gain_out, gain_sem))
    copies[-1].start()
    for copy in copies:
        copy.wait()


def call(kernel, outs, scratch=(), ins=None, out_specs=None, mib=8, aliases=None):
    more = {"input_output_aliases": aliases or {}}
    if ins is not None:
        more["in_specs"] = ins
    if out_specs is not None:
        more["out_specs"] = out_specs
    return pl.pallas_call(
        kernel,
        out_shape=outs,
        scratch_shapes=list(scratch),
        compiler_params=pltpu.CompilerParams(vmem_limit_bytes=mib * 1024 * 1024),
        **more,
    )


def in_hbm(array):
    return pltpu.with_memory_space_constraint(array, pltpu.HBM)


def shaped(shape, dtype):
    return jax.ShapeDtypeStruct(shape, dtype)


def moved(block, lat_step, lon_step):
    route = [
        (lat * 8 + lon, (lat + lat_step) % 32 * 8 + (lon + lon_step) % 8)
        for lat in range(32)
        for lon in range(8)
    ]
    return lax.ppermute(block, AXES, route)


def swapped(block):
    return lax.ppermute(block, "c", [(0, 1), (1, 0)])


def on_device(tokens, cotangent, region, gain, qkv_weight, proj_weight):
    tok = tokens.transpose(1, 2, 0, 3)
    cot = cotangent.transpose(1, 2, 0, 3)
    anywhere = pl.BlockSpec(memory_space=pl.ANY)
    vmem = pl.BlockSpec(memory_space=pltpu.VMEM)
    hbm = pl.BlockSpec(memory_space=pltpu.HBM)
    own, right, below, corner = call(
        pack_kernel,
        [shaped(PIECE, BF16)] * 4,
        [pltpu.SemaphoreType.DMA((8,))],
        [hbm] * 2,
        [vmem] * 4,
        mib=2,
    )(in_hbm(tok), in_hbm(cot))
    corner = moved(corner, -1, -1)
    right = moved(right, 0, -1)
    below = moved(below, -1, 0)
    ids = region.reshape(2, 2, 2, HALF_R, 2, HALF_C).transpose(0, 2, 4, 3, 5, 1).reshape(2, COUNT)
    bias = jnp.where(ids[:, :, None] == ids[:, None, :], 0.0, -1e30).astype(F32)
    gain = gain.reshape(1, D)
    qkv_weight, proj_weight, gain = call(
        weights_kernel,
        [shaped((D, 3 * D), BF16), shaped((D, D), BF16), shaped((1, D), F32)],
        [pltpu.SemaphoreType.DMA((3,))],
        [hbm] * 3,
        [vmem] * 3,
        mib=1,
    )(in_hbm(qkv_weight), in_hbm(proj_weight), in_hbm(gain))
    send, *state = call(
        attend_kernel,
        [
            shaped((4, HALF_D, D), BF16),
            shaped((2, D, TOKENS), BF16),
            shaped((4, TOKENS, D), BF16),
            shaped((TOKENS, D), BF16),
            shaped((TOKENS, D), F32),
            shaped((TOKENS, 1), F32),
        ],
        mib=16,
    )(corner, right, below, own, bias, gain, qkv_weight, proj_weight)
    got = swapped(send)
    pair = shaped((2,) + PIECE, BF16)
    keep, own_back, right_back, lower_back = call(
        rest_kernel,
        [shaped((4, HALF_D, D), BF16), shaped(PIECE, BF16), shaped(PIECE, BF16), pair],
        mib=16,
    )(*state, gain, qkv_weight, proj_weight)
    half = call(add_kernel, pltpu.VMEM((4, HALF_D, D), BF16), mib=4)(keep, got)
    got = lax.all_to_all(half.reshape(N_NEAR, CHUNK, D), NEAR, 0, 0)
    lower_back = moved(lower_back, 1, 0)
    part, side_back = call(
        sum_kernel, [shaped((CHUNK, D), BF16), pair], ins=[vmem] * 3, out_specs=[vmem] * 2, mib=6
    )(got, lower_back, right_back)
    other = lax.ppermute(part, FAR, [(n, n ^ 1) for n in range(N_FAR)])
    part = call(pair_kernel, shaped((CHUNK, D), BF16), mib=1)(part, other)
    other = lax.ppermute(part, FAR, [(n, n ^ 2) for n in range(N_FAR)])
    side_back = moved(side_back, 0, 1)
    parts = call(
        spread_kernel,
        shaped((N_NEAR, CHUNK, D), BF16),
        ins=[vmem] * 2 + [anywhere],
        out_specs=vmem,
        mib=4,
    )(part, other, side_back)
    mine = lax.all_to_all(parts, NEAR, 0, 0)
    mine = mine.reshape(4, HALF_D, D)
    other = swapped(mine)
    grads = call(
        mine_kernel,
        [shaped((D, 3 * D), F32), shaped((D, D), F32), shaped((1, D), F32)],
        [pltpu.VMEM((4, HALF_D, D), F32), pltpu.SemaphoreType.DMA((4,))],
        [vmem] * 3,
        [anywhere, anywhere, vmem],
        mib=6,
    )(mine, qkv_weight, gain)
    grad_qkv, grad_proj, grad_gain = call(
        other_kernel,
        [shaped((D, 3 * D), F32), shaped((D, D), F32), shaped((1, D), F32)],
        [
            pltpu.VMEM((4, HALF_D, D), F32),
            pltpu.SemaphoreType.DMA((4,)),
            pltpu.VMEM((1, D), F32),
            pltpu.SemaphoreType.DMA,
        ],
        [vmem] * 3 + [anywhere] * 2 + [vmem],
        [anywhere] * 3,
        mib=6,
        aliases={3: 0, 4: 1},
    )(other, qkv_weight, gain, *grads)
    mixed, grad_tokens = call(finish_kernel, [shaped((6, 12, 4, D), BF16)] * 2, mib=6)(
        tok, cot, own_back, lower_back, side_back
    )
    return (
        mixed.transpose(2, 0, 1, 3),
        grad_tokens.transpose(2, 0, 1, 3),
        grad_qkv,
        grad_proj,
        grad_gain.reshape(D),
    )


def solution(mesh):
    fine = Mesh(mesh.devices.reshape(tuple(SIZES.values())), AXES)
    grid = P(None, LAT, LON, None)
    return jax.shard_map(
        on_device,
        mesh=fine,
        in_specs=(grid, grid, P(None, LAT, LON), P(), P(), P()),
        out_specs=(grid, grid, P(), P(), P()),
        check_vma=False,
    )
```

```python
import jax
import jax.numpy as jnp
from jax import lax
from jax.experimental import pallas as pl
from jax.experimental.pallas import tpu as pltpu
from jax.sharding import Mesh, PartitionSpec as P

D = 512
HALF_D = D // 2
HEADS = 8
HEAD = 64
PAIRS = HEADS // 2
WINDOWS = 2
COUNT = 144
TOKENS = WINDOWS * COUNT
HALF_R = 3
HALF_C = 6
EPS = 1e-05
TOGETHER = 8
SIZES = {"xl": 2, "zh": 4, "zl": 2, "c": 2, "y": 4, "xh": 2}
AXES = tuple(SIZES)
LAT = AXES[:4]
LON = AXES[4:]
N_NEAR = 32
FAR = "zh"
N_FAR = 4
CHUNK = 2 * D // N_NEAR
PIECE = (2, HALF_R, HALF_C, 4, D)
F32 = jnp.float32
BF16 = jnp.bfloat16


def spot(x, y, z, core):
    return ((x % 2) * 16 + z * 2 + core) * 8 + y * 2 + x // 2


FOUR, EIGHT, TWO = range(4), range(8), range(2)
LINES = [[spot(x, y, z, 0) for x in FOUR] for y in FOUR for z in EIGHT]
LINES += [[spot(x, y, z, 1) for y in FOUR] for x in FOUR for z in EIGHT]
SHEETS = [[spot(x, y, 2 * f + z, 0) for y in FOUR for z in TWO] for x in FOUR for f in FOUR]
SHEETS += [[spot(x, y, 2 * f + z, 1) for x in FOUR for z in TWO] for y in FOUR for f in FOUR]
NEAR = [[spot(x, y, 2 * f + z, 0) for x in FOUR for y in FOUR for z in TWO] for f in FOUR]
NEAR += [[spot(x, y, 2 * f + z, 1) for y in FOUR for x in FOUR for z in TWO] for f in FOUR]


def exchanged(parts, groups):
    return lax.all_to_all(parts, AXES, 0, 0, axis_index_groups=groups)


def dot(left, right):
    return jnp.dot(left, right, preferred_element_type=F32)


def dot_first(left, right):
    return lax.dot_general(left, right, (((0,), (0,)), ((), ())), preferred_element_type=F32)


def dot_last(left, right):
    return lax.dot_general(left, right, (((1,), (1,)), ((), ())), preferred_element_type=F32)


def pack_kernel(tok_ref, cot_ref, own_ref, right_ref, below_ref, corner_ref, sems):
    copies = []
    for n, ref in enumerate((tok_ref, cot_ref)):
        for rows, cols, piece in quadrants(own_ref, right_ref, below_ref, corner_ref):
            sem = sems.at[len(copies)]
            copies.append(pltpu.make_async_copy(ref.at[rows, cols], piece.at[n], sem))
    for copy in copies:
        copy.start()
    for copy in copies:
        copy.wait()


def quadrants(own, right, below, corner):
    late_r, early_r = pl.ds(HALF_R, HALF_R), pl.ds(0, HALF_R)
    late_c, early_c = pl.ds(HALF_C, HALF_C), pl.ds(0, HALF_C)
    return (
        (late_r, late_c, own),
        (late_r, early_c, right),
        (early_r, late_c, below),
        (early_r, early_c, corner),
    )


def source_of(place):
    window = place // COUNT
    rest = place - window * COUNT
    level = (1 + 2 * window + rest % 2) % 4
    return (rest // 2) * 4 + level


def attend_kernel(
    corner_ref, right_ref, below_ref, own_ref, bias_ref, gain_ref, qkv_ref, proj_ref,
    send_ref, left_ref, rows_ref, att_ref, normed_ref, inv_ref,
):
    first = lax.broadcasted_iota(jnp.int32, (TOKENS, 1), 0)
    second = lax.broadcasted_iota(jnp.int32, (TOKENS, TOKENS), 1)
    to_order = (second == source_of(first)).astype(BF16)
    pieces = (own_ref, right_ref, below_ref, corner_ref)

    def gathered(n):
        return jnp.concatenate([ref[n] for ref in pieces], axis=0).reshape(TOKENS, D)

    values = dot(to_order, gathered(0))
    cot = dot(to_order, gathered(1)).astype(BF16)
    gain = gain_ref[...]
    mean = jnp.mean(values, -1, keepdims=True)
    centred = values - mean
    inv_std = lax.rsqrt(jnp.mean(centred * centred, -1, keepdims=True) + EPS)
    normed = centred * inv_std
    hidden = (normed * gain).astype(BF16)
    projected = dot(hidden, qkv_ref[...]).astype(BF16)
    grad_att = dot_last(cot, proj_ref[...]).astype(BF16)
    normed_ref[...] = normed
    inv_ref[...] = inv_std
    left_ref[0] = hidden.T
    rows_ref[3] = cot

    lane = lax.broadcasted_iota(jnp.int32, (COUNT, 2 * HEAD), 1)
    low = lane < HEAD
    zero = jnp.zeros((COUNT, 2 * HEAD), BF16)

    def both(pair):
        return jnp.concatenate([jnp.where(low, pair, zero), jnp.where(low, zero, pair)], axis=0)

    def merged(stacked):
        return jnp.where(low, stacked[:COUNT], stacked[COUNT:])

    factor = HEAD ** (-0.5)
    biases = [jnp.concatenate([bias_ref[w]] * 2, axis=1) for w in range(WINDOWS)]
    spots = [(w, p) for w in range(WINDOWS) for p in range(PAIRS)]
    for at in range(0, len(spots), TOGETHER):
        here, cols, bias = [], [], []
        for window, pair in spots[at : at + TOGETHER]:
            here.append(slice(window * COUNT, (window + 1) * COUNT))
            cols.append(slice(pair * 2 * HEAD, (pair + 1) * 2 * HEAD))
            bias.append(biases[window])
        each = range(len(here))
        query = [both(projected[here[i], cols[i]] * jnp.asarray(factor, BF16)) for i in each]
        keys = [projected[here[i], D + cols[i].start : D + cols[i].stop] for i in each]
        vals = [projected[here[i], 2 * D + cols[i].start : 2 * D + cols[i].stop] for i in each]
        grad_out = [both(grad_att[here[i], cols[i]]) for i in each]
        scores = [dot_last(keys[i], query[i]) + bias[i] for i in each]
        grad_weights = [dot_last(vals[i], grad_out[i]) for i in each]
        numer = [jnp.exp(s - jnp.max(s, 0, keepdims=True)) for s in scores]
        weights = [n * (1.0 / jnp.sum(n, 0, keepdims=True)) for n in numer]
        weights_low = [w.astype(BF16) for w in weights]
        inner = [jnp.sum(g * w, 0, keepdims=True) for g, w in zip(grad_weights, weights)]
        grad_scores = [
            (w * (g - i)).astype(BF16) for w, g, i in zip(weights, grad_weights, inner)
        ]
        for i in each:
            att_ref[here[i], cols[i]] = merged(dot_first(weights_low[i], vals[i])).astype(BF16)
            rows_ref[2, here[i], cols[i]] = dot(weights_low[i], grad_out[i]).astype(BF16)
        for i in each:
            grad_query = merged(dot_first(grad_scores[i], keys[i])) * factor
            rows_ref[0, here[i], cols[i]] = grad_query.astype(BF16)
            rows_ref[1, here[i], cols[i]] = dot(grad_scores[i], query[i]).astype(BF16)

    left_ref[1] = att_ref[...].T
    half_grads(1 - lax.axis_index("c"), left_ref, rows_ref, send_ref)


def half_grads(half, left_ref, rows_ref, out_ref):
    here = pl.ds(pl.multiple_of(half * HALF_D, HALF_D), HALF_D)
    for block in range(4):
        out_ref[block] = dot(left_ref[block // 3, here], rows_ref[block]).astype(BF16)


def rest_kernel(
    left_ref, rows_ref, att_ref, normed_ref, inv_ref, gain_ref, qkv_ref, proj_ref,
    keep_ref, own_out, right_out, lower_out,
):
    half_grads(lax.axis_index("c"), left_ref, rows_ref, keep_ref)
    first = lax.broadcasted_iota(jnp.int32, (TOKENS, TOKENS), 0)
    second = lax.broadcasted_iota(jnp.int32, (1, TOKENS), 1)
    from_order = (first == source_of(second)).astype(BF16)
    normed = normed_ref[...]
    inv_std = inv_ref[...]
    attended = att_ref[...]
    gain = gain_ref[...]
    branch = dot(attended, proj_ref[...]).astype(BF16)
    grad_hidden = dot_last(rows_ref[0], qkv_ref[:, :D])
    grad_hidden += dot_last(rows_ref[1], qkv_ref[:, D : 2 * D])
    grad_hidden += dot_last(rows_ref[2], qkv_ref[:, 2 * D :])
    grad_norm = grad_hidden * gain
    grad_shift = inv_std * (
        grad_norm
        - jnp.mean(grad_norm, -1, keepdims=True)
        - normed * jnp.mean(grad_norm * normed, -1, keepdims=True)
    )
    for n, result in enumerate((branch, grad_shift.astype(BF16))):
        back = dot(from_order, result).reshape(4, HALF_R, HALF_C, 4, D).astype(BF16)
        own_out[n] = back[0]
        right_out[n] = back[1]
        lower_out[0, n] = back[2]
        lower_out[1, n] = back[3]


def weights_kernel(qkv_ref, proj_ref, gain_ref, qkv_out, proj_out, gain_out, sems):
    copies = [
        pltpu.make_async_copy(ref, out, sems.at[n])
        for n, (ref, out) in enumerate(
            ((qkv_ref, qkv_out), (proj_ref, proj_out), (gain_ref, gain_out))
        )
    ]
    for copy in copies:
        copy.start()
    for copy in copies:
        copy.wait()


def add_kernel(keep_ref, got_ref, out_ref, held, sems):
    copies = []
    for block in range(4):
        held[block] = (keep_ref[block].astype(F32) + got_ref[block].astype(F32)).astype(BF16)
        copy = pltpu.make_async_copy(held.at[block], out_ref.at[block], sems.at[block])
        copy.start()
        copies.append(copy)
    for copy in copies:
        copy.wait()


def line_kernel(got_ref, lower_ref, out_ref):
    del lower_ref
    for n in range(8):
        rows = slice(n * CHUNK, (n + 1) * CHUNK)
        total = got_ref[0, rows].astype(F32)
        for line in range(1, 4):
            total += got_ref[line, rows].astype(F32)
        out_ref[n] = total.astype(BF16)


def sum_kernel(got_ref, lower_ref, right_ref, out_ref, side_ref):
    side_ref[0] = right_ref[...]
    side_ref[1] = lower_ref[1]
    total = got_ref[0].astype(F32)
    for n in range(1, got_ref.shape[0]):
        total += got_ref[n].astype(F32)
    out_ref[...] = total.astype(BF16)


def pair_kernel(own_ref, other_ref, out_ref):
    out_ref[...] = (own_ref[...].astype(F32) + other_ref[...].astype(F32)).astype(BF16)


def spread_kernel(own_ref, other_ref, side_ref, out_ref):
    del side_ref
    total = (own_ref[...].astype(F32) + other_ref[...].astype(F32)).astype(BF16)
    for n in range(out_ref.shape[0]):
        out_ref[n] = total


def finish_kernel(tok_ref, cot_ref, own_ref, lower_ref, side_ref, mixed_ref, grad_ref):
    right_ref, below_ref, corner_ref = side_ref.at[0], lower_ref.at[0], side_ref.at[1]
    for n, (ref, out) in enumerate(((tok_ref, mixed_ref), (cot_ref, grad_ref))):
        for rows, cols, piece in quadrants(own_ref, right_ref, below_ref, corner_ref):
            out[rows, cols] = (ref[rows, cols].astype(F32) + piece[n].astype(F32)).astype(BF16)


def grads_half(half, ref, qkv_ref, gain_ref, qkv_out, proj_out, gain_out, wide, sems):
    copies = []
    here = pl.ds(pl.multiple_of(half * HALF_D, HALF_D), HALF_D)
    total = jnp.zeros((HALF_D, 128), F32)
    for block in range(4):
        part = ref[block].astype(F32)
        wide[block] = part
        cols = pl.ds(block * D, D)
        out = proj_out.at[here] if block == 3 else qkv_out.at[here, cols]
        copy = pltpu.make_async_copy(wide.at[block], out, sems.at[block])
        copy.start()
        copies.append(copy)
        if block < 3:
            product = part * qkv_ref[here, cols].astype(F32)
            for q in range(4):
                total += product[:, q * 128 : (q + 1) * 128]
    sums = jnp.sum(total.T, axis=0, keepdims=True)
    gain_out[:, here] = sums / gain_ref[:, here]
    return copies


def mine_kernel(ref, qkv_ref, gain_ref, qkv_out, proj_out, gain_out, wide, sems):
    gain_out[...] = jnp.zeros_like(gain_out)
    core = lax.axis_index("c")
    copies = grads_half(core, ref, qkv_ref, gain_ref, qkv_out, proj_out, gain_out, wide, sems)
    for copy in copies:
        copy.wait()


def other_kernel(
    ref, qkv_ref, gain_ref, qkv_in, proj_in, gain_in, qkv_out, proj_out, gain_out, wide, sems,
    held, gain_sem,
):
    del qkv_in, proj_in
    held[...] = gain_in[...]
    half = 1 - lax.axis_index("c")
    copies = grads_half(half, ref, qkv_ref, gain_ref, qkv_out, proj_out, held, wide, sems)
    copies.append(pltpu.make_async_copy(held, gain_out, gain_sem))
    copies[-1].start()
    for copy in copies:
        copy.wait()


def call(kernel, outs, scratch=(), ins=None, out_specs=None, mib=8, aliases=None):
    more = {"input_output_aliases": aliases or {}}
    if ins is not None:
        more["in_specs"] = ins
    if out_specs is not None:
        more["out_specs"] = out_specs
    return pl.pallas_call(
        kernel,
        out_shape=outs,
        scratch_shapes=list(scratch),
        compiler_params=pltpu.CompilerParams(vmem_limit_bytes=mib * 1024 * 1024),
        **more,
    )


def in_hbm(array):
    return pltpu.with_memory_space_constraint(array, pltpu.HBM)


def shaped(shape, dtype):
    return jax.ShapeDtypeStruct(shape, dtype)


def moved(block, lat_step, lon_step):
    route = [
        (lat * 8 + lon, (lat + lat_step) % 32 * 8 + (lon + lon_step) % 8)
        for lat in range(32)
        for lon in range(8)
    ]
    return lax.ppermute(block, AXES, route)


def swapped(block):
    return lax.ppermute(block, "c", [(0, 1), (1, 0)])


def on_device(tokens, cotangent, region, gain, qkv_weight, proj_weight):
    tok = tokens.transpose(1, 2, 0, 3)
    cot = cotangent.transpose(1, 2, 0, 3)
    anywhere = pl.BlockSpec(memory_space=pl.ANY)
    vmem = pl.BlockSpec(memory_space=pltpu.VMEM)
    hbm = pl.BlockSpec(memory_space=pltpu.HBM)
    own, right, below, corner = call(
        pack_kernel,
        [shaped(PIECE, BF16)] * 4,
        [pltpu.SemaphoreType.DMA((8,))],
        [hbm] * 2,
        [vmem] * 4,
        mib=2,
    )(in_hbm(tok), in_hbm(cot))
    corner = moved(corner, -1, -1)
    right = moved(right, 0, -1)
    below = moved(below, -1, 0)
    ids = region.reshape(2, 2, 2, HALF_R, 2, HALF_C).transpose(0, 2, 4, 3, 5, 1).reshape(2, COUNT)
    bias = jnp.where(ids[:, :, None] == ids[:, None, :], 0.0, -1e30).astype(F32)
    gain = gain.reshape(1, D)
    qkv_weight, proj_weight, gain = call(
        weights_kernel,
        [shaped((D, 3 * D), BF16), shaped((D, D), BF16), shaped((1, D), F32)],
        [pltpu.SemaphoreType.DMA((3,))],
        [hbm] * 3,
        [vmem] * 3,
        mib=1,
    )(in_hbm(qkv_weight), in_hbm(proj_weight), in_hbm(gain))
    send, *state = call(
        attend_kernel,
        [
            shaped((4, HALF_D, D), BF16),
            shaped((2, D, TOKENS), BF16),
            shaped((4, TOKENS, D), BF16),
            shaped((TOKENS, D), BF16),
            shaped((TOKENS, D), F32),
            shaped((TOKENS, 1), F32),
        ],
        mib=16,
    )(corner, right, below, own, bias, gain, qkv_weight, proj_weight)
    got = swapped(send)
    pair = shaped((2,) + PIECE, BF16)
    keep, own_back, right_back, lower_back = call(
        rest_kernel,
        [shaped((4, HALF_D, D), BF16), shaped(PIECE, BF16), shaped(PIECE, BF16), pair],
        mib=16,
    )(*state, gain, qkv_weight, proj_weight)
    half = call(
        add_kernel,
        shaped((4, HALF_D, D), BF16),
        [pltpu.VMEM((4, HALF_D, D), BF16), pltpu.SemaphoreType.DMA((4,))],
        [vmem] * 2,
        anywhere,
        mib=4,
    )(keep, got)
    got = exchanged(half.reshape(4, 8 * CHUNK, D), LINES)
    lower_back = moved(lower_back, 1, 0)
    part = call(
        line_kernel, shaped((8, CHUNK, D), BF16), ins=[vmem, anywhere], out_specs=vmem, mib=6
    )(got, lower_back)
    got = exchanged(part, SHEETS)
    part, side_back = call(
        sum_kernel, [shaped((CHUNK, D), BF16), pair], ins=[vmem] * 3, out_specs=[vmem] * 2, mib=6
    )(got, lower_back, right_back)
    other = lax.ppermute(part, FAR, [(n, n ^ 1) for n in range(N_FAR)])
    part = call(pair_kernel, shaped((CHUNK, D), BF16), mib=1)(part, other)
    other = lax.ppermute(part, FAR, [(n, n ^ 2) for n in range(N_FAR)])
    side_back = moved(side_back, 0, 1)
    parts = call(
        spread_kernel,
        shaped((N_NEAR, CHUNK, D), BF16),
        ins=[vmem] * 2 + [anywhere],
        out_specs=vmem,
        mib=4,
    )(part, other, side_back)
    mine = exchanged(parts, NEAR)
    mine = mine.reshape(4, HALF_D, D)
    other = swapped(mine)
    grads = call(
        mine_kernel,
        [shaped((D, 3 * D), F32), shaped((D, D), F32), shaped((1, D), F32)],
        [pltpu.VMEM((4, HALF_D, D), F32), pltpu.SemaphoreType.DMA((4,))],
        [vmem] * 3,
        [anywhere, anywhere, vmem],
        mib=6,
    )(mine, qkv_weight, gain)
    grad_qkv, grad_proj, grad_gain = call(
        other_kernel,
        [shaped((D, 3 * D), F32), shaped((D, D), F32), shaped((1, D), F32)],
        [
            pltpu.VMEM((4, HALF_D, D), F32),
            pltpu.SemaphoreType.DMA((4,)),
            pltpu.VMEM((1, D), F32),
            pltpu.SemaphoreType.DMA,
        ],
        [vmem] * 3 + [anywhere] * 2 + [vmem],
        [anywhere] * 3,
        mib=6,
        aliases={3: 0, 4: 1},
    )(other, qkv_weight, gain, *grads)
    mixed, grad_tokens = call(finish_kernel, [shaped((6, 12, 4, D), BF16)] * 2, mib=6)(
        tok, cot, own_back, lower_back, side_back
    )
    return (
        mixed.transpose(2, 0, 1, 3),
        grad_tokens.transpose(2, 0, 1, 3),
        grad_qkv,
        grad_proj,
        grad_gain.reshape(D),
    )


def solution(mesh):
    fine = Mesh(mesh.devices.reshape(tuple(SIZES.values())), AXES)
    grid = P(None, LAT, LON, None)
    return jax.shard_map(
        on_device,
        mesh=fine,
        in_specs=(grid, grid, P(None, LAT, LON), P(), P(), P()),
        out_specs=(grid, grid, P(), P(), P()),
        check_vma=False,
    )
```
